128 devices in a mesh: grp: 32 (over y, x, core), sub: 4 (over z).
Axes of the slice: x: 4, y: 4, z: 4, core: 2. Of those that a mesh axis runs over, the one named last changes fastest.
Arguments:
- rhs: float32 [8, 8, 8, 32768], P(None, None, None, ('grp', 'sub')), may hold values from -6 to 6
- spacing_z: float32 [32], P('grp'), may hold values from 0.5 to 2
- spacing_a: float32 [64], replicated, may hold values from 0.5 to 2
- spacing_b: float32 [16], replicated, may hold values from 0.5 to 2
- rotation: int32 [32], replicated, may hold values from 0 to 3, as said below
Outputs:
- solution: float32 [8, 8, 8, 32768], P(None, None, None, ('grp', 'sub'))
- residual: float32 [8, 8, 8, 32768], P(None, None, None, ('grp', 'sub'))
The draws below stay inside these ranges and needn't reach their ends.
Inputs may be any that keep to these rules, and one draw needn't show every extreme that they name: Device (g, s) holds columns (rotation[g] + s * 16 + j) mod 64; some group has 3 and some 0.
All inputs are finite; a program needn't handle non-finite values.
Results may differ from the reference program's by a relative error of at most 0.0003.
Values sent between devices are 32-bit elements; how exact they have to be, the bound alone decides.
No kernel may reach another device: no remote copies, remote signals or barrier semaphores. Data moves between devices by JAX's collectives and lax.ppermute only.
A program may use at most 128 MiB of HBM per device.

```python
import math
import jax
import jax.numpy as jnp
import numpy as np
from jax import lax

PTS = 8
CPTS = 4
LAYERS_DEV = 1
COLS_DEV = 16
RADIAL = 16
SMOOTH = 2
DRIFT = 4
LAYERS = 32
COLS = 64
ELEMS = 32768
N_GRP = 32
N_SUB = 4


def draw_rhs(key, part):
    key = jax.random.fold_in(key, 11)
    shape = (PTS, PTS, PTS, ELEMS)
    values = jax.random.normal(key, shape, jnp.float32)
    return jnp.clip(values, -6.0, 6.0)


def draw_rotation(key, part):
    key = jax.random.fold_in(key, 7)
    first_key, second_key, third_key = jax.random.split(key, 3)
    values = jax.random.randint(first_key, (N_GRP,), 0, DRIFT)
    high_spot = jax.random.randint(second_key, (), 0, N_GRP)
    low_spot = (high_spot + 1 + jax.random.randint(third_key, (), 0, N_GRP - 1)) % N_GRP
    group_ids = jnp.arange(N_GRP)
    values = jnp.where(group_ids == high_spot, DRIFT - 1, values)
    values = jnp.where(group_ids == low_spot, 0, values)
    return values.astype(jnp.int32)


def steps_of(key, shape, pieces, smallest, largest):
    factor_of = 1.0
    for axis_at, shards_of in pieces:
        steps = jax.random.uniform(jax.random.fold_in(jax.random.fold_in(key, 6), axis_at), (shards_of,), jnp.float32, smallest / len(pieces), largest / len(pieces))
        factor_of = factor_of * jnp.repeat(jnp.exp(steps), shape[axis_at] // shards_of).reshape((-1,) + (1,) * (len(shape) - 1 - axis_at))
    return factor_of


def setup_inputs(seed: int = 0) -> dict:
    seeds = jax.random.split(jax.random.key(seed), 6)
    return {
        "rhs": draw_rhs(jax.random.fold_in(seeds[5], 71), 0),
        "spacing_z": jnp.clip(jnp.exp(math.log(2.0) - 1.3862944 * jax.random.uniform(seeds[1], (LAYERS,), jnp.float32) ** steps_of(seeds[1], (LAYERS,), ((0, 32),), -0.2, 0.2)), 0.5, 2.0),
        "spacing_a": jnp.clip(jnp.exp(jax.random.uniform(seeds[2], (COLS,), jnp.float32, math.log(0.5), math.log(2.0))), 0.5, 2.0),
        "spacing_b": jnp.clip(jnp.exp(jax.random.uniform(seeds[3], (RADIAL,), jnp.float32, math.log(0.5), math.log(2.0))), 0.5, 2.0),
        "rotation": draw_rotation(jax.random.fold_in(seeds[5], 71), 0),
    }


highest = lax.Precision.HIGHEST
cheb_upper = 2.0
cheb_ratio = 0.1

def legendre_rows(gll_nodes, poly_order):
    values = np.zeros((gll_nodes.size, poly_order + 1))
    values[:, 0] = 1.0
    values[:, 1] = gll_nodes
    for degree in range(2, poly_order + 1):
        values[:, degree] = ((2 * degree - 1) * gll_nodes * values[:, degree - 1] - (degree - 1) * values[:, degree - 2]) / degree
    return values

def jacobi_eigen(matrix):
    order = matrix.shape[0]
    current = matrix.copy()
    vectors = np.eye(order)
    for sweep in range(12):
        for first in range(order - 1):
            for second in range(first + 1, order):
                off_value = current[first, second]
                spread = current[second, second] - current[first, first]
                sense = np.where(spread >= 0.0, 1.0, -1.0)
                denom = spread + sense * np.sqrt(spread * spread + 4.0 * off_value * off_value)
                denom = np.where(denom == 0.0, 1.0, denom)
                tangent = 2.0 * off_value / denom
                cosine = 1.0 / np.sqrt(1.0 + tangent * tangent)
                sine = tangent * cosine
                rotate = np.eye(order)
                rotate[first, first] = cosine
                rotate[second, second] = cosine
                rotate[first, second] = sine
                rotate[second, first] = -sine
                current = rotate.T @ current @ rotate
                vectors = vectors @ rotate
    diag_ids = np.arange(order)
    return (current[diag_ids, diag_ids].copy(), vectors)

def lobatto(poly_order):
    gll_nodes = np.cos(np.pi * np.arange(poly_order + 1) / poly_order)
    for newton in range(100):
        values = legendre_rows(gll_nodes, poly_order)
        gll_nodes = gll_nodes - (gll_nodes * values[:, poly_order] - values[:, poly_order - 1]) / ((poly_order + 1) * values[:, poly_order])
    values = legendre_rows(gll_nodes, poly_order)
    gll_nodes = gll_nodes[::-1].copy()
    top_poly = values[::-1, poly_order].copy()
    weights = 2.0 / (poly_order * (poly_order + 1) * top_poly ** 2)
    derivative = np.zeros((poly_order + 1, poly_order + 1))
    for row_index in range(poly_order + 1):
        for col_index in range(poly_order + 1):
            if row_index != col_index:
                derivative[row_index, col_index] = top_poly[row_index] / (top_poly[col_index] * (gll_nodes[row_index] - gll_nodes[col_index]))
    derivative[0, 0] = -poly_order * (poly_order + 1) / 4.0
    derivative[poly_order, poly_order] = poly_order * (poly_order + 1) / 4.0
    stiffness = derivative.T @ (weights[:, None] * derivative)
    return (gll_nodes, weights, stiffness)

def basis_tables(fine_count, coarse_count):
    fine_nodes, fine_weights, fine_stiff = lobatto(fine_count - 1)
    coarse_nodes, coarse_weights, coarse_stiff = lobatto(coarse_count - 1)
    interp = np.ones((fine_count, coarse_count))
    for target_col in range(coarse_count):
        for other_col in range(coarse_count):
            if other_col != target_col:
                interp[:, target_col] *= (fine_nodes - coarse_nodes[other_col]) / (coarse_nodes[target_col] - coarse_nodes[other_col])
    poly_order = fine_count - 1
    node_count = 3 * poly_order + 1
    joined_stiff = np.zeros((node_count, node_count))
    joined_mass = np.zeros(node_count)
    for piece_index in range(3):
        first_node = piece_index * poly_order
        joined_stiff[first_node:first_node + fine_count, first_node:first_node + fine_count] += fine_stiff
        joined_mass[first_node:first_node + fine_count] += fine_weights
    kept_stiff = joined_stiff[poly_order - 1:2 * poly_order + 2, poly_order - 1:2 * poly_order + 2]
    root_mass = np.sqrt(joined_mass[poly_order - 1:2 * poly_order + 2])
    eigen_values, eigen_vectors = jacobi_eigen(kept_stiff / root_mass[:, None] / root_mass[None, :])
    eigen_basis = eigen_vectors / root_mass[:, None]
    coarse_ids = np.arange(coarse_count)
    coarse_diag = coarse_stiff[coarse_ids, coarse_ids].copy()
    coarse_z = coarse_diag[:, None, None] * coarse_weights[None, :, None] * coarse_weights[None, None, :]
    coarse_a = coarse_weights[:, None, None] * coarse_diag[None, :, None] * coarse_weights[None, None, :]
    coarse_b = coarse_weights[:, None, None] * coarse_weights[None, :, None] * coarse_diag[None, None, :]
    tables = (fine_stiff, fine_weights, eigen_basis, eigen_values, interp, coarse_z, coarse_a, coarse_b)
    return tuple((jnp.asarray(table, dtype=jnp.float32) for table in tables))

def contract(matrix, field, dimension):
    product = jnp.tensordot(matrix, field, axes=(1, dimension), precision=highest)
    return jnp.moveaxis(product, 0, dimension)

def assemble_phys(field):
    radial = field.shape[-1]
    keep_upper = (jnp.arange(radial) < radial - 1).astype(jnp.float32)
    keep_lower = (jnp.arange(radial) > 0).astype(jnp.float32)
    upper_face, lower_face = (field[-1], field[0])
    field = field.at[-1].set(upper_face + jnp.roll(lower_face, -1, axis=2))
    field = field.at[0].set(lower_face + jnp.roll(upper_face, 1, axis=2))
    left_face, right_face = (field[:, 0], field[:, -1])
    field = field.at[:, -1].set(right_face + jnp.roll(left_face, -1, axis=3))
    field = field.at[:, 0].set(left_face + jnp.roll(right_face, 1, axis=3))
    inner_face, outer_face = (field[:, :, 0], field[:, :, -1])
    field = field.at[:, :, -1].set(outer_face + jnp.roll(inner_face, -1, axis=4) * keep_upper)
    field = field.at[:, :, 0].set(inner_face + jnp.roll(outer_face, 1, axis=4) * keep_lower)
    return field

def reference(rhs, spacing_z, spacing_a, spacing_b, rotation):
    stiffness, weights, eigen_basis, eigen_values, interp, coarse_z, coarse_a, coarse_b = basis_tables(PTS, CPTS)
    col_count = COLS_DEV * N_SUB
    layer_count = LAYERS_DEV * N_GRP

    def turn_groups(blocks, starts):

        def turn_one(block, start):
            doubled = jnp.concatenate([block, block], axis=block.ndim - 2)
            return lax.dynamic_slice_in_dim(doubled, start, col_count, axis=block.ndim - 2)
        return jax.vmap(turn_one)(blocks, starts.astype(jnp.int32))

    def to_phys(stored):
        blocks = stored.reshape(PTS, PTS, PTS, N_GRP, N_SUB, LAYERS_DEV, COLS_DEV, RADIAL)
        blocks = blocks.transpose(3, 0, 1, 2, 5, 4, 6, 7).reshape(N_GRP, PTS, PTS, PTS, LAYERS_DEV, col_count, RADIAL)
        blocks = turn_groups(blocks, (col_count - rotation) % col_count)
        return jnp.moveaxis(blocks, 0, 3).reshape(PTS, PTS, PTS, layer_count, col_count, RADIAL)

    def to_stored(phys):
        blocks = jnp.moveaxis(phys.reshape(PTS, PTS, PTS, N_GRP, LAYERS_DEV, col_count, RADIAL), 3, 0)
        blocks = turn_groups(blocks, rotation)
        blocks = blocks.reshape(N_GRP, PTS, PTS, PTS, LAYERS_DEV, N_SUB, COLS_DEV, RADIAL)
        return blocks.transpose(1, 2, 3, 0, 5, 4, 6, 7).reshape(PTS, PTS, PTS, -1)
    length_z = spacing_z[:, None, None]
    length_a = spacing_a[None, :, None]
    length_b = spacing_b[None, None, :]
    coef_z = length_a * length_b / (2.0 * length_z)
    coef_a = length_z * length_b / (2.0 * length_a)
    coef_b = length_z * length_a / (2.0 * length_b)
    pair = weights[:, None] * weights[None, :]
    pair_jk = pair[:, :, None, None, None]
    pair_ik = pair[:, None, :, None, None, None]
    pair_ij = pair[:, :, None, None, None, None]
    lam_inv = 1.0 / (coef_z * eigen_values[:, None, None, None, None, None] + coef_a * eigen_values[None, :, None, None, None, None] + coef_b * eigen_values[None, None, :, None, None, None])
    radial_pos = jnp.arange(RADIAL)
    keep_upper = (radial_pos < RADIAL - 1).astype(jnp.float32)
    keep_lower = (radial_pos > 0).astype(jnp.float32)
    inv_mult = 1.0 / assemble_phys(jnp.ones((PTS, PTS, PTS, layer_count, col_count, RADIAL), jnp.float32))

    def apply_op(field):
        term_z = contract(stiffness, field, 0) * pair_jk
        term_a = contract(stiffness, field, 1) * pair_ik
        term_b = contract(stiffness, field, 2) * pair_ij
        return assemble_phys(coef_z * term_z + coef_a * term_a + coef_b * term_b)

    def precondition(resid):
        extended = jnp.zeros((PTS + 2, PTS + 2, PTS + 2) + resid.shape[3:], jnp.float32)
        extended = extended.at[1:-1, 1:-1, 1:-1].set(resid)
        extended = extended.at[0, 1:-1, 1:-1].set(jnp.roll(resid[-2], 1, axis=2))
        extended = extended.at[-1, 1:-1, 1:-1].set(jnp.roll(resid[1], -1, axis=2))
        extended = extended.at[1:-1, 0, 1:-1].set(jnp.roll(resid[:, -2], 1, axis=3))
        extended = extended.at[1:-1, -1, 1:-1].set(jnp.roll(resid[:, 1], -1, axis=3))
        extended = extended.at[1:-1, 1:-1, 0].set(jnp.roll(resid[:, :, -2], 1, axis=4) * keep_lower)
        extended = extended.at[1:-1, 1:-1, -1].set(jnp.roll(resid[:, :, 1], -1, axis=4) * keep_upper)
        for dimension in (0, 1, 2):
            extended = contract(eigen_basis.T, extended, dimension)
        extended = extended * lam_inv
        for dimension in (0, 1, 2):
            extended = contract(eigen_basis, extended, dimension)
        return assemble_phys(extended[1:-1, 1:-1, 1:-1] * inv_mult)

    def smooth(solution, resid):
        theta = 0.5 * (cheb_upper + cheb_upper * cheb_ratio)
        delta = 0.5 * (cheb_upper - cheb_upper * cheb_ratio)
        sigma = theta / delta
        rho_now = 1.0 / sigma
        step = precondition(resid) / theta
        for turn in range(SMOOTH):
            solution = solution + step
            resid = resid - apply_op(step)
            if turn + 1 < SMOOTH:
                rho_next = 1.0 / (2.0 * sigma - rho_now)
                step = rho_next * rho_now * step + 2.0 * rho_next / delta * precondition(resid)
                rho_now = rho_next
        return (solution, resid)
    target = assemble_phys(to_phys(rhs) * inv_mult)
    solution, resid = smooth(jnp.zeros_like(target), target)
    weighted = resid * inv_mult
    for dimension in (0, 1, 2):
        weighted = contract(interp.T, weighted, dimension)
    coarse_local = coef_z * coarse_z[:, :, :, None, None, None] + coef_a * coarse_a[:, :, :, None, None, None] + coef_b * coarse_b[:, :, :, None, None, None]
    coarse_resid = assemble_phys(weighted)
    coarse_diag = assemble_phys(coarse_local)
    correction = coarse_resid / coarse_diag
    for dimension in (0, 1, 2):
        correction = contract(interp, correction, dimension)
    solution = solution + correction
    resid = resid - apply_op(correction)
    solution, resid = smooth(solution, resid)
    return (to_stored(solution), to_stored(resid))
```

```python
import functools

import jax
import jax.numpy as jnp
import ml_dtypes
import numpy as np
from jax import lax
from jax.experimental import pallas as pl
from jax.experimental.pallas import tpu as pltpu
from jax.sharding import PartitionSpec as P

PTS = 8
CPTS = 4
COLS_DEV = 16
RADIAL = 16
SMOOTH = 2

WIN = 40
LEFT = 10
LANES = WIN * RADIAL
OWN = COLS_DEV * RADIAL
CLASSES = ((0, 0), (0, 1), (1, 0), (1, 1))
EXT = 224
MODES = 256
CHUNKS = ((0, 256), (256, 512), (512, 640))
TILE = 128
TILES = LANES // TILE

cheb_upper = 2.0
cheb_ratio = 0.1
theta = 0.5 * (cheb_upper + cheb_upper * cheb_ratio)
delta = 0.5 * (cheb_upper - cheb_upper * cheb_ratio)
sigma = theta / delta
rho_first = 1.0 / sigma
rho_second = 1.0 / (2.0 * sigma - rho_first)


def legendre_rows(gll_nodes, poly_order):
    values = np.zeros((gll_nodes.size, poly_order + 1))
    values[:, 0] = 1.0
    values[:, 1] = gll_nodes
    for degree in range(2, poly_order + 1):
        values[:, degree] = (
            (2 * degree - 1) * gll_nodes * values[:, degree - 1]
            - (degree - 1) * values[:, degree - 2]
        ) / degree
    return values


def jacobi_eigen(matrix):
    order = matrix.shape[0]
    current = matrix.copy()
    vectors = np.eye(order)
    for sweep in range(12):
        for first in range(order - 1):
            for second in range(first + 1, order):
                off_value = current[first, second]
                spread = current[second, second] - current[first, first]
                sense = np.where(spread >= 0.0, 1.0, -1.0)
                denom = spread + sense * np.sqrt(spread * spread + 4.0 * off_value * off_value)
                denom = np.where(denom == 0.0, 1.0, denom)
                tangent = 2.0 * off_value / denom
                cosine = 1.0 / np.sqrt(1.0 + tangent * tangent)
                sine = tangent * cosine
                rotate = np.eye(order)
                rotate[first, first] = cosine
                rotate[second, second] = cosine
                rotate[first, second] = sine
                rotate[second, first] = -sine
                current = rotate.T @ current @ rotate
                vectors = vectors @ rotate
    diag_ids = np.arange(order)
    return (current[diag_ids, diag_ids].copy(), vectors)


def lobatto(poly_order):
    gll_nodes = np.cos(np.pi * np.arange(poly_order + 1) / poly_order)
    for newton in range(100):
        values = legendre_rows(gll_nodes, poly_order)
        gll_nodes = gll_nodes - (gll_nodes * values[:, poly_order] - values[:, poly_order - 1]) / (
            (poly_order + 1) * values[:, poly_order]
        )
    values = legendre_rows(gll_nodes, poly_order)
    gll_nodes = gll_nodes[::-1].copy()
    top_poly = values[::-1, poly_order].copy()
    weights = 2.0 / (poly_order * (poly_order + 1) * top_poly**2)
    derivative = np.zeros((poly_order + 1, poly_order + 1))
    for row_index in range(poly_order + 1):
        for col_index in range(poly_order + 1):
            if row_index != col_index:
                derivative[row_index, col_index] = top_poly[row_index] / (
                    top_poly[col_index] * (gll_nodes[row_index] - gll_nodes[col_index])
                )
    derivative[0, 0] = -poly_order * (poly_order + 1) / 4.0
    derivative[poly_order, poly_order] = poly_order * (poly_order + 1) / 4.0
    stiffness = derivative.T @ (weights[:, None] * derivative)
    return (gll_nodes, weights, stiffness)


def element_tables():
    fine_nodes, fine_weights, fine_stiff = lobatto(PTS - 1)
    coarse_nodes, coarse_weights, coarse_stiff = lobatto(CPTS - 1)
    interp = np.ones((PTS, CPTS))
    for target_col in range(CPTS):
        for other_col in range(CPTS):
            if other_col != target_col:
                interp[:, target_col] *= (fine_nodes - coarse_nodes[other_col]) / (
                    coarse_nodes[target_col] - coarse_nodes[other_col]
                )
    poly_order = PTS - 1
    node_count = 3 * poly_order + 1
    joined_stiff = np.zeros((node_count, node_count))
    joined_mass = np.zeros(node_count)
    for piece_index in range(3):
        first_node = piece_index * poly_order
        joined_stiff[first_node : first_node + PTS, first_node : first_node + PTS] += fine_stiff
        joined_mass[first_node : first_node + PTS] += fine_weights
    kept = slice(poly_order - 1, 2 * poly_order + 2)
    root_mass = np.sqrt(joined_mass[kept])
    eigen_values, eigen_vectors = jacobi_eigen(
        joined_stiff[kept, kept] / root_mass[:, None] / root_mass[None, :]
    )
    eigen_basis = eigen_vectors / root_mass[:, None]
    coarse_diag = np.diag(coarse_stiff).copy()
    return fine_stiff, fine_weights, eigen_basis, eigen_values, interp, coarse_diag, coarse_weights


def split(table):
    high = table.astype(np.float32).astype(ml_dtypes.bfloat16)
    low = (table - high.astype(np.float64)).astype(np.float32).astype(ml_dtypes.bfloat16)
    return high, low


def kron3(first, second, third):
    return np.kron(first, np.kron(second, third))


def matrices():
    stiff, weights, basis, values, interp, coarse_diag, coarse_weights = element_tables()
    parts = ([], [])
    for mode in range(PTS + 2):
        column = basis[:, mode]
        odd = np.abs(column + column[::-1]).sum() < np.abs(column - column[::-1]).sum()
        parts[int(odd)].append(mode)
    signs = (1.0, -1.0)
    pure = basis.copy()
    for parity in (0, 1):
        for mode in parts[parity]:
            pure[:, mode] = 0.5 * (basis[:, mode] + signs[parity] * basis[::-1, mode])
    center = pure[1:-1, :]
    edges = pure[[0, -1], :]

    def folded(matrix, parity):
        half = PTS // 2
        return 0.5 * (matrix[:half, :half] + signs[parity] * matrix[:half, ::-1][:, :half])

    mass = np.diag(weights)
    halved = np.ones(PTS // 2)
    halved[0] = 0.5
    forward = np.zeros((4, MODES, EXT))
    backward = np.zeros((4, PTS * 16, MODES))
    apply_rows = np.zeros((4, 3 * PTS * 16, PTS * 16))
    mode_values = np.ones((4, MODES, 8))
    for at, (pi, pk) in enumerate(CLASSES):
        ci, ck = center[:4, parts[pi]], center[:4, parts[pk]]
        ei, ek = edges[:1, parts[pi]], edges[:1, parts[pk]]
        count = len(parts[pi]) * len(parts[pk]) * (PTS + 2)
        columns = np.concatenate(
            [
                kron3(ci, ck, center),
                kron3(ei, ck, center),
                kron3(ci, ek, center),
                kron3(ci, ck, edges[:1]),
                kron3(ci, ck, edges[1:]),
            ],
            axis=0,
        )
        forward[at, :count] = columns.T
        backward[at, :, :count] = kron3(halved[:, None] * ci, halved[:, None] * ck, center)
        vi, vk = values[parts[pi]], values[parts[pk]]
        ones = np.ones
        mode_values[at, :count, 0] = kron3(vi, ones(len(vk)), ones(PTS + 2))
        mode_values[at, :count, 1] = kron3(ones(len(vi)), vk, ones(PTS + 2))
        mode_values[at, :count, 2] = kron3(ones(len(vi)), ones(len(vk)), values)
        si, sk = folded(stiff, pi), folded(stiff, pk)
        mi, mk = folded(mass, pi), folded(mass, pk)
        apply_rows[at] = np.concatenate(
            [kron3(si, mk, mass), kron3(mi, sk, mass), kron3(mi, mk, stiff)], axis=0
        )
    mass_up, stiff_up = mass @ interp, stiff @ interp
    prolong = np.concatenate(
        [
            kron3(interp, interp, interp),
            kron3(stiff_up, mass_up, mass_up),
            kron3(mass_up, stiff_up, mass_up),
            kron3(mass_up, mass_up, stiff_up),
        ],
        axis=0,
    )
    restrict = kron3(interp.T, interp.T, interp.T)
    coarse = np.zeros((CPTS**3, 8))
    coarse[:, 0] = kron3(coarse_diag, coarse_weights, coarse_weights)
    coarse[:, 1] = kron3(coarse_weights, coarse_diag, coarse_weights)
    coarse[:, 2] = kron3(coarse_weights, coarse_weights, coarse_diag)

    def pair(table):
        high, low = split(table)
        return jnp.asarray(np.concatenate([high, high], axis=-1)), jnp.asarray(low)

    high, low = split(prolong)
    return {
        "forward": pair(forward),
        "backward": pair(backward),
        "apply": pair(apply_rows),
        "restrict": pair(restrict),
        "prolong": jnp.asarray(np.concatenate([high, high, low], axis=-1)),
        "modes": jnp.asarray(mode_values.reshape(4 * MODES, 8).astype(np.float32)),
        "coarse": jnp.asarray(coarse.astype(np.float32)),
    }


def halves(value):
    high = value.astype(jnp.bfloat16)
    low = (value - high.astype(jnp.float32)).astype(jnp.bfloat16)
    return high, low


def dot(left, right):
    return jnp.dot(left, right, preferred_element_type=jnp.float32)


def turn(value, steps):
    return pltpu.roll(value, steps % value.shape[-1], axis=value.ndim - 1)


def lane_masks(rows):
    radial = lax.broadcasted_iota(jnp.int32, (rows, LANES), 1) % RADIAL
    keep_upper = (radial < RADIAL - 1).astype(jnp.float32)
    keep_lower = (radial > 0).astype(jnp.float32)
    return keep_upper, keep_lower


def point_factor():
    point = lax.broadcasted_iota(jnp.int32, (PTS, LANES), 0)
    radial = lax.broadcasted_iota(jnp.int32, (PTS, LANES), 1) % RADIAL
    shared = ((point == 0) & (radial > 0)) | ((point == PTS - 1) & (radial < RADIAL - 1))
    return jnp.where(shared, 0.5, 1.0)


def side_factor(i, k):
    return (0.5 if i in (0, PTS - 1) else 1.0) * (0.5 if k in (0, PTS - 1) else 1.0)


def block(plane, k):
    start = plane * 64 + k * PTS
    return slice(start, start + PTS)


def load(ref, rows, base=0):
    return jnp.concatenate([ref[base + t, rows, :] for t in range(TILES)], axis=1)


def store(ref, rows, value, base=0, first=0):
    for t in range(value.shape[1] // TILE):
        ref[base + first + t, rows, :] = value[:, t * TILE : (t + 1) * TILE]


def assemble_sides(field, planes):
    keep_upper, keep_lower = lane_masks(PTS)
    for plane in range(planes):
        left = load(field, block(plane, 0))
        right = load(field, block(plane, PTS - 1))
        store(field, block(plane, PTS - 1), right + turn(left, -RADIAL))
        store(field, block(plane, 0), left + turn(right, RADIAL))
    for plane in range(planes):
        inner_at = pl.ds(plane * 64, PTS, stride=PTS)
        outer_at = pl.ds(plane * 64 + PTS - 1, PTS, stride=PTS)
        inner = load(field, inner_at)
        outer = load(field, outer_at)
        store(field, outer_at, outer + turn(inner, -1) * keep_upper)
        store(field, inner_at, inner + turn(outer, 1) * keep_lower)


def fold(a, b, c, d):
    sum_k, diff_k = a + b, a - b
    sum_m, diff_m = c + d, c - d
    return sum_k + sum_m, sum_k - sum_m, diff_k + diff_m, diff_k - diff_m


def pack(parts, packed, rows):
    for c in range(4):
        for t in range(TILES):
            lanes = slice(t * TILE, (t + 1) * TILE)
            high, low = halves(parts[c * TILES + t, 0:rows, :])
            packed[c, 0:rows, lanes] = high
            packed[c, rows : 2 * rows, lanes] = low


def unfold(parts, at):
    ss, sa, as_, aa = (load(parts, at, c * TILES) for c in range(4))
    sum_k, sum_m = ss + sa, ss - sa
    diff_k, diff_m = as_ + aa, as_ - aa
    return sum_k + diff_k, sum_k - diff_k, sum_m + diff_m, sum_m - diff_m


def mirrored(i, k):
    return (i, k), (PTS - 1 - i, k), (i, PTS - 1 - k), (PTS - 1 - i, PTS - 1 - k)


def tables_kernel(geo, modes, lam, coef):
    la, lb, lz = (jnp.broadcast_to(geo[n : n + 1], (PTS, LANES)) for n in range(3))
    cz = la * lb / (2.0 * lz)
    ca = lz * lb / (2.0 * la)
    cb = lz * la / (2.0 * lb)
    coef[0:8] = cz
    coef[8:16] = ca
    coef[16:24] = cb

    def rows(at, carry):
        here = pl.ds(pl.multiple_of(at * 8, 8), 8)
        mu = modes[here, :]
        lam[here, :] = 1.0 / (cz * mu[:, 0:1] + ca * mu[:, 1:2] + cb * mu[:, 2:3])
        return carry

    lax.fori_loop(0, 4 * MODES // 8, rows, 0)


def window_kernel(rot, left, own, right, geo, field, up, down):
    factor = point_factor()
    for case in range(4):

        @pl.when(rot[0] == case)
        def _(case=case):
            shift = (COLS_DEV - LEFT - case) * RADIAL

            for i in range(PTS):
                for k in range(PTS):
                    here = block(i, k)
                    joined = jnp.concatenate([left[here], own[here], right[here]], axis=1)
                    value = turn(joined, -shift)[:, :LANES]
                    field[here] = value * (factor * side_factor(i, k))

    up[0:128] = field[384:512]
    down[0:128] = field[0:128]
    length = jnp.broadcast_to(geo[2:3], (PTS, LANES))
    up[128:136] = length
    down[128:136] = length


def solve_kernel(
    field, below, above, lam, fwd, fwd_low, bwd, bwd_low, share, out, up, down, ext, parts, packed, modes
):
    store(ext, slice(0, 64), below[0:64])
    store(ext, slice(64, 128), field[0:64] + below[64:128])
    for i in range(1, PTS - 1):
        store(ext, slice(i * 64 + 64, i * 64 + 128), field[i * 64 : i * 64 + 64])
    store(ext, slice(512, 576), field[448:512] + above[0:64])
    store(ext, slice(576, 640), above[64:128])
    assemble_sides(ext, PTS + 2)
    factor = point_factor()
    for i in range(PTS):
        for k in range(PTS):
            share[block(i, k)] = load(ext, block(i + 1, k)) * (factor * side_factor(i, k))

    def put(at, values):
        for c in range(4):
            store(parts, at, values[c], c * TILES)

    for i in range(4):
        for k in range(4):
            put(block(0, i * 4 + k), fold(*(load(ext, block(p + 1, q)) for p, q in mirrored(i, k))))
    for k in range(4):
        put(
            block(2, k),
            fold(*(load(ext, block(p, q)) for p, q in ((0, k), (9, k), (0, 7 - k), (9, 7 - k)))),
        )
    for i in range(4):
        before = [turn(load(ext, block(p + 1, PTS - 2)), RADIAL) for p in (i, 7 - i)]
        after = [turn(load(ext, block(p + 1, 1)), -RADIAL) for p in (i, 7 - i)]
        put(block(2, 4 + i), fold(*before, *after))
    keep_upper, keep_lower = lane_masks(16)
    for c in range(4):
        base = c * TILES
        lower = load(parts, pl.ds(PTS - 2, 16, stride=PTS), base)
        upper = load(parts, pl.ds(1, 16, stride=PTS), base)
        store(parts, slice(192, 208), turn(lower, 1) * keep_lower, base)
        store(parts, slice(208, 224), turn(upper, -1) * keep_upper, base)
    pack(parts, packed, EXT)
    for c in range(4):
        for start, stop in CHUNKS:
            spectrum = dot(fwd[c], packed[c, :, start:stop])
            spectrum = spectrum + dot(fwd_low[c], packed[c, 0:EXT, start:stop])
            spectrum = spectrum * lam[c * MODES : (c + 1) * MODES, start:stop]
            modes[0:MODES, start:stop], modes[MODES:, start:stop] = halves(spectrum)
        for start, stop in CHUNKS:
            value = dot(bwd[c], modes[:, start:stop])
            value = value + dot(bwd_low[c], modes[0:MODES, start:stop])
            store(parts, slice(0, 128), value, c * TILES, start // TILE)
    for i in range(4):
        for k in range(4):
            values = unfold(parts, block(0, i * 4 + k))
            for (p, q), value in zip(mirrored(i, k), values):
                out[block(p, q)] = value * factor
    up[...] = out[448:512]
    down[...] = out[0:64]


def step_kernel(kind, *refs):
    take = iter(refs)
    local, below, above = next(take), next(take), next(take)
    before = next(take) if kind in (1, 3) else None
    total = next(take) if kind != 0 else None
    share, coef, app, app_low = (next(take) for _ in range(4))
    res, res_low = (next(take), next(take)) if kind == 1 else (None, None)
    step = next(take) if kind in (0, 2) else None
    sum_out = next(take) if kind != 0 else None
    field, up, down = next(take), next(take), next(take)
    coarse = next(take) if kind == 1 else None
    ext, parts, packed = next(take), next(take), next(take)
    wide = next(take) if kind == 1 else None
    store(ext, slice(0, 64), local[0:64] + below[...])
    for i in range(1, PTS - 1):
        store(ext, slice(i * 64, i * 64 + 64), local[i * 64 : i * 64 + 64])
    store(ext, slice(448, 512), local[448:512] + above[...])
    assemble_sides(ext, PTS)
    for i in range(PTS):
        here = slice(i * 64, i * 64 + 64)
        value = load(ext, here)
        if kind in (0, 2):
            value = value * (1.0 / theta)
            step[here] = value
        else:
            value = before[here] * (rho_second * rho_first) + value * (2.0 * rho_second / delta)
        store(ext, here, value)
        if kind != 0:
            sum_out[here] = total[here] + value
    for i in range(4):
        for k in range(4):
            values = fold(*(load(ext, block(p, q)) for p, q in mirrored(i, k)))
            for c in range(4):
                store(parts, block(0, i * 4 + k), values[c], c * TILES)
    pack(parts, packed, 128)
    for c in range(4):
        for start, stop in CHUNKS:
            terms = dot(app[c], packed[c, :, start:stop])
            terms = terms + dot(app_low[c], packed[c, 0:128, start:stop])
            terms = terms.reshape(3, 16, PTS, stop - start)
            value = (
                terms[0] * coef[0:8, start:stop]
                + terms[1] * coef[8:16, start:stop]
                + terms[2] * coef[16:24, start:stop]
            )
            store(parts, slice(0, 128), value.reshape(128, stop - start), c * TILES, start // TILE)
    for i in range(4):
        for k in range(4):
            values = unfold(parts, block(0, i * 4 + k))
            for (p, q), value in zip(mirrored(i, k), values):
                field[block(p, q)] = share[block(p, q)] - value
    if kind == 1:
        wide[0:512], wide[512:1024] = halves(field[...])
        for start, stop in CHUNKS:
            value = dot(res[...], wide[:, start:stop])
            coarse[:, start:stop] = value + dot(res_low[...], wide[0:512, start:stop])
        up[...] = coarse[48:64]
        down[...] = coarse[0:16]
    elif kind == 3:
        up[...] = field[448:512]
        down[...] = field[0:64]
    else:
        up[...] = field[384:512]
        down[...] = field[0:128]


def assemble_coarse(value):
    row = lax.broadcasted_iota(jnp.int32, (64, LANES), 0)
    keep_upper, keep_lower = lane_masks(64)
    first = (row % 16) < 4
    last = (row % 16) >= 12
    over = pltpu.roll(turn(value, -RADIAL), 12, axis=0)
    under = pltpu.roll(turn(value, RADIAL), 64 - 12, axis=0)
    value = value + jnp.where(last, over, 0.0) + jnp.where(first, under, 0.0)
    first = (row % 4) == 0
    last = (row % 4) == 3
    over = pltpu.roll(turn(value, -1) * keep_upper, 3, axis=0)
    under = pltpu.roll(turn(value, 1) * keep_lower, 64 - 3, axis=0)
    return value + jnp.where(last, over, 0.0) + jnp.where(first, under, 0.0)


def coarse_kernel(
    local, below, above, lower, upper, geo, coef, table, prolong, total, field, sum_out, out, up, down, packed
):
    value = local[...]
    value = jnp.concatenate([value[0:16] + below[...], value[16:48], value[48:64] + above[...]])
    value = assemble_coarse(value)
    la, lb = geo[0:1], geo[1:2]

    def diagonal(lz, rows):
        return (
            la * lb / (2.0 * lz) * table[rows, 0:1]
            + lz * lb / (2.0 * la) * table[rows, 1:2]
            + lz * la / (2.0 * lb) * table[rows, 2:3]
        )

    scale = diagonal(geo[2:3], slice(0, 64))
    scale = jnp.concatenate(
        [
            scale[0:16] + diagonal(lower[128:129], slice(48, 64)),
            scale[16:48],
            scale[48:64] + diagonal(upper[128:129], slice(0, 16)),
        ]
    )
    value = value / assemble_coarse(scale)
    high, low = halves(value)
    packed[0:64] = high
    packed[64:128] = low
    packed[128:192] = high
    for start, stop in CHUNKS:
        for i in range(PTS):
            here = slice(i * 64, i * 64 + 64)
            sides = (8, PTS, stop - start)
            terms = [
                dot(prolong[n * 512 + i * 64 : n * 512 + i * 64 + 64], packed[:, start:stop]) for n in range(4)
            ]
            sum_out[here, start:stop] = total[here, start:stop] + terms[0]
            value = (
                terms[1].reshape(sides) * coef[0:8, start:stop]
                + terms[2].reshape(sides) * coef[8:16, start:stop]
                + terms[3].reshape(sides) * coef[16:24, start:stop]
            )
            out[here, start:stop] = field[here, start:stop] - value.reshape(64, stop - start)
    up[...] = out[384:512]
    down[...] = out[0:128]


def finish_kernel(rot, local, below, above, total, sol, res, ext):
    store(ext, slice(0, 64), local[0:64] + below[...])
    for i in range(1, PTS - 1):
        store(ext, slice(i * 64, i * 64 + 64), local[i * 64 : i * 64 + 64])
    store(ext, slice(448, 512), local[448:512] + above[...])
    assemble_sides(ext, PTS)
    for case in range(4):

        @pl.when(rot[0] == case)
        def _(case=case):
            start = (LEFT + case) * RADIAL
            for plane in range(PTS):
                here = slice(plane * 64, plane * 64 + 64)
                sol[here] = total[here, start : start + OWN]
                res[here] = load(ext, here)[:, start : start + OWN]


def call(kernel, name, args, outs, scratch=(), scalars=0, flops=0):
    shape = lambda rows, lanes=LANES: jax.ShapeDtypeStruct((rows, lanes), jnp.float32)
    in_specs = [
        pl.BlockSpec(memory_space=pltpu.SMEM if n < scalars else pltpu.VMEM) for n in range(len(args))
    ]
    return pl.pallas_call(
        kernel,
        out_shape=[shape(*out) if isinstance(out, tuple) else shape(out) for out in outs],
        in_specs=in_specs,
        out_specs=[pl.BlockSpec(memory_space=pltpu.VMEM) for _ in outs],
        scratch_shapes=list(scratch),
        name=name,
        cost_estimate=pl.CostEstimate(flops=flops, bytes_accessed=8_000_000, transcendentals=0),
        compiler_params=pltpu.CompilerParams(vmem_limit_bytes=40 * 1024 * 1024),
    )(*args)


def per_device(rhs, spacing_z, spacing_a, spacing_b, rotation):
    mats = matrices()
    group = lax.axis_index("grp")
    member = lax.axis_index("sub")
    groups = lax.axis_size("grp")
    members = lax.axis_size("sub")
    wide, narrow = jnp.float32, jnp.bfloat16
    vmem = pltpu.VMEM

    def shifted(value, axis, count, steps):
        return lax.ppermute(value, axis, [(n, (n + steps) % count) for n in range(count)])

    def neighbours(up, down):
        return shifted(up, "grp", groups, 1), shifted(down, "grp", groups, -1)

    own = rhs.reshape(512, OWN)
    left = shifted(own, "sub", members, 1)
    right = shifted(own, "sub", members, -1)
    rot = lax.dynamic_slice(rotation, (group,), (1,))
    ring = jnp.concatenate([spacing_a, spacing_a, spacing_a])
    columns = lax.dynamic_slice(ring, (spacing_a.shape[0] + member * COLS_DEV - LEFT,), (WIN,))
    geo = jnp.stack(
        [
            jnp.repeat(columns, RADIAL),
            jnp.tile(spacing_b, WIN),
            jnp.broadcast_to(spacing_z, (LANES,)),
        ]
    )
    geo = jnp.concatenate([geo, jnp.ones((5, LANES), wide)])
    lam, coef = call(tables_kernel, "tables", (geo, mats["modes"]), (4 * MODES, 24))
    field, up, down = call(
        window_kernel, "window", (rot, left, own, right, geo), (512, 136, 136), scalars=1
    )

    def solve(field, below, above):
        return call(
            solve_kernel,
            "solve",
            (field, below, above, lam, *mats["forward"], *mats["backward"]),
            (512, 512, 64, 64),
            (
                vmem((TILES, 640, TILE), wide),
                vmem((4 * TILES, EXT, TILE), wide),
                vmem((4, 2 * EXT, LANES), narrow),
                vmem((2 * MODES, LANES), narrow),
            ),
        )

    def advance(kind, args, outs):
        scratch = [
            vmem((TILES, 512, TILE), wide),
            vmem((4 * TILES, 128, TILE), wide),
            vmem((4, 256, LANES), narrow),
        ]
        if kind == 1:
            scratch.append(vmem((1024, LANES), narrow))
        return call(functools.partial(step_kernel, kind), f"step{kind}", args, outs, scratch)

    lower, upper = neighbours(up, down)
    share, local, up, down = solve(field, lower, upper)
    below, above = neighbours(up, down)
    total, field, up, down = advance(
        0, (local, below, above, share, coef, *mats["apply"]), (512, 512, 128, 128)
    )
    below, above = neighbours(up, down)
    share, local, up, down = solve(field, below, above)
    below, above = neighbours(up, down)
    total, field, up, down, coarse = advance(
        1,
        (local, below, above, total, total, share, coef, *mats["apply"], *mats["restrict"]),
        (512, 512, 16, 16, 64),
    )
    below, above = neighbours(up, down)
    total, field, up, down = call(
        coarse_kernel,
        "coarse",
        (coarse, below, above, lower, upper, geo, coef, mats["coarse"], mats["prolong"], total, field),
        (512, 512, 128, 128),
        (vmem((192, LANES), narrow),),
    )
    below, above = neighbours(up, down)
    share, local, up, down = solve(field, below, above)
    below, above = neighbours(up, down)
    step, total, field, up, down = advance(
        2, (local, below, above, total, share, coef, *mats["apply"]), (512, 512, 512, 128, 128)
    )
    below, above = neighbours(up, down)
    share, local, up, down = solve(field, below, above)
    below, above = neighbours(up, down)
    total, field, up, down = advance(
        3, (local, below, above, step, total, share, coef, *mats["apply"]), (512, 512, 64, 64)
    )
    below, above = neighbours(up, down)
    sol, res = call(
        finish_kernel,
        "finish",
        (rot, field, below, above, total),
        ((512, OWN), (512, OWN)),
        (vmem((TILES, 512, TILE), wide),),
        scalars=1,
    )
    return sol.reshape(rhs.shape), res.reshape(rhs.shape)


def solution(mesh):
    return jax.shard_map(
        per_device,
        mesh=mesh,
        in_specs=(P(None, None, None, ("grp", "sub")), P("grp"), P(), P(), P()),
        out_specs=(P(None, None, None, ("grp", "sub")), P(None, None, None, ("grp", "sub"))),
        check_vma=False,
    )
```

```python
import functools

import jax
import jax.numpy as jnp
import ml_dtypes
import numpy as np
from jax import lax
from jax.experimental import pallas as pl
from jax.experimental.pallas import tpu as pltpu
from jax.sharding import PartitionSpec as P

PTS = 8
CPTS = 4
COLS_DEV = 16
RADIAL = 16
SMOOTH = 2

WIN = 40
LEFT = 10
LANES = WIN * RADIAL
RINGS = ((8, 32), (4, 8), (32, 36), (0, 4), (36, 40))
OWN = COLS_DEV * RADIAL
CLASSES = ((0, 0), (0, 1), (1, 0), (1, 1))
INNER = 160
OUTER = 80
MODES = 256
TILE = 128
TILES = LANES // TILE
TERMS = 32
BATCH = 4

cheb_upper = 2.0
cheb_ratio = 0.1
theta = 0.5 * (cheb_upper + cheb_upper * cheb_ratio)
delta = 0.5 * (cheb_upper - cheb_upper * cheb_ratio)
sigma = theta / delta
rho_first = 1.0 / sigma
rho_second = 1.0 / (2.0 * sigma - rho_first)


def legendre_rows(gll_nodes, poly_order):
    values = np.zeros((gll_nodes.size, poly_order + 1))
    values[:, 0] = 1.0
    values[:, 1] = gll_nodes
    for degree in range(2, poly_order + 1):
        values[:, degree] = (
            (2 * degree - 1) * gll_nodes * values[:, degree - 1]
            - (degree - 1) * values[:, degree - 2]
        ) / degree
    return values


def jacobi_eigen(matrix):
    order = matrix.shape[0]
    current = matrix.copy()
    vectors = np.eye(order)
    for sweep in range(12):
        for first in range(order - 1):
            for second in range(first + 1, order):
                off_value = current[first, second]
                spread = current[second, second] - current[first, first]
                sense = np.where(spread >= 0.0, 1.0, -1.0)
                denom = spread + sense * np.sqrt(spread * spread + 4.0 * off_value * off_value)
                denom = np.where(denom == 0.0, 1.0, denom)
                tangent = 2.0 * off_value / denom
                cosine = 1.0 / np.sqrt(1.0 + tangent * tangent)
                sine = tangent * cosine
                rotate = np.eye(order)
                rotate[first, first] = cosine
                rotate[second, second] = cosine
                rotate[first, second] = sine
                rotate[second, first] = -sine
                current = rotate.T @ current @ rotate
                vectors = vectors @ rotate
    diag_ids = np.arange(order)
    return (current[diag_ids, diag_ids].copy(), vectors)


def lobatto(poly_order):
    gll_nodes = np.cos(np.pi * np.arange(poly_order + 1) / poly_order)
    for newton in range(100):
        values = legendre_rows(gll_nodes, poly_order)
        gll_nodes = gll_nodes - (gll_nodes * values[:, poly_order] - values[:, poly_order - 1]) / (
            (poly_order + 1) * values[:, poly_order]
        )
    values = legendre_rows(gll_nodes, poly_order)
    gll_nodes = gll_nodes[::-1].copy()
    top_poly = values[::-1, poly_order].copy()
    weights = 2.0 / (poly_order * (poly_order + 1) * top_poly**2)
    derivative = np.zeros((poly_order + 1, poly_order + 1))
    for row_index in range(poly_order + 1):
        for col_index in range(poly_order + 1):
            if row_index != col_index:
                derivative[row_index, col_index] = top_poly[row_index] / (
                    top_poly[col_index] * (gll_nodes[row_index] - gll_nodes[col_index])
                )
    derivative[0, 0] = -poly_order * (poly_order + 1) / 4.0
    derivative[poly_order, poly_order] = poly_order * (poly_order + 1) / 4.0
    stiffness = derivative.T @ (weights[:, None] * derivative)
    return (gll_nodes, weights, stiffness)


def element_tables():
    fine_nodes, fine_weights, fine_stiff = lobatto(PTS - 1)
    coarse_nodes, coarse_weights, coarse_stiff = lobatto(CPTS - 1)
    interp = np.ones((PTS, CPTS))
    for target_col in range(CPTS):
        for other_col in range(CPTS):
            if other_col != target_col:
                interp[:, target_col] *= (fine_nodes - coarse_nodes[other_col]) / (
                    coarse_nodes[target_col] - coarse_nodes[other_col]
                )
    poly_order = PTS - 1
    node_count = 3 * poly_order + 1
    joined_stiff = np.zeros((node_count, node_count))
    joined_mass = np.zeros(node_count)
    for piece_index in range(3):
        first_node = piece_index * poly_order
        joined_stiff[first_node : first_node + PTS, first_node : first_node + PTS] += fine_stiff
        joined_mass[first_node : first_node + PTS] += fine_weights
    kept = slice(poly_order - 1, 2 * poly_order + 2)
    root_mass = np.sqrt(joined_mass[kept])
    eigen_values, eigen_vectors = jacobi_eigen(
        joined_stiff[kept, kept] / root_mass[:, None] / root_mass[None, :]
    )
    eigen_basis = eigen_vectors / root_mass[:, None]
    coarse_diag = np.diag(coarse_stiff).copy()
    return fine_stiff, fine_weights, eigen_basis, eigen_values, interp, coarse_diag, coarse_weights


def split(table):
    high = table.astype(np.float32).astype(ml_dtypes.bfloat16)
    low = (table - high.astype(np.float64)).astype(np.float32).astype(ml_dtypes.bfloat16)
    return high, low


def kron3(first, second, third):
    return np.kron(first, np.kron(second, third))


def spread(values):
    terms = np.zeros((values.shape[0], TERMS), ml_dtypes.bfloat16)
    for at in range(3):
        high, rest = split(values[:, at])
        middle, low = split(values[:, at] - high.astype(np.float64))
        for n, part in enumerate((high, high, high, middle, middle, low)):
            terms[:, at * 6 + n] = part
    return terms


def matrices():
    stiff, weights, basis, values, interp, coarse_diag, coarse_weights = element_tables()
    parts = ([], [])
    for mode in range(PTS + 2):
        column = basis[:, mode]
        odd = np.abs(column + column[::-1]).sum() < np.abs(column - column[::-1]).sum()
        parts[int(odd)].append(mode)
    signs = (1.0, -1.0)
    pure = basis.copy()
    for parity in (0, 1):
        for mode in parts[parity]:
            pure[:, mode] = 0.5 * (basis[:, mode] + signs[parity] * basis[::-1, mode])
    center = pure[1:-1, :]
    edges = pure[[0, -1], :]

    def folded(matrix, parity):
        half = PTS // 2
        return 0.5 * (matrix[:half, :half] + signs[parity] * matrix[:half, ::-1][:, :half])

    mass = np.diag(weights)
    halved = np.ones(PTS // 2)
    halved[0] = 0.5
    forward_inner = np.zeros((4, MODES, INNER))
    forward_outer = np.zeros((4, MODES, OUTER))
    backward = np.zeros((4, PTS * 16, MODES))
    apply_inner = np.zeros((4, 320, 96))
    apply_outer = np.zeros((4, 192, 32))
    mode_values = np.ones((4, MODES, 3))
    for at, (pi, pk) in enumerate(CLASSES):
        ci, ck = center[:4, parts[pi]], center[:4, parts[pk]]
        ei, ek = edges[:1, parts[pi]], edges[:1, parts[pk]]
        count = len(parts[pi]) * len(parts[pk]) * (PTS + 2)
        rest = ci[1:]
        gap = lambda rows: np.zeros((rows, count))
        columns = [kron3(rest, ck, center), kron3(rest, ek, center), gap(8)]
        columns += [kron3(rest, ck, edges[:1]), gap(4), kron3(rest, ck, edges[1:]), gap(4)]
        forward_inner[at, :count] = np.concatenate(columns, axis=0).T
        columns = [kron3(ci[:1], ck, center), kron3(ei, ck, center), kron3(ci[:1], ek, center)]
        columns += [kron3(ci[:1], ck, edges[:1]), kron3(ci[:1], ck, edges[1:])]
        forward_outer[at, :count] = np.concatenate(columns, axis=0).T
        backward[at, :, :count] = kron3(halved[:, None] * ci, halved[:, None] * ck, center)
        vi, vk = values[parts[pi]], values[parts[pk]]
        ones = np.ones
        mode_values[at, :count, 0] = kron3(vi, ones(len(vk)), ones(PTS + 2))
        mode_values[at, :count, 1] = kron3(ones(len(vi)), vk, ones(PTS + 2))
        mode_values[at, :count, 2] = kron3(ones(len(vi)), ones(len(vk)), values)
        si, sk = folded(stiff, pi), folded(stiff, pk)
        mi, mk = folded(mass, pi), folded(mass, pk)
        along_z, along_a, along_b = kron3(si, mk, mass), kron3(mi, sk, mass), kron3(mi, mk, stiff)
        apply_inner[at] = np.concatenate([along_z[:, 32:], along_a[32:, 32:], along_b[32:, 32:]])
        apply_outer[at] = np.concatenate([along_z[:, :32], along_a[:32, :32], along_b[:32, :32]])
    mass_up, stiff_up = mass @ interp, stiff @ interp
    prolong = np.concatenate(
        [
            kron3(interp, interp, interp),
            kron3(stiff_up, mass_up, mass_up),
            kron3(mass_up, stiff_up, mass_up),
            kron3(mass_up, mass_up, stiff_up),
        ],
        axis=0,
    )
    restrict = kron3(interp.T, interp.T, interp.T)
    coarse = np.zeros((CPTS**3, 8))
    coarse[:, 0] = kron3(coarse_diag, coarse_weights, coarse_weights)
    coarse[:, 1] = kron3(coarse_weights, coarse_diag, coarse_weights)
    coarse[:, 2] = kron3(coarse_weights, coarse_weights, coarse_diag)

    def pair(table):
        high, low = split(table)
        return jnp.asarray(np.concatenate([high, high], axis=-1)), jnp.asarray(low)

    def triple(table):
        high, low = split(table)
        return jnp.asarray(np.concatenate([high, high, low], axis=-1))

    return {
        "forward_inner": triple(forward_inner),
        "forward_outer": triple(forward_outer),
        "backward": pair(backward),
        "apply_inner": triple(apply_inner),
        "apply_outer": triple(apply_outer),
        "restrict": pair(restrict),
        "prolong": triple(prolong),
        "modes": jnp.asarray(spread(mode_values.reshape(4 * MODES, 3))),
        "coarse": jnp.asarray(coarse.astype(np.float32)),
    }


def halves(value):
    high = value.astype(jnp.bfloat16)
    low = (value - high.astype(jnp.float32)).astype(jnp.bfloat16)
    return high, low


def dot(left, right):
    return jnp.dot(left, right, preferred_element_type=jnp.float32)


def join(tiles):
    return jnp.concatenate(tiles, axis=1)


def tiles_of(value):
    return [value[:, t * TILE : (t + 1) * TILE] for t in range(value.shape[1] // TILE)]


def radial_turn(value, steps):
    return join([pltpu.roll(tile, steps % TILE, axis=1) for tile in tiles_of(value)])


def column_turn(value, direction):
    tiles = tiles_of(value)
    count = len(tiles)
    lane = lax.broadcasted_iota(jnp.int32, tiles[0].shape, 1)
    near = [pltpu.roll(tile, (direction * RADIAL) % TILE, axis=1) for tile in tiles]
    far = lambda at: pltpu.roll(tiles[at], (TILE // 2 + direction * RADIAL) % TILE, axis=1)
    out = list(near)
    if direction < 0:
        high_end, low_end = lane >= TILE - RADIAL, (lane >= TILE // 2 - RADIAL) & (lane < TILE // 2)
        out[0] = jnp.where(high_end, near[1], near[0])
        out[1] = jnp.where(high_end, near[2], near[1])
        inner, outer, middle = 2, high_end, low_end
        edge = 0
    else:
        high_end, low_end = lane < RADIAL, (lane >= TILE // 2) & (lane < TILE // 2 + RADIAL)
        out[1] = jnp.where(high_end, near[0], near[1])
        out[2] = jnp.where(high_end, near[1], near[2])
        inner, outer, middle = 0, high_end, low_end
        edge = 2
    if count > 3:
        first_ring = far(3)
        out[inner] = jnp.where(outer, first_ring, out[inner])
        out[3] = jnp.where(middle, far(edge), near[3])
    if count > 4:
        out[3] = jnp.where(outer, far(4), out[3])
        out[4] = jnp.where(middle, first_ring, near[4])
    return join(out)


def lane_masks(rows, lanes):
    radial = lax.broadcasted_iota(jnp.int32, (rows, lanes), 1) % RADIAL
    keep_upper = (radial < RADIAL - 1).astype(jnp.float32)
    keep_lower = (radial > 0).astype(jnp.float32)
    return keep_upper, keep_lower


def chunks(lanes):
    return [(start, min(start + 2 * TILE, lanes)) for start in range(0, lanes, 2 * TILE)]


def point_factor(lanes):
    point = lax.broadcasted_iota(jnp.int32, (PTS, lanes), 0)
    radial = lax.broadcasted_iota(jnp.int32, (PTS, lanes), 1) % RADIAL
    shared = ((point == 0) & (radial > 0)) | ((point == PTS - 1) & (radial < RADIAL - 1))
    return jnp.where(shared, 0.5, 1.0)


def side_factor(i, k):
    return (0.5 if i in (0, PTS - 1) else 1.0) * (0.5 if k in (0, PTS - 1) else 1.0)


def plane_factor(factor, i):
    return jnp.concatenate([factor * side_factor(i, k) for k in range(PTS)])


def block(plane, k):
    start = plane * 64 + k * PTS
    return slice(start, start + PTS)


def load(ref, rows, tiles, base=0):
    return join([ref[base + t, rows, :] for t in range(tiles)])


def store(ref, rows, value, base=0):
    for t, tile in enumerate(tiles_of(value)):
        ref[base + t, rows, :] = tile


def assemble_sides(field, planes, tiles):
    batches = [planes[start : start + BATCH] for start in range(0, len(planes), BATCH)]
    for batch in batches:
        left = jnp.concatenate([load(field, block(plane, 0), tiles) for plane in batch])
        right = jnp.concatenate([load(field, block(plane, PTS - 1), tiles) for plane in batch])
        new_right = right + column_turn(left, -1)
        new_left = left + column_turn(right, 1)
        for at, plane in enumerate(batch):
            store(field, block(plane, PTS - 1), new_right[at * PTS : (at + 1) * PTS])
            store(field, block(plane, 0), new_left[at * PTS : (at + 1) * PTS])
    keep_upper, keep_lower = lane_masks(PTS * BATCH, tiles * TILE)
    for batch in batches:
        rows = len(batch) * PTS
        inner_at = [pl.ds(plane * 64, PTS, stride=PTS) for plane in batch]
        outer_at = [pl.ds(plane * 64 + PTS - 1, PTS, stride=PTS) for plane in batch]
        inner = jnp.concatenate([load(field, at, tiles) for at in inner_at])
        outer = jnp.concatenate([load(field, at, tiles) for at in outer_at])
        new_outer = outer + radial_turn(inner, -1) * keep_upper[:rows]
        new_inner = inner + radial_turn(outer, 1) * keep_lower[:rows]
        for at in range(len(batch)):
            store(field, outer_at[at], new_outer[at * PTS : (at + 1) * PTS])
            store(field, inner_at[at], new_inner[at * PTS : (at + 1) * PTS])


def fold(a, b, c, d):
    sum_k, diff_k = a + b, a - b
    sum_m, diff_m = c + d, c - d
    return sum_k + sum_m, sum_k - sum_m, diff_k + diff_m, diff_k - diff_m


def pack(parts, packed, rows, tiles):
    for c in range(4):
        for t in range(tiles):
            lanes = slice(t * TILE, (t + 1) * TILE)
            high, low = halves(parts[c * tiles + t, 0:rows, :])
            packed[c, 0:rows, lanes] = high
            packed[c, rows : 2 * rows, lanes] = low
            packed[c, 2 * rows : 3 * rows, lanes] = high


def unfold(ss, sa, as_, aa):
    sum_k, sum_m = ss + sa, ss - sa
    diff_k, diff_m = as_ + aa, as_ - aa
    return sum_k + diff_k, sum_k - diff_k, sum_m + diff_m, sum_m - diff_m


def mirrored(i, k):
    return (i, k), (PTS - 1 - i, k), (i, PTS - 1 - k), (PTS - 1 - i, PTS - 1 - k)


def coefficient_terms(values):
    rows = []
    for value in values:
        parts = []
        for _ in range(3):
            part = value.astype(jnp.bfloat16).astype(jnp.float32)
            parts.append(part)
            value = value - part
        high, middle, low = parts
        rows += [high, middle, low, high, middle, high]
    rows.append(jnp.zeros((TERMS - len(rows), value.shape[1]), jnp.float32))
    return jnp.concatenate(rows).astype(jnp.bfloat16)


def tables_kernel(geo, modes, own, lam, coef, kept):
    kept[...] = own[...]
    la, lb, lz = (geo[n : n + 1] for n in range(3))
    cz = la * lb / (2.0 * lz)
    ca = lz * lb / (2.0 * la)
    cb = lz * la / (2.0 * lb)
    for at, value in enumerate((cz, ca, cb)):
        coef[at * PTS : (at + 1) * PTS] = jnp.broadcast_to(value, (PTS, LANES))
    terms = coefficient_terms((cz, ca, cb))
    for start, stop in chunks(LANES):
        for c in range(4):
            here = slice(c * MODES, (c + 1) * MODES)
            lam[here, start:stop] = 1.0 / dot(modes[here], terms[:, start:stop])


def window(case, left, own, right, rows):
    shift = (COLS_DEV - LEFT - case) * RADIAL
    joined = join([left[rows], own, right[rows]])
    joined = pltpu.roll(joined, joined.shape[1] - shift, axis=1)[:, :LANES]
    first, *center, last = tiles_of(joined)
    lane = lax.broadcasted_iota(jnp.int32, first.shape, 1)
    half = TILE // 2
    near = jnp.where(lane < half, pltpu.roll(first, half, axis=1), pltpu.roll(last, half, axis=1))
    return join([*center, near, jnp.where(lane < half, first, last)])


def outer_kernel(rot, left, own, right, geo, field, up, down, inner):
    factor = point_factor(LANES)
    for case in range(4):

        @pl.when(rot[0] == case)
        def _(case=case):
            for at, i in enumerate((0, 1, 6, 7)):
                here = slice(at * 64, at * 64 + 64)
                value = window(case, left, own[i * 64 : i * 64 + 64], right, here)
                field[here] = value * plane_factor(factor, i)

    up[0:128] = field[128:256]
    down[0:128] = field[0:128]
    length = jnp.broadcast_to(geo[2:3], (PTS, LANES))
    up[128:136] = length
    down[128:136] = length
    inner[...] = own[128:384]


def inner_kernel(rot, left, own, right, field):
    factor = point_factor(LANES)
    for case in range(4):

        @pl.when(rot[0] == case)
        def _(case=case):
            for at, i in enumerate((2, 3, 4, 5)):
                here = slice(at * 64, at * 64 + 64)
                field[here] = window(case, left, own[here], right, here) * plane_factor(factor, i)


def put(parts, tiles, at, values):
    for c in range(4):
        store(parts, at, values[c], c * tiles)


def layer(value, at):
    return value[at * PTS : (at + 1) * PTS]


def column_halos(field, planes, wide, lanes):
    before = jnp.concatenate([load(field, block(plane, PTS - 2), wide) for plane in planes])
    after = jnp.concatenate([load(field, block(plane, 1), wide) for plane in planes])
    return column_turn(before, 1)[:, :lanes], column_turn(after, -1)[:, :lanes]


def radial_halos(parts, tiles, count):
    masks = lane_masks(4 * count, tiles * TILE)
    found = []
    for first, steps, keep in ((PTS - 2, 1, masks[1]), (1, -1, masks[0])):
        rows = pl.ds(first, count, stride=PTS)
        values = [load(parts, rows, tiles, c * tiles) for c in range(4)]
        values = radial_turn(jnp.concatenate(values), steps) * keep
        found.append([values[c * count : (c + 1) * count] for c in range(4)])
    return found


def solve_inner_kernel(start_up, wide, tiles, *refs):
    if start_up:
        outer, inner, *refs = refs
        planes = [outer[64:128]] + [inner[i * 64 : i * 64 + 64] for i in range(4)] + [outer[128:192]]
    else:
        field, *refs = refs
        planes = [field[i * 64 : i * 64 + 64] for i in range(1, 7)]
    fwd, share, spectrum, ext, parts, packed = refs
    lanes = tiles * TILE
    factor = point_factor(lanes)
    for at, plane in enumerate(planes):
        store(ext, slice(at * 64, at * 64 + 64), plane)
    assemble_sides(ext, range(6), wide)
    for at in range(6):
        here = slice(at * 64, at * 64 + 64)
        share[here] = load(ext, here, tiles) * plane_factor(factor, at + 1)
    for i in range(3):
        for k in range(4):
            corners = ((i, k), (5 - i, k), (i, 7 - k), (5 - i, 7 - k))
            values = fold(*(load(ext, block(p, q), tiles) for p, q in corners))
            put(parts, tiles, block(0, i * 4 + k), values)
    before, after = column_halos(ext, range(6), wide, lanes)
    for i in range(3):
        values = fold(layer(before, i), layer(before, 5 - i), layer(after, i), layer(after, 5 - i))
        put(parts, tiles, slice(96 + i * 8, 104 + i * 8), values)
    put(parts, tiles, slice(120, 128), [jnp.zeros((PTS, lanes), jnp.float32)] * 4)
    lower, upper = radial_halos(parts, tiles, 16)
    put(parts, tiles, slice(128, 144), lower)
    put(parts, tiles, slice(144, 160), upper)
    pack(parts, packed, INNER, tiles)
    for c in range(4):
        for start, stop in chunks(lanes):
            spectrum[c * MODES : (c + 1) * MODES, start:stop] = dot(fwd[c], packed[c, :, start:stop])


def solve_outer_kernel(start_up, wide, tiles, *refs):
    field, below, above, spectrum, lam, fwd, bwd, bwd_low = refs[:8]
    share, out, up, down, ext, parts, packed, modes = refs[8:]
    lanes = tiles * TILE
    factor = point_factor(lanes)
    last = 192 if start_up else 448
    store(ext, slice(0, 64), below[0:64])
    store(ext, slice(64, 128), field[0:64] + below[64:128])
    store(ext, slice(128, 192), field[last : last + 64] + above[0:64])
    store(ext, slice(192, 256), above[64:128])
    assemble_sides(ext, range(4), wide)
    share[0:64] = load(ext, slice(64, 128), tiles) * plane_factor(factor, 0)
    share[64:128] = load(ext, slice(128, 192), tiles) * plane_factor(factor, 7)
    for k in range(4):
        for at, (p, q) in enumerate(((1, 2), (0, 3))):
            corners = ((p, k), (q, k), (p, 7 - k), (q, 7 - k))
            values = fold(*(load(ext, block(*corner), tiles) for corner in corners))
            put(parts, tiles, block(0, at * 4 + k), values)
    before, after = column_halos(ext, (1, 2), wide, lanes)
    values = fold(layer(before, 0), layer(before, 1), layer(after, 0), layer(after, 1))
    put(parts, tiles, slice(64, 72), values)
    lower, upper = radial_halos(parts, tiles, 4)
    put(parts, tiles, slice(72, 80), [jnp.concatenate(pair) for pair in zip(lower, upper)])
    pack(parts, packed, OUTER, tiles)
    for c in range(4):
        for start, stop in chunks(lanes):
            here = slice(c * MODES, (c + 1) * MODES)
            value = dot(fwd[c], packed[c, :, start:stop]) + spectrum[here, start:stop]
            modes[0:MODES, start:stop], modes[MODES:, start:stop] = halves(value * lam[here, start:stop])
        for start, stop in chunks(lanes):
            value = dot(bwd[c], modes[:, start:stop])
            value = value + dot(bwd_low[c], modes[0:MODES, start:stop])
            store(parts, slice(0, 128), value, c * tiles + start // TILE)
    for i in range(4):
        for k in range(4):
            classes = (load(parts, block(0, i * 4 + k), tiles, c * tiles) for c in range(4))
            for (p, q), value in zip(mirrored(i, k), unfold(*classes)):
                out[block(p, q)] = value * factor
    up[...] = out[448:512]
    down[...] = out[0:64]


def stepped(kind, value, before):
    if kind in (0, 2):
        return value * (1.0 / theta)
    return before * (rho_second * rho_first) + value * (2.0 * rho_second / delta)


def step_inner_kernel(kind, wide, tiles, *refs):
    take = iter(refs)
    local = next(take)
    before = next(take) if kind in (1, 3) else None
    total = next(take) if kind != 0 else None
    coef, app = next(take), next(take)
    step = next(take) if kind in (0, 2) else None
    sum_out = next(take) if kind != 0 else None
    image, ext, parts, packed = take
    lanes = tiles * TILE
    for i in range(6):
        store(ext, slice(i * 64, i * 64 + 64), local[i * 64 + 64 : i * 64 + 128])
    assemble_sides(ext, range(6), wide)
    for i in range(6):
        here = slice(i * 64, i * 64 + 64)
        value = stepped(kind, load(ext, here, tiles), None if before is None else before[here, :lanes])
        if step is not None:
            step[here] = value
        if sum_out is not None:
            sum_out[here] = total[here, :lanes] + value
        store(ext, here, value)
    for i in range(3):
        for k in range(4):
            corners = ((i, k), (5 - i, k), (i, 7 - k), (5 - i, 7 - k))
            values = fold(*(load(ext, block(p, q), tiles) for p, q in corners))
            put(parts, tiles, block(0, i * 4 + k), values)
    pack(parts, packed, 96, tiles)
    for c in range(4):
        for start, stop in chunks(lanes):
            terms = dot(app[c], packed[c, :, start:stop]).reshape(40, PTS, stop - start)
            value = terms[0:16] * coef[0:8, start:stop]
            sides = terms[16:28] * coef[8:16, start:stop] + terms[28:40] * coef[16:24, start:stop]
            value = jnp.concatenate([value[0:4], value[4:16] + sides])
            image[c * 128 : (c + 1) * 128, start:stop] = value.reshape(128, stop - start)


def step_outer_kernel(kind, wide, tiles, *refs):
    take = iter(refs)
    local, below, above = next(take), next(take), next(take)
    before = next(take) if kind in (1, 3) else None
    total = next(take) if kind != 0 else None
    share_inner, share_outer, image, coef, app = (next(take) for _ in range(5))
    res, res_low = (next(take), next(take)) if kind == 1 else (None, None)
    step = next(take) if kind in (0, 2) else None
    sum_out = next(take) if kind != 0 else None
    field, up, down = next(take), next(take), next(take)
    coarse = next(take) if kind == 1 else None
    ext, parts, packed = next(take), next(take), next(take)
    split_field = next(take) if kind == 1 else None
    lanes = tiles * TILE
    store(ext, slice(0, 64), local[0:64] + below[...])
    store(ext, slice(64, 128), local[448:512] + above[...])
    assemble_sides(ext, range(2), wide)
    for at in range(2):
        here = slice(at * 64, at * 64 + 64)
        value = stepped(kind, load(ext, here, tiles), None if before is None else before[here, :lanes])
        if step is not None:
            step[here] = value
        if sum_out is not None:
            sum_out[here] = total[here, :lanes] + value
        store(ext, here, value)
    for k in range(4):
        corners = ((0, k), (1, k), (0, 7 - k), (1, 7 - k))
        values = fold(*(load(ext, block(p, q), tiles) for p, q in corners))
        put(parts, tiles, block(0, k), values)
    pack(parts, packed, 32, tiles)
    for c in range(4):
        for start, stop in chunks(lanes):
            terms = dot(app[c], packed[c, :, start:stop]).reshape(24, PTS, stop - start)
            value = terms[0:16] * coef[0:8, start:stop]
            sides = terms[16:20] * coef[8:16, start:stop] + terms[20:24] * coef[16:24, start:stop]
            value = jnp.concatenate([value[0:4] + sides, value[4:16]]).reshape(128, stop - start)
            value = value + image[c * 128 : (c + 1) * 128, start:stop]
            store(parts, slice(0, 128), value, c * tiles + start // TILE)
    for i in range(4):
        for k in range(4):
            classes = (load(parts, block(0, i * 4 + k), tiles, c * tiles) for c in range(4))
            for (p, q), value in zip(mirrored(i, k), unfold(*classes)):
                if p in (0, 7):
                    shared = share_outer[block(p // 7, q), :lanes]
                else:
                    shared = share_inner[block(p - 1, q), :lanes]
                field[block(p, q)] = shared - value
    if kind == 1:
        split_field[0:512], split_field[512:1024] = halves(field[...])
        for start, stop in chunks(lanes):
            value = dot(res[...], split_field[:, start:stop])
            coarse[:, start:stop] = value + dot(res_low[...], split_field[0:512, start:stop])
        up[...] = coarse[48:64]
        down[...] = coarse[0:16]
    elif kind == 3:
        up[...] = field[448:512]
        down[...] = field[0:64]
    else:
        up[...] = field[384:512]
        down[...] = field[0:128]


def assemble_coarse(value):
    lanes = value.shape[1]
    row = lax.broadcasted_iota(jnp.int32, (64, lanes), 0)
    keep_upper, keep_lower = lane_masks(64, lanes)
    first = (row % 16) < 4
    last = (row % 16) >= 12
    over = pltpu.roll(column_turn(value, -1), 12, axis=0)
    under = pltpu.roll(column_turn(value, 1), 64 - 12, axis=0)
    value = value + jnp.where(last, over, 0.0) + jnp.where(first, under, 0.0)
    first = (row % 4) == 0
    last = (row % 4) == 3
    over = pltpu.roll(radial_turn(value, -1) * keep_upper, 3, axis=0)
    under = pltpu.roll(radial_turn(value, 1) * keep_lower, 64 - 3, axis=0)
    return value + jnp.where(last, over, 0.0) + jnp.where(first, under, 0.0)


def diagonal_kernel(lower, upper, geo, table, scale):
    lanes = scale.shape[1]
    la, lb = geo[0:1, :lanes], geo[1:2, :lanes]

    def local(lz, rows):
        return (
            la * lb / (2.0 * lz) * table[rows, 0:1]
            + lz * lb / (2.0 * la) * table[rows, 1:2]
            + lz * la / (2.0 * lb) * table[rows, 2:3]
        )

    value = local(geo[2:3, :lanes], slice(0, 64))
    first = value[0:16] + local(lower[128:129, :lanes], slice(48, 64))
    last = value[48:64] + local(upper[128:129, :lanes], slice(0, 16))
    scale[...] = assemble_coarse(jnp.concatenate([first, value[16:48], last]))


def coarse_kernel(local, below, above, scale, coef, prolong, *refs):
    total_inner, total_outer, field, sum_inner, sum_outer, out, up, down, packed = refs
    lanes = local.shape[1]
    value = local[...]
    value = jnp.concatenate([value[0:16] + below[...], value[16:48], value[48:64] + above[...]])
    value = assemble_coarse(value) / scale[...]
    high, low = halves(value)
    packed[0:64] = high
    packed[64:128] = low
    packed[128:192] = high
    for start, stop in chunks(lanes):
        for i in range(PTS):
            here = slice(i * 64, i * 64 + 64)
            sides = (8, PTS, stop - start)
            terms = [
                dot(prolong[n * 512 + i * 64 : n * 512 + i * 64 + 64], packed[:, start:stop]) for n in range(4)
            ]
            if i in (0, 7):
                at = slice(i // 7 * 64, i // 7 * 64 + 64)
                sum_outer[at, start:stop] = total_outer[at, start:stop] + terms[0]
            else:
                at = slice(i * 64 - 64, i * 64)
                sum_inner[at, start:stop] = total_inner[at, start:stop] + terms[0]
            value = (
                terms[1].reshape(sides) * coef[0:8, start:stop]
                + terms[2].reshape(sides) * coef[8:16, start:stop]
                + terms[3].reshape(sides) * coef[16:24, start:stop]
            )
            out[here, start:stop] = field[here, start:stop] - value.reshape(64, stop - start)
    up[...] = out[384:512]
    down[...] = out[0:128]


def finish_inner_kernel(rot, local, total_inner, total_outer, sol, res, ext):
    tiles = local.shape[1] // TILE
    for i in range(6):
        store(ext, slice(i * 64, i * 64 + 64), local[i * 64 + 64 : i * 64 + 128])
    assemble_sides(ext, range(6), tiles)
    for case in range(4):

        @pl.when(rot[0] == case)
        def _(case=case):
            start = (LEFT + case - RINGS[0][0]) * RADIAL
            for plane in range(PTS):
                here = slice(plane * 64, plane * 64 + 64)
                if plane in (0, 7):
                    at = plane // 7 * 64
                    sol[here] = total_outer[at : at + 64, start : start + OWN]
                else:
                    before = slice(plane * 64 - 64, plane * 64)
                    sol[here] = total_inner[before, start : start + OWN]
                    res[before] = load(ext, before, tiles)[:, start : start + OWN]


def finish_outer_kernel(rot, local, below, above, inner, res, ext):
    tiles = local.shape[1] // TILE
    store(ext, slice(0, 64), local[0:64] + below[...])
    store(ext, slice(64, 128), local[448:512] + above[...])
    assemble_sides(ext, range(2), tiles)
    res[64:448] = inner[...]
    for case in range(4):

        @pl.when(rot[0] == case)
        def _(case=case):
            start = (LEFT + case - RINGS[0][0]) * RADIAL
            res[0:64] = load(ext, slice(0, 64), tiles)[:, start : start + OWN]
            res[448:512] = load(ext, slice(64, 128), tiles)[:, start : start + OWN]


def call(kernel, name, args, outs, scratch=(), scalars=0, flops=0):
    in_specs = [
        pl.BlockSpec(memory_space=pltpu.SMEM if n < scalars else pltpu.VMEM) for n in range(len(args))
    ]
    return pl.pallas_call(
        kernel,
        out_shape=[jax.ShapeDtypeStruct(out, jnp.float32) for out in outs],
        in_specs=in_specs,
        out_specs=[pl.BlockSpec(memory_space=pltpu.VMEM) for _ in outs],
        scratch_shapes=list(scratch),
        name=name,
        cost_estimate=pl.CostEstimate(flops=flops, bytes_accessed=4_000_000, transcendentals=0),
        compiler_params=pltpu.CompilerParams(vmem_limit_bytes=40 * 1024 * 1024),
    )(*args)


def per_device(rhs, spacing_z, spacing_a, spacing_b, rotation):
    mats = matrices()
    group = lax.axis_index("grp")
    member = lax.axis_index("sub")
    groups = lax.axis_size("grp")
    members = lax.axis_size("sub")
    wide, narrow = jnp.float32, jnp.bfloat16
    vmem = pltpu.VMEM

    def shifted(value, axis, count, steps):
        return lax.ppermute(value, axis, [(n, (n + steps) % count) for n in range(count)])

    def neighbours(up, down):
        return shifted(up, "grp", groups, 1), shifted(down, "grp", groups, -1)

    def beside(value):
        return shifted(value, "sub", members, 1), shifted(value, "sub", members, -1)

    def shapes(tiles, *rows):
        return tuple((count, tiles * TILE) for count in rows)

    own = rhs.reshape(512, OWN)
    left, right = beside(jnp.concatenate([own[0:128], own[384:512]]))
    rot = lax.dynamic_slice(rotation, (group,), (1,))
    ring = jnp.concatenate([spacing_a, spacing_a, spacing_a])
    columns = lax.dynamic_slice(ring, (spacing_a.shape[0] + member * COLS_DEV - LEFT,), (WIN,))
    columns = jnp.concatenate([columns[start:stop] for start, stop in RINGS])
    geo = jnp.stack(
        [
            jnp.repeat(columns, RADIAL),
            jnp.tile(spacing_b, WIN),
            jnp.broadcast_to(spacing_z, (LANES,)),
        ]
    )
    geo = jnp.concatenate([geo, jnp.ones((5, LANES), wide)])
    lam, coef, own = call(
        tables_kernel, "tables", (geo, mats["modes"], own), ((4 * MODES, LANES), (24, LANES), (512, OWN))
    )
    outer, up, down, inner = call(
        outer_kernel,
        "outer",
        (rot, left, own, right, geo),
        ((256, LANES), (136, LANES), (136, LANES), (256, OWN)),
        scalars=1,
    )
    lower, upper = neighbours(up, down)
    left, right = beside(inner)
    (inner,) = call(inner_kernel, "inner", (rot, left, inner, right), ((256, LANES),), scalars=1)

    def solve(fields, below, above, before, tiles):
        lanes = tiles * TILE
        start_up = len(fields) == 2
        share_inner, spectrum = call(
            functools.partial(solve_inner_kernel, start_up, before, tiles),
            "solve_inner",
            (*fields, mats["forward_inner"]),
            shapes(tiles, 384, 4 * MODES),
            (
                vmem((before, 384, TILE), wide),
                vmem((4 * tiles, INNER, TILE), wide),
                vmem((4, 3 * INNER, lanes), narrow),
            ),
        )
        share_outer, local, up, down = call(
            functools.partial(solve_outer_kernel, start_up, before, tiles),
            "solve_outer",
            (fields[0], below, above, spectrum, lam, mats["forward_outer"], *mats["backward"]),
            shapes(tiles, 128, 512, 64, 64),
            (
                vmem((before, 256, TILE), wide),
                vmem((4 * tiles, 128, TILE), wide),
                vmem((4, 3 * OUTER, lanes), narrow),
                vmem((2 * MODES, lanes), narrow),
            ),
        )
        return (share_inner, share_outer), local, neighbours(up, down)

    def advance(kind, local, messages, share, before, total, width, tiles):
        lanes = tiles * TILE

        def scratch(rows, folded):
            return [
                vmem((width, rows, TILE), wide),
                vmem((4 * tiles, 128, TILE), wide),
                vmem((4, folded, lanes), narrow),
            ]

        def pick(at):
            return [pair[at] for pair in (before, total) if pair is not None]

        kept = [count for count, used in ((1, kind in (0, 2)), (1, kind != 0)) if used]
        *inner, image = call(
            functools.partial(step_inner_kernel, kind, width, tiles),
            f"step{kind}_inner",
            (local, *pick(0), coef, mats["apply_inner"]),
            shapes(tiles, *(384 for _ in kept), 512),
            scratch(384, 288),
        )
        sent = {0: 128, 1: 16, 2: 128, 3: 64}[kind]
        extra = scratch(128, 96)
        if kind == 1:
            extra.append(vmem((1024, lanes), narrow))
        out = call(
            functools.partial(step_outer_kernel, kind, width, tiles),
            f"step{kind}_outer",
            (
                *(local, *messages, *pick(1), *share, image, coef, mats["apply_outer"]),
                *(mats["restrict"] if kind == 1 else ()),
            ),
            shapes(tiles, *(128 for _ in kept), 512, sent, sent, *((64,) if kind == 1 else ())),
            extra,
        )
        outer, (field, up, down, *coarse) = out[: len(kept)], out[len(kept) :]
        return list(zip(inner, outer)), field, neighbours(up, down), *coarse

    share, local, messages = solve((outer, inner), lower, upper, 5, 5)
    (step,), field, messages = advance(0, local, messages, share, None, None, 5, 5)
    share, local, messages = solve((field,), *messages, 5, 5)
    (total,), field, messages, coarse = advance(1, local, messages, share, step, step, 5, 4)
    (scale,) = call(diagonal_kernel, "diagonal", (lower, upper, geo, mats["coarse"]), shapes(4, 64))
    *total, field, up, down = call(
        coarse_kernel,
        "coarse",
        (coarse, *messages, scale, coef, mats["prolong"], *total, field),
        shapes(4, 384, 128, 512, 128, 128),
        (vmem((192, 4 * TILE), narrow),),
    )
    share, local, messages = solve((field,), *neighbours(up, down), 4, 4)
    (step, total), field, messages = advance(2, local, messages, share, None, total, 4, 4)
    share, local, messages = solve((field,), *messages, 4, 3)
    (total,), field, messages = advance(3, local, messages, share, step, total, 3, 3)
    sol, inner = call(
        finish_inner_kernel,
        "finish_inner",
        (rot, field, *total),
        ((512, OWN), (384, OWN)),
        (vmem((3, 384, TILE), wide),),
        scalars=1,
    )
    (res,) = call(
        finish_outer_kernel,
        "finish_outer",
        (rot, field, *messages, inner),
        ((512, OWN),),
        (vmem((3, 128, TILE), wide),),
        scalars=1,
    )
    return sol.reshape(rhs.shape), res.reshape(rhs.shape)


def solution(mesh):
    return jax.shard_map(
        per_device,
        mesh=mesh,
        in_specs=(P(None, None, None, ("grp", "sub")), P("grp"), P(), P(), P()),
        out_specs=(P(None, None, None, ("grp", "sub")), P(None, None, None, ("grp", "sub"))),
        check_vma=False,
    )
```

```python
import functools

import jax
import jax.numpy as jnp
import ml_dtypes
import numpy as np
from jax import lax
from jax.experimental import pallas as pl
from jax.experimental.pallas import tpu as pltpu
from jax.sharding import PartitionSpec as P

PTS = 8
CPTS = 4
COLS_DEV = 16
RADIAL = 16
SMOOTH = 2

WIN = 40
LEFT = 10
LANES = WIN * RADIAL
RINGS = ((8, 32), (4, 8), (32, 36), (0, 4), (36, 40))
OWN = COLS_DEV * RADIAL
CLASSES = ((0, 0), (0, 1), (1, 0), (1, 1))
INNER = 160
OUTER = 80
MODES = 256
TILE = 128
TILES = LANES // TILE
TERMS = 32
BATCH = 4
EARLY = 20_000_000_000

cheb_upper = 2.0
cheb_ratio = 0.1
theta = 0.5 * (cheb_upper + cheb_upper * cheb_ratio)
delta = 0.5 * (cheb_upper - cheb_upper * cheb_ratio)
sigma = theta / delta
rho_first = 1.0 / sigma
rho_second = 1.0 / (2.0 * sigma - rho_first)


def legendre_rows(gll_nodes, poly_order):
    values = np.zeros((gll_nodes.size, poly_order + 1))
    values[:, 0] = 1.0
    values[:, 1] = gll_nodes
    for degree in range(2, poly_order + 1):
        values[:, degree] = (
            (2 * degree - 1) * gll_nodes * values[:, degree - 1]
            - (degree - 1) * values[:, degree - 2]
        ) / degree
    return values


def jacobi_eigen(matrix):
    order = matrix.shape[0]
    current = matrix.copy()
    vectors = np.eye(order)
    for sweep in range(12):
        for first in range(order - 1):
            for second in range(first + 1, order):
                off_value = current[first, second]
                spread = current[second, second] - current[first, first]
                sense = np.where(spread >= 0.0, 1.0, -1.0)
                denom = spread + sense * np.sqrt(spread * spread + 4.0 * off_value * off_value)
                denom = np.where(denom == 0.0, 1.0, denom)
                tangent = 2.0 * off_value / denom
                cosine = 1.0 / np.sqrt(1.0 + tangent * tangent)
                sine = tangent * cosine
                rotate = np.eye(order)
                rotate[first, first] = cosine
                rotate[second, second] = cosine
                rotate[first, second] = sine
                rotate[second, first] = -sine
                current = rotate.T @ current @ rotate
                vectors = vectors @ rotate
    diag_ids = np.arange(order)
    return (current[diag_ids, diag_ids].copy(), vectors)


def lobatto(poly_order):
    gll_nodes = np.cos(np.pi * np.arange(poly_order + 1) / poly_order)
    for newton in range(100):
        values = legendre_rows(gll_nodes, poly_order)
        gll_nodes = gll_nodes - (gll_nodes * values[:, poly_order] - values[:, poly_order - 1]) / (
            (poly_order + 1) * values[:, poly_order]
        )
    values = legendre_rows(gll_nodes, poly_order)
    gll_nodes = gll_nodes[::-1].copy()
    top_poly = values[::-1, poly_order].copy()
    weights = 2.0 / (poly_order * (poly_order + 1) * top_poly**2)
    derivative = np.zeros((poly_order + 1, poly_order + 1))
    for row_index in range(poly_order + 1):
        for col_index in range(poly_order + 1):
            if row_index != col_index:
                derivative[row_index, col_index] = top_poly[row_index] / (
                    top_poly[col_index] * (gll_nodes[row_index] - gll_nodes[col_index])
                )
    derivative[0, 0] = -poly_order * (poly_order + 1) / 4.0
    derivative[poly_order, poly_order] = poly_order * (poly_order + 1) / 4.0
    stiffness = derivative.T @ (weights[:, None] * derivative)
    return (gll_nodes, weights, stiffness)


def element_tables():
    fine_nodes, fine_weights, fine_stiff = lobatto(PTS - 1)
    coarse_nodes, coarse_weights, coarse_stiff = lobatto(CPTS - 1)
    interp = np.ones((PTS, CPTS))
    for target_col in range(CPTS):
        for other_col in range(CPTS):
            if other_col != target_col:
                interp[:, target_col] *= (fine_nodes - coarse_nodes[other_col]) / (
                    coarse_nodes[target_col] - coarse_nodes[other_col]
                )
    poly_order = PTS - 1
    node_count = 3 * poly_order + 1
    joined_stiff = np.zeros((node_count, node_count))
    joined_mass = np.zeros(node_count)
    for piece_index in range(3):
        first_node = piece_index * poly_order
        joined_stiff[first_node : first_node + PTS, first_node : first_node + PTS] += fine_stiff
        joined_mass[first_node : first_node + PTS] += fine_weights
    kept = slice(poly_order - 1, 2 * poly_order + 2)
    root_mass = np.sqrt(joined_mass[kept])
    eigen_values, eigen_vectors = jacobi_eigen(
        joined_stiff[kept, kept] / root_mass[:, None] / root_mass[None, :]
    )
    eigen_basis = eigen_vectors / root_mass[:, None]
    coarse_diag = np.diag(coarse_stiff).copy()
    return fine_stiff, fine_weights, eigen_basis, eigen_values, interp, coarse_diag, coarse_weights


def split(table):
    high = table.astype(np.float32).astype(ml_dtypes.bfloat16)
    low = (table - high.astype(np.float64)).astype(np.float32).astype(ml_dtypes.bfloat16)
    return high, low


def kron3(first, second, third):
    return np.kron(first, np.kron(second, third))


def spread(values):
    terms = np.zeros((values.shape[0], TERMS), ml_dtypes.bfloat16)
    for at in range(3):
        high, rest = split(values[:, at])
        middle, low = split(values[:, at] - high.astype(np.float64))
        for n, part in enumerate((high, high, high, middle, middle, low)):
            terms[:, at * 6 + n] = part
    return terms


def matrices():
    stiff, weights, basis, values, interp, coarse_diag, coarse_weights = element_tables()
    parts = ([], [])
    for mode in range(PTS + 2):
        column = basis[:, mode]
        odd = np.abs(column + column[::-1]).sum() < np.abs(column - column[::-1]).sum()
        parts[int(odd)].append(mode)
    signs = (1.0, -1.0)
    pure = basis.copy()
    for parity in (0, 1):
        for mode in parts[parity]:
            pure[:, mode] = 0.5 * (basis[:, mode] + signs[parity] * basis[::-1, mode])
    center = pure[1:-1, :]
    edges = pure[[0, -1], :]

    def folded(matrix, parity):
        half = PTS // 2
        return 0.5 * (matrix[:half, :half] + signs[parity] * matrix[:half, ::-1][:, :half])

    mass = np.diag(weights)
    halved = np.ones(PTS // 2)
    halved[0] = 0.5
    forward_inner = np.zeros((4, MODES, INNER))
    forward_outer = np.zeros((4, MODES, OUTER))
    backward = np.zeros((4, PTS * 16, MODES))
    apply_inner = np.zeros((4, 320, 96))
    apply_outer = np.zeros((4, 192, 32))
    mode_values = np.ones((4, MODES, 3))
    for at, (pi, pk) in enumerate(CLASSES):
        ci, ck = center[:4, parts[pi]], center[:4, parts[pk]]
        ei, ek = edges[:1, parts[pi]], edges[:1, parts[pk]]
        count = len(parts[pi]) * len(parts[pk]) * (PTS + 2)
        rest = ci[1:]
        gap = lambda rows: np.zeros((rows, count))
        columns = [kron3(rest, ck, center), kron3(rest, ek, center), gap(8)]
        columns += [kron3(rest, ck, edges[:1]), gap(4), kron3(rest, ck, edges[1:]), gap(4)]
        forward_inner[at, :count] = np.concatenate(columns, axis=0).T
        columns = [kron3(ci[:1], ck, center), kron3(ei, ck, center), kron3(ci[:1], ek, center)]
        columns += [kron3(ci[:1], ck, edges[:1]), kron3(ci[:1], ck, edges[1:])]
        forward_outer[at, :count] = np.concatenate(columns, axis=0).T
        backward[at, :, :count] = kron3(halved[:, None] * ci, halved[:, None] * ck, center)
        vi, vk = values[parts[pi]], values[parts[pk]]
        ones = np.ones
        mode_values[at, :count, 0] = kron3(vi, ones(len(vk)), ones(PTS + 2))
        mode_values[at, :count, 1] = kron3(ones(len(vi)), vk, ones(PTS + 2))
        mode_values[at, :count, 2] = kron3(ones(len(vi)), ones(len(vk)), values)
        si, sk = folded(stiff, pi), folded(stiff, pk)
        mi, mk = folded(mass, pi), folded(mass, pk)
        along_z, along_a, along_b = kron3(si, mk, mass), kron3(mi, sk, mass), kron3(mi, mk, stiff)
        apply_inner[at] = np.concatenate([along_z[:, 32:], along_a[32:, 32:], along_b[32:, 32:]])
        apply_outer[at] = np.concatenate([along_z[:, :32], along_a[:32, :32], along_b[:32, :32]])
    mass_up, stiff_up = mass @ interp, stiff @ interp
    prolong = np.concatenate(
        [
            kron3(interp, interp, interp),
            kron3(stiff_up, mass_up, mass_up),
            kron3(mass_up, stiff_up, mass_up),
            kron3(mass_up, mass_up, stiff_up),
        ],
        axis=0,
    )
    restrict = kron3(interp.T, interp.T, interp.T)
    coarse = np.zeros((CPTS**3, 8))
    coarse[:, 0] = kron3(coarse_diag, coarse_weights, coarse_weights)
    coarse[:, 1] = kron3(coarse_weights, coarse_diag, coarse_weights)
    coarse[:, 2] = kron3(coarse_weights, coarse_weights, coarse_diag)

    def pair(table):
        high, low = split(table)
        return jnp.asarray(np.concatenate([high, high], axis=-1)), jnp.asarray(low)

    def triple(table):
        high, low = split(table)
        return jnp.asarray(np.concatenate([high, high, low], axis=-1))

    return {
        "forward_inner": triple(forward_inner),
        "forward_outer": triple(forward_outer),
        "backward_outer": pair(backward[:, :32]),
        "backward_inner": pair(backward[:, 32:]),
        "apply_inner": triple(apply_inner),
        "apply_outer": triple(apply_outer),
        "restrict": pair(restrict),
        "prolong": triple(prolong),
        "modes": jnp.asarray(spread(mode_values.reshape(4 * MODES, 3))),
        "coarse": jnp.asarray(coarse.astype(np.float32)),
    }


def halves(value):
    high = value.astype(jnp.bfloat16)
    low = (value - high.astype(jnp.float32)).astype(jnp.bfloat16)
    return high, low


def dot(left, right):
    return jnp.dot(left, right, preferred_element_type=jnp.float32)


def join(tiles):
    return jnp.concatenate(tiles, axis=1)


def tiles_of(value):
    return [value[:, t * TILE : (t + 1) * TILE] for t in range(value.shape[1] // TILE)]


def radial_turn(value, steps):
    return join([pltpu.roll(tile, steps % TILE, axis=1) for tile in tiles_of(value)])


def column_turn(value, direction):
    tiles = tiles_of(value)
    count = len(tiles)
    lane = lax.broadcasted_iota(jnp.int32, tiles[0].shape, 1)
    near = [pltpu.roll(tile, (direction * RADIAL) % TILE, axis=1) for tile in tiles]
    far = lambda at: pltpu.roll(tiles[at], (TILE // 2 + direction * RADIAL) % TILE, axis=1)
    out = list(near)
    if direction < 0:
        high_end, low_end = lane >= TILE - RADIAL, (lane >= TILE // 2 - RADIAL) & (lane < TILE // 2)
        out[0] = jnp.where(high_end, near[1], near[0])
        out[1] = jnp.where(high_end, near[2], near[1])
        inner, outer, middle = 2, high_end, low_end
        edge = 0
    else:
        high_end, low_end = lane < RADIAL, (lane >= TILE // 2) & (lane < TILE // 2 + RADIAL)
        out[1] = jnp.where(high_end, near[0], near[1])
        out[2] = jnp.where(high_end, near[1], near[2])
        inner, outer, middle = 0, high_end, low_end
        edge = 2
    if count > 3:
        first_ring = far(3)
        out[inner] = jnp.where(outer, first_ring, out[inner])
        out[3] = jnp.where(middle, far(edge), near[3])
    if count > 4:
        out[3] = jnp.where(outer, far(4), out[3])
        out[4] = jnp.where(middle, first_ring, near[4])
    return join(out)


def lane_masks(rows, lanes):
    radial = lax.broadcasted_iota(jnp.int32, (rows, lanes), 1) % RADIAL
    keep_upper = (radial < RADIAL - 1).astype(jnp.float32)
    keep_lower = (radial > 0).astype(jnp.float32)
    return keep_upper, keep_lower


def chunks(lanes):
    return [(start, min(start + 2 * TILE, lanes)) for start in range(0, lanes, 2 * TILE)]


def point_factor(lanes):
    point = lax.broadcasted_iota(jnp.int32, (PTS, lanes), 0)
    radial = lax.broadcasted_iota(jnp.int32, (PTS, lanes), 1) % RADIAL
    shared = ((point == 0) & (radial > 0)) | ((point == PTS - 1) & (radial < RADIAL - 1))
    return jnp.where(shared, 0.5, 1.0)


def side_factor(i, k):
    return (0.5 if i in (0, PTS - 1) else 1.0) * (0.5 if k in (0, PTS - 1) else 1.0)


def plane_factor(factor, i):
    return jnp.concatenate([factor * side_factor(i, k) for k in range(PTS)])


def block(plane, k):
    start = plane * 64 + k * PTS
    return slice(start, start + PTS)


def load(ref, rows, tiles, base=0):
    return join([ref[base + t, rows, :] for t in range(tiles)])


def store(ref, rows, value, base=0):
    for t, tile in enumerate(tiles_of(value)):
        ref[base + t, rows, :] = tile


def assemble_sides(field, planes, tiles):
    batches = [planes[start : start + BATCH] for start in range(0, len(planes), BATCH)]
    for batch in batches:
        left = jnp.concatenate([load(field, block(plane, 0), tiles) for plane in batch])
        right = jnp.concatenate([load(field, block(plane, PTS - 1), tiles) for plane in batch])
        new_right = right + column_turn(left, -1)
        new_left = left + column_turn(right, 1)
        for at, plane in enumerate(batch):
            store(field, block(plane, PTS - 1), new_right[at * PTS : (at + 1) * PTS])
            store(field, block(plane, 0), new_left[at * PTS : (at + 1) * PTS])
    keep_upper, keep_lower = lane_masks(PTS * BATCH, tiles * TILE)
    for batch in batches:
        rows = len(batch) * PTS
        inner_at = [pl.ds(plane * 64, PTS, stride=PTS) for plane in batch]
        outer_at = [pl.ds(plane * 64 + PTS - 1, PTS, stride=PTS) for plane in batch]
        inner = jnp.concatenate([load(field, at, tiles) for at in inner_at])
        outer = jnp.concatenate([load(field, at, tiles) for at in outer_at])
        new_outer = outer + radial_turn(inner, -1) * keep_upper[:rows]
        new_inner = inner + radial_turn(outer, 1) * keep_lower[:rows]
        for at in range(len(batch)):
            store(field, outer_at[at], new_outer[at * PTS : (at + 1) * PTS])
            store(field, inner_at[at], new_inner[at * PTS : (at + 1) * PTS])


def fold(a, b, c, d):
    sum_k, diff_k = a + b, a - b
    sum_m, diff_m = c + d, c - d
    return sum_k + sum_m, sum_k - sum_m, diff_k + diff_m, diff_k - diff_m


def pack(parts, packed, rows, tiles):
    for c in range(4):
        for t in range(tiles):
            lanes = slice(t * TILE, (t + 1) * TILE)
            high, low = halves(parts[c * tiles + t, 0:rows, :])
            packed[c, 0:rows, lanes] = high
            packed[c, rows : 2 * rows, lanes] = low
            packed[c, 2 * rows : 3 * rows, lanes] = high


def unfold(ss, sa, as_, aa):
    sum_k, sum_m = ss + sa, ss - sa
    diff_k, diff_m = as_ + aa, as_ - aa
    return sum_k + diff_k, sum_k - diff_k, sum_m + diff_m, sum_m - diff_m


def mirrored(i, k):
    return (i, k), (PTS - 1 - i, k), (i, PTS - 1 - k), (PTS - 1 - i, PTS - 1 - k)


def coefficient_terms(values):
    rows = []
    for value in values:
        parts = []
        for _ in range(3):
            part = value.astype(jnp.bfloat16).astype(jnp.float32)
            parts.append(part)
            value = value - part
        high, middle, low = parts
        rows += [high, middle, low, high, middle, high]
    rows.append(jnp.zeros((TERMS - len(rows), value.shape[1]), jnp.float32))
    return jnp.concatenate(rows).astype(jnp.bfloat16)


def tables_kernel(geo, modes, own, lam, coef, kept, middle):
    kept[0:128] = own[0:128]
    kept[128:256] = own[384:512]
    middle[...] = own[128:384]
    la, lb, lz = (geo[n : n + 1] for n in range(3))
    cz = la * lb / (2.0 * lz)
    ca = lz * lb / (2.0 * la)
    cb = lz * la / (2.0 * lb)
    for at, value in enumerate((cz, ca, cb)):
        coef[at * PTS : (at + 1) * PTS] = jnp.broadcast_to(value, (PTS, LANES))
    terms = coefficient_terms((cz, ca, cb))
    for start, stop in chunks(LANES):
        for c in range(4):
            here = slice(c * MODES, (c + 1) * MODES)
            lam[here, start:stop] = 1.0 / dot(modes[here], terms[:, start:stop])


def window(case, left, own, right, rows):
    shift = (COLS_DEV - LEFT - case) * RADIAL
    joined = join([left[rows], own, right[rows]])
    joined = pltpu.roll(joined, joined.shape[1] - shift, axis=1)[:, :LANES]
    first, *center, last = tiles_of(joined)
    lane = lax.broadcasted_iota(jnp.int32, first.shape, 1)
    half = TILE // 2
    near = jnp.where(lane < half, pltpu.roll(first, half, axis=1), pltpu.roll(last, half, axis=1))
    return join([*center, near, jnp.where(lane < half, first, last)])


def outer_kernel(rot, left, own, right, geo, field, up, down):
    factor = point_factor(LANES)
    for case in range(4):

        @pl.when(rot[0] == case)
        def _(case=case):
            for at, i in enumerate((0, 1, 6, 7)):
                here = slice(at * 64, at * 64 + 64)
                value = window(case, left, own[here], right, here)
                field[here] = value * plane_factor(factor, i)

    up[0:128] = field[128:256]
    down[0:128] = field[0:128]
    length = jnp.broadcast_to(geo[2:3], (PTS, LANES))
    up[128:136] = length
    down[128:136] = length


def follow_kernel(left, right, own, inner):
    inner[...] = own[...]


def inner_kernel(rot, left, own, right, field):
    factor = point_factor(LANES)
    for case in range(4):

        @pl.when(rot[0] == case)
        def _(case=case):
            for at, i in enumerate((2, 3, 4, 5)):
                here = slice(at * 64, at * 64 + 64)
                field[here] = window(case, left, own[here], right, here) * plane_factor(factor, i)


def put(parts, tiles, at, values):
    for c in range(4):
        store(parts, at, values[c], c * tiles)


def layer(value, at):
    return value[at * PTS : (at + 1) * PTS]


def column_halos(field, planes, wide, lanes):
    before = jnp.concatenate([load(field, block(plane, PTS - 2), wide) for plane in planes])
    after = jnp.concatenate([load(field, block(plane, 1), wide) for plane in planes])
    return column_turn(before, 1)[:, :lanes], column_turn(after, -1)[:, :lanes]


def radial_halos(parts, tiles, count):
    masks = lane_masks(4 * count, tiles * TILE)
    found = []
    for first, steps, keep in ((PTS - 2, 1, masks[1]), (1, -1, masks[0])):
        rows = pl.ds(first, count, stride=PTS)
        values = [load(parts, rows, tiles, c * tiles) for c in range(4)]
        values = radial_turn(jnp.concatenate(values), steps) * keep
        found.append([values[c * count : (c + 1) * count] for c in range(4)])
    return found


def solve_inner_kernel(start_up, wide, tiles, *refs):
    if start_up:
        outer, inner, *refs = refs
        planes = [outer[64:128]] + [inner[i * 64 : i * 64 + 64] for i in range(4)] + [outer[128:192]]
    else:
        field, *refs = refs
        planes = [field[i * 64 : i * 64 + 64] for i in range(1, 7)]
    fwd, share, spectrum, ext, parts, packed = refs
    lanes = tiles * TILE
    factor = point_factor(lanes)
    for at, plane in enumerate(planes):
        store(ext, slice(at * 64, at * 64 + 64), plane)
    assemble_sides(ext, range(6), wide)
    for at in range(6):
        here = slice(at * 64, at * 64 + 64)
        share[here] = load(ext, here, tiles) * plane_factor(factor, at + 1)
    for i in range(3):
        for k in range(4):
            corners = ((i, k), (5 - i, k), (i, 7 - k), (5 - i, 7 - k))
            values = fold(*(load(ext, block(p, q), tiles) for p, q in corners))
            put(parts, tiles, block(0, i * 4 + k), values)
    before, after = column_halos(ext, range(6), wide, lanes)
    for i in range(3):
        values = fold(layer(before, i), layer(before, 5 - i), layer(after, i), layer(after, 5 - i))
        put(parts, tiles, slice(96 + i * 8, 104 + i * 8), values)
    put(parts, tiles, slice(120, 128), [jnp.zeros((PTS, lanes), jnp.float32)] * 4)
    lower, upper = radial_halos(parts, tiles, 16)
    put(parts, tiles, slice(128, 144), lower)
    put(parts, tiles, slice(144, 160), upper)
    pack(parts, packed, INNER, tiles)
    for c in range(4):
        for start, stop in chunks(lanes):
            spectrum[c * MODES : (c + 1) * MODES, start:stop] = dot(fwd[c], packed[c, :, start:stop])


def solve_outer_kernel(start_up, wide, tiles, *refs):
    field, below, above, spectrum, lam, fwd, bwd, bwd_low = refs[:8]
    share, modes, up, down, ext, parts, packed = refs[8:]
    lanes = tiles * TILE
    factor = point_factor(lanes)
    last = 192 if start_up else 448
    store(ext, slice(0, 64), below[0:64])
    store(ext, slice(64, 128), field[0:64] + below[64:128])
    store(ext, slice(128, 192), field[last : last + 64] + above[0:64])
    store(ext, slice(192, 256), above[64:128])
    assemble_sides(ext, range(4), wide)
    share[0:64] = load(ext, slice(64, 128), tiles) * plane_factor(factor, 0)
    share[64:128] = load(ext, slice(128, 192), tiles) * plane_factor(factor, 7)
    for k in range(4):
        for at, (p, q) in enumerate(((1, 2), (0, 3))):
            corners = ((p, k), (q, k), (p, 7 - k), (q, 7 - k))
            values = fold(*(load(ext, block(*corner), tiles) for corner in corners))
            put(parts, tiles, block(0, at * 4 + k), values)
    before, after = column_halos(ext, (1, 2), wide, lanes)
    values = fold(layer(before, 0), layer(before, 1), layer(after, 0), layer(after, 1))
    put(parts, tiles, slice(64, 72), values)
    lower, upper = radial_halos(parts, tiles, 4)
    put(parts, tiles, slice(72, 80), [jnp.concatenate(pair) for pair in zip(lower, upper)])
    pack(parts, packed, OUTER, tiles)
    for c in range(4):
        for start, stop in chunks(lanes):
            here = slice(c * MODES, (c + 1) * MODES)
            value = dot(fwd[c], packed[c, :, start:stop]) + spectrum[here, start:stop]
            modes[c, 0:MODES, start:stop], modes[c, MODES:, start:stop] = halves(value * lam[here, start:stop])
    back(modes, bwd, bwd_low, parts, tiles, 32)
    for k in range(4):
        classes = (load(parts, block(0, k), tiles, c * tiles) for c in range(4))
        values = unfold(*classes)
        for (p, q), value in zip(mirrored(0, k), values):
            (down if p == 0 else up)[block(0, q)] = value * factor


def back(modes, bwd, bwd_low, parts, tiles, rows):
    for c in range(4):
        for start, stop in chunks(tiles * TILE):
            value = dot(bwd[c], modes[c, :, start:stop])
            value = value + dot(bwd_low[c], modes[c, 0:MODES, start:stop])
            store(parts, slice(0, rows), value, c * tiles + start // TILE)


def stepped(kind, value, before):
    if kind in (0, 2):
        return value * (1.0 / theta)
    return before * (rho_second * rho_first) + value * (2.0 * rho_second / delta)


def step_inner_kernel(kind, wide, tiles, *refs):
    take = iter(refs)
    modes = next(take)
    before = next(take) if kind in (1, 3) else None
    total = next(take) if kind != 0 else None
    coef, app, bwd, bwd_low = (next(take) for _ in range(4))
    step = next(take) if kind in (0, 2) else None
    sum_out = next(take) if kind != 0 else None
    image, ext, parts, packed = take
    lanes = tiles * TILE
    factor = point_factor(wide * TILE)
    back(modes, bwd, bwd_low, parts, wide, 96)
    for i in range(3):
        for k in range(4):
            classes = (load(parts, block(0, i * 4 + k), wide, c * wide) for c in range(4))
            corners = ((i, k), (5 - i, k), (i, 7 - k), (5 - i, 7 - k))
            for corner, value in zip(corners, unfold(*classes)):
                store(ext, block(*corner), value * factor)
    assemble_sides(ext, range(6), wide)
    for i in range(6):
        here = slice(i * 64, i * 64 + 64)
        value = stepped(kind, load(ext, here, tiles), None if before is None else before[here, :lanes])
        if step is not None:
            step[here] = value
        if sum_out is not None:
            sum_out[here] = total[here, :lanes] + value
        store(ext, here, value)
    for i in range(3):
        for k in range(4):
            corners = ((i, k), (5 - i, k), (i, 7 - k), (5 - i, 7 - k))
            values = fold(*(load(ext, block(p, q), tiles) for p, q in corners))
            put(parts, tiles, block(0, i * 4 + k), values)
    pack(parts, packed, 96, tiles)
    for c in range(4):
        for start, stop in chunks(lanes):
            terms = dot(app[c], packed[c, :, start:stop]).reshape(40, PTS, stop - start)
            value = terms[0:16] * coef[0:8, start:stop]
            sides = terms[16:28] * coef[8:16, start:stop] + terms[28:40] * coef[16:24, start:stop]
            value = jnp.concatenate([value[0:4], value[4:16] + sides])
            image[c * 128 : (c + 1) * 128, start:stop] = value.reshape(128, stop - start)


def step_outer_kernel(kind, wide, tiles, *refs):
    take = iter(refs)
    last, below, first, above = (next(take) for _ in range(4))
    before = next(take) if kind in (1, 3) else None
    total = next(take) if kind != 0 else None
    share_inner, share_outer, image, coef, app = (next(take) for _ in range(5))
    res, res_low = (next(take), next(take)) if kind == 1 else (None, None)
    step = next(take) if kind in (0, 2) else None
    sum_out = next(take) if kind != 0 else None
    field, up, down = next(take), next(take), next(take)
    coarse = next(take) if kind == 1 else None
    ext, parts, packed = next(take), next(take), next(take)
    split_field = next(take) if kind == 1 else None
    lanes = tiles * TILE
    store(ext, slice(0, 64), first[...] + below[...])
    store(ext, slice(64, 128), last[...] + above[...])
    assemble_sides(ext, range(2), wide)
    for at in range(2):
        here = slice(at * 64, at * 64 + 64)
        value = stepped(kind, load(ext, here, tiles), None if before is None else before[here, :lanes])
        if step is not None:
            step[here] = value
        if sum_out is not None:
            sum_out[here] = total[here, :lanes] + value
        store(ext, here, value)
    for k in range(4):
        corners = ((0, k), (1, k), (0, 7 - k), (1, 7 - k))
        values = fold(*(load(ext, block(p, q), tiles) for p, q in corners))
        put(parts, tiles, block(0, k), values)
    pack(parts, packed, 32, tiles)
    for c in range(4):
        for start, stop in chunks(lanes):
            terms = dot(app[c], packed[c, :, start:stop]).reshape(24, PTS, stop - start)
            value = terms[0:16] * coef[0:8, start:stop]
            sides = terms[16:20] * coef[8:16, start:stop] + terms[20:24] * coef[16:24, start:stop]
            value = jnp.concatenate([value[0:4] + sides, value[4:16]]).reshape(128, stop - start)
            value = value + image[c * 128 : (c + 1) * 128, start:stop]
            store(parts, slice(0, 128), value, c * tiles + start // TILE)
    for i in range(4):
        for k in range(4):
            classes = (load(parts, block(0, i * 4 + k), tiles, c * tiles) for c in range(4))
            for (p, q), value in zip(mirrored(i, k), unfold(*classes)):
                if p in (0, 7):
                    shared = share_outer[block(p // 7, q), :lanes]
                else:
                    shared = share_inner[block(p - 1, q), :lanes]
                field[block(p, q)] = shared - value
    if kind == 1:
        split_field[0:512], split_field[512:1024] = halves(field[...])
        for start, stop in chunks(lanes):
            value = dot(res[...], split_field[:, start:stop])
            coarse[:, start:stop] = value + dot(res_low[...], split_field[0:512, start:stop])
        up[...] = coarse[48:64]
        down[...] = coarse[0:16]
    elif kind == 3:
        up[...] = field[448:512]
        down[...] = field[0:64]
    else:
        up[...] = field[384:512]
        down[...] = field[0:128]


def assemble_coarse(value):
    lanes = value.shape[1]
    row = lax.broadcasted_iota(jnp.int32, (64, lanes), 0)
    keep_upper, keep_lower = lane_masks(64, lanes)
    first = (row % 16) < 4
    last = (row % 16) >= 12
    over = pltpu.roll(column_turn(value, -1), 12, axis=0)
    under = pltpu.roll(column_turn(value, 1), 64 - 12, axis=0)
    value = value + jnp.where(last, over, 0.0) + jnp.where(first, under, 0.0)
    first = (row % 4) == 0
    last = (row % 4) == 3
    over = pltpu.roll(radial_turn(value, -1) * keep_upper, 3, axis=0)
    under = pltpu.roll(radial_turn(value, 1) * keep_lower, 64 - 3, axis=0)
    return value + jnp.where(last, over, 0.0) + jnp.where(first, under, 0.0)


def diagonal_kernel(lower, upper, geo, table, scale):
    lanes = scale.shape[1]
    la, lb = geo[0:1, :lanes], geo[1:2, :lanes]

    def local(lz, rows):
        return (
            la * lb / (2.0 * lz) * table[rows, 0:1]
            + lz * lb / (2.0 * la) * table[rows, 1:2]
            + lz * la / (2.0 * lb) * table[rows, 2:3]
        )

    value = local(geo[2:3, :lanes], slice(0, 64))
    first = value[0:16] + local(lower[128:129, :lanes], slice(48, 64))
    last = value[48:64] + local(upper[128:129, :lanes], slice(0, 16))
    scale[...] = assemble_coarse(jnp.concatenate([first, value[16:48], last]))


def coarse_outer_kernel(local, below, above, scale, coef, prolong, field, out, pack, up, down):
    lanes = local.shape[1]
    value = local[...]
    value = jnp.concatenate([value[0:16] + below[...], value[16:48], value[48:64] + above[...]])
    value = assemble_coarse(value) / scale[...]
    high, low = halves(value)
    pack[0, 0:64] = high
    pack[0, 64:128] = low
    pack[0, 128:192] = high
    for at, i in enumerate((0, 1, 6, 7)):
        correct(i, slice(at * 64, at * 64 + 64), coef, prolong, pack, field, out)
    up[...] = out[128:256]
    down[...] = out[0:128]


def coarse_inner_kernel(pack, coef, prolong, total_inner, total_outer, field, sum_inner, sum_outer, out):
    for at, i in enumerate((2, 3, 4, 5)):
        correct(i, slice(at * 64, at * 64 + 64), coef, prolong, pack, field, out)
    for start, stop in chunks(pack.shape[2]):
        for i in range(PTS):
            value = dot(prolong[i * 64 : i * 64 + 64], pack[0, :, start:stop])
            if i in (0, 7):
                at = slice(i // 7 * 64, i // 7 * 64 + 64)
                sum_outer[at, start:stop] = total_outer[at, start:stop] + value
            else:
                at = slice(i * 64 - 64, i * 64)
                sum_inner[at, start:stop] = total_inner[at, start:stop] + value


def correct(i, to, coef, prolong, pack, field, out):
    here = slice(i * 64, i * 64 + 64)
    for start, stop in chunks(pack.shape[2]):
        sides = (8, PTS, stop - start)
        value = 0.0
        for n in range(3):
            rows = slice((n + 1) * 512 + i * 64, (n + 1) * 512 + i * 64 + 64)
            term = dot(prolong[rows], pack[0, :, start:stop]).reshape(sides)
            value = value + term * coef[n * PTS : (n + 1) * PTS, start:stop]
        out[to, start:stop] = field[here, start:stop] - value.reshape(64, stop - start)


def finish_inner_kernel(rot, local, total_inner, total_outer, sol, res, ext):
    tiles = local.shape[1] // TILE
    for i in range(6):
        store(ext, slice(i * 64, i * 64 + 64), local[i * 64 + 64 : i * 64 + 128])
    assemble_sides(ext, range(6), tiles)
    for case in range(4):

        @pl.when(rot[0] == case)
        def _(case=case):
            start = (LEFT + case - RINGS[0][0]) * RADIAL
            for plane in range(PTS):
                here = slice(plane * 64, plane * 64 + 64)
                if plane in (0, 7):
                    at = plane // 7 * 64
                    sol[here] = total_outer[at : at + 64, start : start + OWN]
                else:
                    before = slice(plane * 64 - 64, plane * 64)
                    sol[here] = total_inner[before, start : start + OWN]
                    res[before] = load(ext, before, tiles)[:, start : start + OWN]


def finish_outer_kernel(rot, local, below, above, inner, res, ext):
    tiles = local.shape[1] // TILE
    store(ext, slice(0, 64), local[0:64] + below[...])
    store(ext, slice(64, 128), local[448:512] + above[...])
    assemble_sides(ext, range(2), tiles)
    res[64:448] = inner[...]
    for case in range(4):

        @pl.when(rot[0] == case)
        def _(case=case):
            start = (LEFT + case - RINGS[0][0]) * RADIAL
            res[0:64] = load(ext, slice(0, 64), tiles)[:, start : start + OWN]
            res[448:512] = load(ext, slice(64, 128), tiles)[:, start : start + OWN]


def call(kernel, name, args, outs, scratch=(), scalars=0, flops=0, untouched=0):
    spaces = [pltpu.SMEM] * scalars + [pl.ANY] * untouched
    spaces += [pltpu.VMEM] * (len(args) - len(spaces))
    in_specs = [pl.BlockSpec(memory_space=space) for space in spaces]
    return pl.pallas_call(
        kernel,
        out_shape=[
            jax.ShapeDtypeStruct(out, jnp.float32 if len(out) == 2 else jnp.bfloat16) for out in outs
        ],
        in_specs=in_specs,
        out_specs=[pl.BlockSpec(memory_space=pltpu.VMEM) for _ in outs],
        scratch_shapes=list(scratch),
        name=name,
        cost_estimate=pl.CostEstimate(flops=flops, bytes_accessed=4_000_000, transcendentals=0),
        compiler_params=pltpu.CompilerParams(vmem_limit_bytes=40 * 1024 * 1024),
    )(*args)


def per_device(rhs, spacing_z, spacing_a, spacing_b, rotation):
    mats = matrices()
    group = lax.axis_index("grp")
    member = lax.axis_index("sub")
    groups = lax.axis_size("grp")
    members = lax.axis_size("sub")
    wide, narrow = jnp.float32, jnp.bfloat16
    vmem = pltpu.VMEM

    def shifted(value, axis, count, steps):
        return lax.ppermute(value, axis, [(n, (n + steps) % count) for n in range(count)])

    def neighbours(up, down):
        return shifted(up, "grp", groups, 1), shifted(down, "grp", groups, -1)

    def beside(value):
        return shifted(value, "sub", members, 1), shifted(value, "sub", members, -1)

    def shapes(tiles, *rows):
        return tuple((count, tiles * TILE) for count in rows)

    own = rhs.reshape(512, OWN)
    left, right = beside(jnp.concatenate([own[0:128], own[384:512]]))
    rot = lax.dynamic_slice(rotation, (group,), (1,))
    ring = jnp.concatenate([spacing_a, spacing_a, spacing_a])
    columns = lax.dynamic_slice(ring, (spacing_a.shape[0] + member * COLS_DEV - LEFT,), (WIN,))
    columns = jnp.concatenate([columns[start:stop] for start, stop in RINGS])
    geo = jnp.stack(
        [
            jnp.repeat(columns, RADIAL),
            jnp.tile(spacing_b, WIN),
            jnp.broadcast_to(spacing_z, (LANES,)),
        ]
    )
    geo = jnp.concatenate([geo, jnp.ones((5, LANES), wide)])
    lam, coef, own, middle = call(
        tables_kernel,
        "tables",
        (geo, mats["modes"], own),
        ((4 * MODES, LANES), (24, LANES), (256, OWN), (256, OWN)),
    )
    (middle,) = call(follow_kernel, "follow", (left, right, middle), ((256, OWN),), untouched=2)
    near, far = beside(middle)
    outer, up, down = call(
        outer_kernel,
        "outer",
        (rot, left, own, right, geo),
        ((256, LANES), (136, LANES), (136, LANES)),
        scalars=1,
    )
    lower, upper = neighbours(up, down)
    (inner,) = call(
        inner_kernel, "inner", (rot, near, middle, far), ((256, LANES),), scalars=1, flops=EARLY
    )

    def solve(fields, below, above, before, tiles):
        lanes = tiles * TILE
        start_up = len(fields) == 2
        share_inner, spectrum = call(
            functools.partial(solve_inner_kernel, start_up, before, tiles),
            "solve_inner",
            (*fields, mats["forward_inner"]),
            shapes(tiles, 384, 4 * MODES),
            (
                vmem((before, 384, TILE), wide),
                vmem((4 * tiles, INNER, TILE), wide),
                vmem((4, 3 * INNER, lanes), narrow),
            ),
        )
        share_outer, modes, up, down = call(
            functools.partial(solve_outer_kernel, start_up, before, tiles),
            "solve_outer",
            (fields[0], below, above, spectrum, lam, mats["forward_outer"], *mats["backward_outer"]),
            (*shapes(tiles, 128), (4, 2 * MODES, lanes), *shapes(tiles, 64, 64)),
            (
                vmem((before, 256, TILE), wide),
                vmem((4 * tiles, 128, TILE), wide),
                vmem((4, 3 * OUTER, lanes), narrow),
            ),
        )
        return (share_inner, share_outer), (modes, up, down), neighbours(up, down)

    def advance(kind, local, messages, share, before, total, width, tiles):
        lanes = tiles * TILE

        def scratch(rows, folded):
            return [
                vmem((width, rows, TILE), wide),
                vmem((4 * width, 128, TILE), wide),
                vmem((4, folded, lanes), narrow),
            ]

        def pick(at):
            return [pair[at] for pair in (before, total) if pair is not None]

        kept = [count for count, used in ((1, kind in (0, 2)), (1, kind != 0)) if used]
        *inner, image = call(
            functools.partial(step_inner_kernel, kind, width, tiles),
            f"step{kind}_inner",
            (local[0], *pick(0), coef, mats["apply_inner"], *mats["backward_inner"]),
            shapes(tiles, *(384 for _ in kept), 512),
            scratch(384, 288),
        )
        sent = {0: 128, 1: 16, 2: 128, 3: 64}[kind]
        extra = scratch(128, 96)
        if kind == 1:
            extra.append(vmem((1024, lanes), narrow))
        out = call(
            functools.partial(step_outer_kernel, kind, width, tiles),
            f"step{kind}_outer",
            (
                *(local[1], messages[0], local[2], messages[1]),
                *(*pick(1), *share, image, coef, mats["apply_outer"]),
                *(mats["restrict"] if kind == 1 else ()),
            ),
            shapes(tiles, *(128 for _ in kept), 512, sent, sent, *((64,) if kind == 1 else ())),
            extra,
        )
        outer, (field, up, down, *coarse) = out[: len(kept)], out[len(kept) :]
        return list(zip(inner, outer)), field, neighbours(up, down), *coarse

    share, local, messages = solve((outer, inner), lower, upper, 5, 5)
    (step,), field, messages = advance(0, local, messages, share, None, None, 5, 5)
    share, local, messages = solve((field,), *messages, 5, 5)
    (total,), field, messages, coarse = advance(1, local, messages, share, step, step, 5, 4)
    (scale,) = call(diagonal_kernel, "diagonal", (lower, upper, geo, mats["coarse"]), shapes(4, 64))
    outer, terms, up, down = call(
        coarse_outer_kernel,
        "coarse_outer",
        (coarse, *messages, scale, coef, mats["prolong"], field),
        (*shapes(4, 256), (1, 192, 4 * TILE), *shapes(4, 128, 128)),
    )
    messages = neighbours(up, down)
    *total, inner = call(
        coarse_inner_kernel,
        "coarse_inner",
        (terms, coef, mats["prolong"], *total, field),
        shapes(4, 384, 128, 256),
    )
    share, local, messages = solve((outer, inner), *messages, 4, 4)
    (step, total), field, messages = advance(2, local, messages, share, None, total, 4, 4)
    share, local, messages = solve((field,), *messages, 4, 3)
    (total,), field, messages = advance(3, local, messages, share, step, total, 3, 3)
    sol, inner = call(
        finish_inner_kernel,
        "finish_inner",
        (rot, field, *total),
        ((512, OWN), (384, OWN)),
        (vmem((3, 384, TILE), wide),),
        scalars=1,
    )
    (res,) = call(
        finish_outer_kernel,
        "finish_outer",
        (rot, field, *messages, inner),
        ((512, OWN),),
        (vmem((3, 128, TILE), wide),),
        scalars=1,
    )
    return sol.reshape(rhs.shape), res.reshape(rhs.shape)


def solution(mesh):
    return jax.shard_map(
        per_device,
        mesh=mesh,
        in_specs=(P(None, None, None, ("grp", "sub")), P("grp"), P(), P(), P()),
        out_specs=(P(None, None, None, ("grp", "sub")), P(None, None, None, ("grp", "sub"))),
        check_vma=False,
    )
```

```python
import functools

import jax
import jax.numpy as jnp
import ml_dtypes
import numpy as np
from jax import lax
from jax.experimental import pallas as pl
from jax.experimental.pallas import tpu as pltpu
from jax.sharding import PartitionSpec as P

PTS = 8
CPTS = 4
COLS_DEV = 16
RADIAL = 16
SMOOTH = 2

WIN = 40
LEFT = 10
LANES = WIN * RADIAL
RINGS = ((8, 32), (4, 8), (32, 36), (0, 4), (36, 40))
OWN = COLS_DEV * RADIAL
CLASSES = ((0, 0), (0, 1), (1, 0), (1, 1))
INNER = 160
OUTER = 80
MODES = 256
TILE = 128
TILES = LANES // TILE
TERMS = 32
BATCH = 4
EARLY = 20_000_000_000

cheb_upper = 2.0
cheb_ratio = 0.1
theta = 0.5 * (cheb_upper + cheb_upper * cheb_ratio)
delta = 0.5 * (cheb_upper - cheb_upper * cheb_ratio)
sigma = theta / delta
rho_first = 1.0 / sigma
rho_second = 1.0 / (2.0 * sigma - rho_first)


def legendre_rows(gll_nodes, poly_order):
    values = np.zeros((gll_nodes.size, poly_order + 1))
    values[:, 0] = 1.0
    values[:, 1] = gll_nodes
    for degree in range(2, poly_order + 1):
        values[:, degree] = (
            (2 * degree - 1) * gll_nodes * values[:, degree - 1]
            - (degree - 1) * values[:, degree - 2]
        ) / degree
    return values


def jacobi_eigen(matrix):
    order = matrix.shape[0]
    current = matrix.copy()
    vectors = np.eye(order)
    for sweep in range(12):
        for first in range(order - 1):
            for second in range(first + 1, order):
                off_value = current[first, second]
                spread = current[second, second] - current[first, first]
                sense = np.where(spread >= 0.0, 1.0, -1.0)
                denom = spread + sense * np.sqrt(spread * spread + 4.0 * off_value * off_value)
                denom = np.where(denom == 0.0, 1.0, denom)
                tangent = 2.0 * off_value / denom
                cosine = 1.0 / np.sqrt(1.0 + tangent * tangent)
                sine = tangent * cosine
                rotate = np.eye(order)
                rotate[first, first] = cosine
                rotate[second, second] = cosine
                rotate[first, second] = sine
                rotate[second, first] = -sine
                current = rotate.T @ current @ rotate
                vectors = vectors @ rotate
    diag_ids = np.arange(order)
    return (current[diag_ids, diag_ids].copy(), vectors)


def lobatto(poly_order):
    gll_nodes = np.cos(np.pi * np.arange(poly_order + 1) / poly_order)
    for newton in range(100):
        values = legendre_rows(gll_nodes, poly_order)
        gll_nodes = gll_nodes - (gll_nodes * values[:, poly_order] - values[:, poly_order - 1]) / (
            (poly_order + 1) * values[:, poly_order]
        )
    values = legendre_rows(gll_nodes, poly_order)
    gll_nodes = gll_nodes[::-1].copy()
    top_poly = values[::-1, poly_order].copy()
    weights = 2.0 / (poly_order * (poly_order + 1) * top_poly**2)
    derivative = np.zeros((poly_order + 1, poly_order + 1))
    for row_index in range(poly_order + 1):
        for col_index in range(poly_order + 1):
            if row_index != col_index:
                derivative[row_index, col_index] = top_poly[row_index] / (
                    top_poly[col_index] * (gll_nodes[row_index] - gll_nodes[col_index])
                )
    derivative[0, 0] = -poly_order * (poly_order + 1) / 4.0
    derivative[poly_order, poly_order] = poly_order * (poly_order + 1) / 4.0
    stiffness = derivative.T @ (weights[:, None] * derivative)
    return (gll_nodes, weights, stiffness)


def element_tables():
    fine_nodes, fine_weights, fine_stiff = lobatto(PTS - 1)
    coarse_nodes, coarse_weights, coarse_stiff = lobatto(CPTS - 1)
    interp = np.ones((PTS, CPTS))
    for target_col in range(CPTS):
        for other_col in range(CPTS):
            if other_col != target_col:
                interp[:, target_col] *= (fine_nodes - coarse_nodes[other_col]) / (
                    coarse_nodes[target_col] - coarse_nodes[other_col]
                )
    poly_order = PTS - 1
    node_count = 3 * poly_order + 1
    joined_stiff = np.zeros((node_count, node_count))
    joined_mass = np.zeros(node_count)
    for piece_index in range(3):
        first_node = piece_index * poly_order
        joined_stiff[first_node : first_node + PTS, first_node : first_node + PTS] += fine_stiff
        joined_mass[first_node : first_node + PTS] += fine_weights
    kept = slice(poly_order - 1, 2 * poly_order + 2)
    root_mass = np.sqrt(joined_mass[kept])
    eigen_values, eigen_vectors = jacobi_eigen(
        joined_stiff[kept, kept] / root_mass[:, None] / root_mass[None, :]
    )
    eigen_basis = eigen_vectors / root_mass[:, None]
    coarse_diag = np.diag(coarse_stiff).copy()
    return fine_stiff, fine_weights, eigen_basis, eigen_values, interp, coarse_diag, coarse_weights


def split(table):
    high = table.astype(np.float32).astype(ml_dtypes.bfloat16)
    low = (table - high.astype(np.float64)).astype(np.float32).astype(ml_dtypes.bfloat16)
    return high, low


def kron3(first, second, third):
    return np.kron(first, np.kron(second, third))


def spread(values):
    terms = np.zeros((values.shape[0], TERMS), ml_dtypes.bfloat16)
    for at in range(3):
        high, rest = split(values[:, at])
        middle, low = split(values[:, at] - high.astype(np.float64))
        for n, part in enumerate((high, high, high, middle, middle, low)):
            terms[:, at * 6 + n] = part
    return terms


def matrices():
    stiff, weights, basis, values, interp, coarse_diag, coarse_weights = element_tables()
    parts = ([], [])
    for mode in range(PTS + 2):
        column = basis[:, mode]
        odd = np.abs(column + column[::-1]).sum() < np.abs(column - column[::-1]).sum()
        parts[int(odd)].append(mode)
    signs = (1.0, -1.0)
    pure = basis.copy()
    for parity in (0, 1):
        for mode in parts[parity]:
            pure[:, mode] = 0.5 * (basis[:, mode] + signs[parity] * basis[::-1, mode])
    center = pure[1:-1, :]
    edges = pure[[0, -1], :]

    def folded(matrix, parity):
        half = PTS // 2
        return 0.5 * (matrix[:half, :half] + signs[parity] * matrix[:half, ::-1][:, :half])

    mass = np.diag(weights)
    halved = np.ones(PTS // 2)
    halved[0] = 0.5
    forward_inner = np.zeros((4, MODES, INNER))
    forward_outer = np.zeros((4, MODES, OUTER))
    backward = np.zeros((4, PTS * 16, MODES))
    apply_inner = np.zeros((4, 320, 96))
    apply_outer = np.zeros((4, 192, 32))
    mode_values = np.ones((4, MODES, 3))
    for at, (pi, pk) in enumerate(CLASSES):
        ci, ck = center[:4, parts[pi]], center[:4, parts[pk]]
        ei, ek = edges[:1, parts[pi]], edges[:1, parts[pk]]
        count = len(parts[pi]) * len(parts[pk]) * (PTS + 2)
        rest = ci[1:]
        gap = lambda rows: np.zeros((rows, count))
        columns = [kron3(rest, ck, center), kron3(rest, ek, center), gap(8)]
        columns += [kron3(rest, ck, edges[:1]), gap(4), kron3(rest, ck, edges[1:]), gap(4)]
        forward_inner[at, :count] = np.concatenate(columns, axis=0).T
        columns = [kron3(ci[:1], ck, center), kron3(ei, ck, center), kron3(ci[:1], ek, center)]
        columns += [kron3(ci[:1], ck, edges[:1]), kron3(ci[:1], ck, edges[1:])]
        forward_outer[at, :count] = np.concatenate(columns, axis=0).T
        backward[at, :, :count] = kron3(halved[:, None] * ci, halved[:, None] * ck, center)
        vi, vk = values[parts[pi]], values[parts[pk]]
        ones = np.ones
        mode_values[at, :count, 0] = kron3(vi, ones(len(vk)), ones(PTS + 2))
        mode_values[at, :count, 1] = kron3(ones(len(vi)), vk, ones(PTS + 2))
        mode_values[at, :count, 2] = kron3(ones(len(vi)), ones(len(vk)), values)
        si, sk = folded(stiff, pi), folded(stiff, pk)
        mi, mk = folded(mass, pi), folded(mass, pk)
        along_z, along_a, along_b = kron3(si, mk, mass), kron3(mi, sk, mass), kron3(mi, mk, stiff)
        apply_inner[at] = np.concatenate([along_z[:, 32:], along_a[32:, 32:], along_b[32:, 32:]])
        apply_outer[at] = np.concatenate([along_z[:, :32], along_a[:32, :32], along_b[:32, :32]])
    mass_up, stiff_up = mass @ interp, stiff @ interp
    prolong = np.concatenate(
        [
            kron3(interp, interp, interp),
            kron3(stiff_up, mass_up, mass_up),
            kron3(mass_up, stiff_up, mass_up),
            kron3(mass_up, mass_up, stiff_up),
        ],
        axis=0,
    )
    restrict = kron3(interp.T, interp.T, interp.T)
    coarse = np.zeros((CPTS**3, 8))
    coarse[:, 0] = kron3(coarse_diag, coarse_weights, coarse_weights)
    coarse[:, 1] = kron3(coarse_weights, coarse_diag, coarse_weights)
    coarse[:, 2] = kron3(coarse_weights, coarse_weights, coarse_diag)

    def pair(table):
        high, low = split(table)
        return jnp.asarray(np.concatenate([high, high], axis=-1)), jnp.asarray(low)

    def triple(table):
        high, low = split(table)
        return jnp.asarray(np.concatenate([high, high, low], axis=-1))

    return {
        "forward_inner": triple(forward_inner),
        "forward_outer": triple(forward_outer),
        "backward_outer": pair(backward[:, :32]),
        "backward_inner": pair(backward[:, 32:]),
        "apply_inner": triple(apply_inner),
        "apply_outer": triple(apply_outer),
        "restrict": pair(restrict),
        "prolong": triple(prolong),
        "modes": jnp.asarray(spread(mode_values.reshape(4 * MODES, 3))),
        "coarse": jnp.asarray(coarse.astype(np.float32)),
    }


def halves(value):
    high = value.astype(jnp.bfloat16)
    low = (value - high.astype(jnp.float32)).astype(jnp.bfloat16)
    return high, low


def dot(left, right):
    return jnp.dot(left, right, preferred_element_type=jnp.float32)


def join(tiles):
    return jnp.concatenate(tiles, axis=1)


def tiles_of(value):
    return [value[:, t * TILE : (t + 1) * TILE] for t in range(value.shape[1] // TILE)]


def radial_turn(value, steps):
    return join([pltpu.roll(tile, steps % TILE, axis=1) for tile in tiles_of(value)])


def column_turn(value, direction):
    tiles = tiles_of(value)
    count = len(tiles)
    lane = lax.broadcasted_iota(jnp.int32, tiles[0].shape, 1)
    near = [pltpu.roll(tile, (direction * RADIAL) % TILE, axis=1) for tile in tiles]
    far = lambda at: pltpu.roll(tiles[at], (TILE // 2 + direction * RADIAL) % TILE, axis=1)
    out = list(near)
    if direction < 0:
        high_end, low_end = lane >= TILE - RADIAL, (lane >= TILE // 2 - RADIAL) & (lane < TILE // 2)
        out[0] = jnp.where(high_end, near[1], near[0])
        out[1] = jnp.where(high_end, near[2], near[1])
        inner, outer, middle = 2, high_end, low_end
        edge = 0
    else:
        high_end, low_end = lane < RADIAL, (lane >= TILE // 2) & (lane < TILE // 2 + RADIAL)
        out[1] = jnp.where(high_end, near[0], near[1])
        out[2] = jnp.where(high_end, near[1], near[2])
        inner, outer, middle = 0, high_end, low_end
        edge = 2
    if count > 3:
        first_ring = far(3)
        out[inner] = jnp.where(outer, first_ring, out[inner])
        out[3] = jnp.where(middle, far(edge), near[3])
    if count > 4:
        out[3] = jnp.where(outer, far(4), out[3])
        out[4] = jnp.where(middle, first_ring, near[4])
    return join(out)


def lane_masks(rows, lanes):
    radial = lax.broadcasted_iota(jnp.int32, (rows, lanes), 1) % RADIAL
    keep_upper = (radial < RADIAL - 1).astype(jnp.float32)
    keep_lower = (radial > 0).astype(jnp.float32)
    return keep_upper, keep_lower


def chunks(lanes):
    return [(start, min(start + 2 * TILE, lanes)) for start in range(0, lanes, 2 * TILE)]


def point_factor(lanes):
    point = lax.broadcasted_iota(jnp.int32, (PTS, lanes), 0)
    radial = lax.broadcasted_iota(jnp.int32, (PTS, lanes), 1) % RADIAL
    shared = ((point == 0) & (radial > 0)) | ((point == PTS - 1) & (radial < RADIAL - 1))
    return jnp.where(shared, 0.5, 1.0)


def side_factor(i, k):
    return (0.5 if i in (0, PTS - 1) else 1.0) * (0.5 if k in (0, PTS - 1) else 1.0)


def plane_factor(factor, i):
    return jnp.concatenate([factor * side_factor(i, k) for k in range(PTS)])


def block(plane, k):
    start = plane * 64 + k * PTS
    return slice(start, start + PTS)


def load(ref, rows, tiles, base=0):
    return join([ref[base + t, rows, :] for t in range(tiles)])


def store(ref, rows, value, base=0):
    for t, tile in enumerate(tiles_of(value)):
        ref[base + t, rows, :] = tile


def assemble_sides(field, planes, tiles):
    batches = [planes[start : start + BATCH] for start in range(0, len(planes), BATCH)]
    for batch in batches:
        left = jnp.concatenate([load(field, block(plane, 0), tiles) for plane in batch])
        right = jnp.concatenate([load(field, block(plane, PTS - 1), tiles) for plane in batch])
        new_right = right + column_turn(left, -1)
        new_left = left + column_turn(right, 1)
        for at, plane in enumerate(batch):
            store(field, block(plane, PTS - 1), new_right[at * PTS : (at + 1) * PTS])
            store(field, block(plane, 0), new_left[at * PTS : (at + 1) * PTS])
    keep_upper, keep_lower = lane_masks(PTS * BATCH, tiles * TILE)
    for batch in batches:
        rows = len(batch) * PTS
        inner_at = [pl.ds(plane * 64, PTS, stride=PTS) for plane in batch]
        outer_at = [pl.ds(plane * 64 + PTS - 1, PTS, stride=PTS) for plane in batch]
        inner = jnp.concatenate([load(field, at, tiles) for at in inner_at])
        outer = jnp.concatenate([load(field, at, tiles) for at in outer_at])
        new_outer = outer + radial_turn(inner, -1) * keep_upper[:rows]
        new_inner = inner + radial_turn(outer, 1) * keep_lower[:rows]
        for at in range(len(batch)):
            store(field, outer_at[at], new_outer[at * PTS : (at + 1) * PTS])
            store(field, inner_at[at], new_inner[at * PTS : (at + 1) * PTS])


def fold(a, b, c, d):
    sum_k, diff_k = a + b, a - b
    sum_m, diff_m = c + d, c - d
    return sum_k + sum_m, sum_k - sum_m, diff_k + diff_m, diff_k - diff_m


def each_class(body, rolled):
    if rolled:

        def step(c, carry):
            body(c)
            return carry

        lax.fori_loop(0, 4, step, 0)
    else:
        for c in range(4):
            body(c)


def class_rows(c, rows):
    return slice(c * rows, (c + 1) * rows) if isinstance(c, int) else pl.ds(pl.multiple_of(c * rows, rows), rows)


def pack(parts, packed, rows, tiles, rolled=False):
    def body(c):
        for t in range(tiles):
            lanes = slice(t * TILE, (t + 1) * TILE)
            high, low = halves(parts[c * tiles + t, 0:rows, :])
            packed[c, 0:rows, lanes] = high
            packed[c, rows : 2 * rows, lanes] = low
            packed[c, 2 * rows : 3 * rows, lanes] = high

    each_class(body, rolled)


def unfold(ss, sa, as_, aa):
    sum_k, sum_m = ss + sa, ss - sa
    diff_k, diff_m = as_ + aa, as_ - aa
    return sum_k + diff_k, sum_k - diff_k, sum_m + diff_m, sum_m - diff_m


def mirrored(i, k):
    return (i, k), (PTS - 1 - i, k), (i, PTS - 1 - k), (PTS - 1 - i, PTS - 1 - k)


def coefficient_terms(values):
    rows = []
    for value in values:
        parts = []
        for _ in range(3):
            part = value.astype(jnp.bfloat16).astype(jnp.float32)
            parts.append(part)
            value = value - part
        high, middle, low = parts
        rows += [high, middle, low, high, middle, high]
    rows.append(jnp.zeros((TERMS - len(rows), value.shape[1]), jnp.float32))
    return jnp.concatenate(rows).astype(jnp.bfloat16)


def tables_kernel(geo, modes, own, lam, coef, kept, middle):
    kept[0:128] = own[0:128]
    kept[128:256] = own[384:512]
    middle[...] = own[128:384]
    la, lb, lz = (geo[n : n + 1] for n in range(3))
    cz = la * lb / (2.0 * lz)
    ca = lz * lb / (2.0 * la)
    cb = lz * la / (2.0 * lb)
    for at, value in enumerate((cz, ca, cb)):
        coef[at * PTS : (at + 1) * PTS] = jnp.broadcast_to(value, (PTS, LANES))
    terms = coefficient_terms((cz, ca, cb))
    for start, stop in chunks(LANES):
        for c in range(4):
            here = slice(c * MODES, (c + 1) * MODES)
            lam[here, start:stop] = 1.0 / dot(modes[here], terms[:, start:stop])


def window(case, left, own, right, rows):
    shift = (COLS_DEV - LEFT - case) * RADIAL
    joined = join([left[rows], own, right[rows]])
    joined = pltpu.roll(joined, joined.shape[1] - shift, axis=1)[:, :LANES]
    first, *center, last = tiles_of(joined)
    lane = lax.broadcasted_iota(jnp.int32, first.shape, 1)
    half = TILE // 2
    near = jnp.where(lane < half, pltpu.roll(first, half, axis=1), pltpu.roll(last, half, axis=1))
    return join([*center, near, jnp.where(lane < half, first, last)])


def outer_kernel(rot, left, own, right, geo, field, up, down):
    factor = point_factor(LANES)
    for case in range(4):

        @pl.when(rot[0] == case)
        def _(case=case):
            for at, i in enumerate((0, 1, 6, 7)):
                here = slice(at * 64, at * 64 + 64)
                value = window(case, left, own[here], right, here)
                field[here] = value * plane_factor(factor, i)

    up[0:128] = field[128:256]
    down[0:128] = field[0:128]
    length = jnp.broadcast_to(geo[2:3], (PTS, LANES))
    up[128:136] = length
    down[128:136] = length


def follow_kernel(left, right, own, inner):
    inner[...] = own[...]


def inner_kernel(rot, left, own, right, field):
    factor = point_factor(LANES)
    for case in range(4):

        @pl.when(rot[0] == case)
        def _(case=case):
            for at, i in enumerate((2, 3, 4, 5)):
                here = slice(at * 64, at * 64 + 64)
                field[here] = window(case, left, own[here], right, here) * plane_factor(factor, i)


def put(parts, tiles, at, values):
    for c in range(4):
        store(parts, at, values[c], c * tiles)


def layer(value, at):
    return value[at * PTS : (at + 1) * PTS]


def column_halos(field, planes, wide, lanes):
    before = jnp.concatenate([load(field, block(plane, PTS - 2), wide) for plane in planes])
    after = jnp.concatenate([load(field, block(plane, 1), wide) for plane in planes])
    return column_turn(before, 1)[:, :lanes], column_turn(after, -1)[:, :lanes]


def radial_halos(parts, tiles, count):
    masks = lane_masks(4 * count, tiles * TILE)
    found = []
    for first, steps, keep in ((PTS - 2, 1, masks[1]), (1, -1, masks[0])):
        rows = pl.ds(first, count, stride=PTS)
        values = [load(parts, rows, tiles, c * tiles) for c in range(4)]
        values = radial_turn(jnp.concatenate(values), steps) * keep
        found.append([values[c * count : (c + 1) * count] for c in range(4)])
    return found


def solve_inner_kernel(start_up, wide, tiles, *refs):
    if start_up:
        outer, inner, *refs = refs
        planes = [outer[64:128]] + [inner[i * 64 : i * 64 + 64] for i in range(4)] + [outer[128:192]]
    else:
        field, *refs = refs
        planes = [field[i * 64 : i * 64 + 64] for i in range(1, 7)]
    fwd, share, spectrum, ext, parts, packed = refs
    lanes = tiles * TILE
    factor = point_factor(lanes)
    for at, plane in enumerate(planes):
        store(ext, slice(at * 64, at * 64 + 64), plane)
    assemble_sides(ext, range(6), wide)
    for at in range(6):
        here = slice(at * 64, at * 64 + 64)
        share[here] = load(ext, here, tiles) * plane_factor(factor, at + 1)
    for i in range(3):
        for k in range(4):
            corners = ((i, k), (5 - i, k), (i, 7 - k), (5 - i, 7 - k))
            values = fold(*(load(ext, block(p, q), tiles) for p, q in corners))
            put(parts, tiles, block(0, i * 4 + k), values)
    before, after = column_halos(ext, range(6), wide, lanes)
    for i in range(3):
        values = fold(layer(before, i), layer(before, 5 - i), layer(after, i), layer(after, 5 - i))
        put(parts, tiles, slice(96 + i * 8, 104 + i * 8), values)
    put(parts, tiles, slice(120, 128), [jnp.zeros((PTS, lanes), jnp.float32)] * 4)
    lower, upper = radial_halos(parts, tiles, 16)
    put(parts, tiles, slice(128, 144), lower)
    put(parts, tiles, slice(144, 160), upper)
    pack(parts, packed, INNER, tiles, True)

    def forward(c):
        for start, stop in chunks(lanes):
            spectrum[class_rows(c, MODES), start:stop] = dot(fwd[c], packed[c, :, start:stop])

    each_class(forward, True)


def solve_outer_kernel(start_up, wide, tiles, *refs):
    field, below, above, spectrum, lam, fwd, bwd, bwd_low = refs[:8]
    share, modes, up, down, ext, parts, packed = refs[8:]
    lanes = tiles * TILE
    factor = point_factor(lanes)
    last = 192 if start_up else 448
    store(ext, slice(0, 64), below[0:64])
    store(ext, slice(64, 128), field[0:64] + below[64:128])
    store(ext, slice(128, 192), field[last : last + 64] + above[0:64])
    store(ext, slice(192, 256), above[64:128])
    assemble_sides(ext, range(4), wide)
    share[0:64] = load(ext, slice(64, 128), tiles) * plane_factor(factor, 0)
    share[64:128] = load(ext, slice(128, 192), tiles) * plane_factor(factor, 7)
    for k in range(4):
        for at, (p, q) in enumerate(((1, 2), (0, 3))):
            corners = ((p, k), (q, k), (p, 7 - k), (q, 7 - k))
            values = fold(*(load(ext, block(*corner), tiles) for corner in corners))
            put(parts, tiles, block(0, at * 4 + k), values)
    before, after = column_halos(ext, (1, 2), wide, lanes)
    values = fold(layer(before, 0), layer(before, 1), layer(after, 0), layer(after, 1))
    put(parts, tiles, slice(64, 72), values)
    lower, upper = radial_halos(parts, tiles, 4)
    put(parts, tiles, slice(72, 80), [jnp.concatenate(pair) for pair in zip(lower, upper)])
    pack(parts, packed, OUTER, tiles)
    for c in range(4):
        for start, stop in chunks(lanes):
            here = slice(c * MODES, (c + 1) * MODES)
            value = dot(fwd[c], packed[c, :, start:stop]) + spectrum[here, start:stop]
            modes[c, 0:MODES, start:stop], modes[c, MODES:, start:stop] = halves(value * lam[here, start:stop])
    back(modes, bwd, bwd_low, parts, tiles, 32, False)
    for k in range(4):
        classes = (load(parts, block(0, k), tiles, c * tiles) for c in range(4))
        values = unfold(*classes)
        for (p, q), value in zip(mirrored(0, k), values):
            (down if p == 0 else up)[block(0, q)] = value * factor


def back(modes, bwd, bwd_low, parts, tiles, rows, rolled):
    def body(c):
        for start, stop in chunks(tiles * TILE):
            value = dot(bwd[c], modes[c, :, start:stop])
            value = value + dot(bwd_low[c], modes[c, 0:MODES, start:stop])
            store(parts, slice(0, rows), value, c * tiles + start // TILE)

    each_class(body, rolled)


def stepped(kind, value, before):
    if kind in (0, 2):
        return value * (1.0 / theta)
    return before * (rho_second * rho_first) + value * (2.0 * rho_second / delta)


def step_inner_kernel(kind, wide, tiles, *refs):
    take = iter(refs)
    modes = next(take)
    before = next(take) if kind in (1, 3) else None
    total = next(take) if kind != 0 else None
    coef, app, bwd, bwd_low = (next(take) for _ in range(4))
    step = next(take) if kind in (0, 2) else None
    sum_out = next(take) if kind != 0 else None
    image, ext, parts, packed = take
    lanes = tiles * TILE
    factor = point_factor(wide * TILE)
    back(modes, bwd, bwd_low, parts, wide, 96, True)
    for i in range(3):
        for k in range(4):
            classes = (load(parts, block(0, i * 4 + k), wide, c * wide) for c in range(4))
            corners = ((i, k), (5 - i, k), (i, 7 - k), (5 - i, 7 - k))
            for corner, value in zip(corners, unfold(*classes)):
                store(ext, block(*corner), value * factor)
    assemble_sides(ext, range(6), wide)
    for i in range(6):
        here = slice(i * 64, i * 64 + 64)
        value = stepped(kind, load(ext, here, tiles), None if before is None else before[here, :lanes])
        if step is not None:
            step[here] = value
        if sum_out is not None:
            sum_out[here] = total[here, :lanes] + value
        store(ext, here, value)
    for i in range(3):
        for k in range(4):
            corners = ((i, k), (5 - i, k), (i, 7 - k), (5 - i, 7 - k))
            values = fold(*(load(ext, block(p, q), tiles) for p, q in corners))
            put(parts, tiles, block(0, i * 4 + k), values)
    pack(parts, packed, 96, tiles, True)

    def operate(c):
        for start, stop in chunks(lanes):
            terms = dot(app[c], packed[c, :, start:stop]).reshape(40, PTS, stop - start)
            value = terms[0:16] * coef[0:8, start:stop]
            sides = terms[16:28] * coef[8:16, start:stop] + terms[28:40] * coef[16:24, start:stop]
            value = jnp.concatenate([value[0:4], value[4:16] + sides])
            image[class_rows(c, 128), start:stop] = value.reshape(128, stop - start)

    each_class(operate, True)


def step_outer_kernel(kind, wide, tiles, *refs):
    take = iter(refs)
    last, below, first, above = (next(take) for _ in range(4))
    before = next(take) if kind in (1, 3) else None
    total = next(take) if kind != 0 else None
    share_inner, share_outer, image, coef, app = (next(take) for _ in range(5))
    res, res_low = (next(take), next(take)) if kind == 1 else (None, None)
    step = next(take) if kind in (0, 2) else None
    sum_out = next(take) if kind != 0 else None
    field, up, down = next(take), next(take), next(take)
    coarse = next(take) if kind == 1 else None
    ext, parts, packed = next(take), next(take), next(take)
    split_field = next(take) if kind == 1 else None
    lanes = tiles * TILE
    store(ext, slice(0, 64), first[...] + below[...])
    store(ext, slice(64, 128), last[...] + above[...])
    assemble_sides(ext, range(2), wide)
    for at in range(2):
        here = slice(at * 64, at * 64 + 64)
        value = stepped(kind, load(ext, here, tiles), None if before is None else before[here, :lanes])
        if step is not None:
            step[here] = value
        if sum_out is not None:
            sum_out[here] = total[here, :lanes] + value
        store(ext, here, value)
    for k in range(4):
        corners = ((0, k), (1, k), (0, 7 - k), (1, 7 - k))
        values = fold(*(load(ext, block(p, q), tiles) for p, q in corners))
        put(parts, tiles, block(0, k), values)
    pack(parts, packed, 32, tiles)
    for c in range(4):
        for start, stop in chunks(lanes):
            terms = dot(app[c], packed[c, :, start:stop]).reshape(24, PTS, stop - start)
            value = terms[0:16] * coef[0:8, start:stop]
            sides = terms[16:20] * coef[8:16, start:stop] + terms[20:24] * coef[16:24, start:stop]
            value = jnp.concatenate([value[0:4] + sides, value[4:16]]).reshape(128, stop - start)
            value = value + image[c * 128 : (c + 1) * 128, start:stop]
            store(parts, slice(0, 128), value, c * tiles + start // TILE)
    for i in range(4):
        for k in range(4):
            classes = (load(parts, block(0, i * 4 + k), tiles, c * tiles) for c in range(4))
            for (p, q), value in zip(mirrored(i, k), unfold(*classes)):
                if p in (0, 7):
                    shared = share_outer[block(p // 7, q), :lanes]
                else:
                    shared = share_inner[block(p - 1, q), :lanes]
                field[block(p, q)] = shared - value
    if kind == 1:
        split_field[0:512], split_field[512:1024] = halves(field[...])
        for start, stop in chunks(lanes):
            value = dot(res[...], split_field[:, start:stop])
            coarse[:, start:stop] = value + dot(res_low[...], split_field[0:512, start:stop])
        up[...] = coarse[48:64]
        down[...] = coarse[0:16]
    elif kind == 3:
        up[...] = field[448:512]
        down[...] = field[0:64]
    else:
        up[...] = field[384:512]
        down[...] = field[0:128]


def assemble_coarse(value):
    lanes = value.shape[1]
    row = lax.broadcasted_iota(jnp.int32, (64, lanes), 0)
    keep_upper, keep_lower = lane_masks(64, lanes)
    first = (row % 16) < 4
    last = (row % 16) >= 12
    over = pltpu.roll(column_turn(value, -1), 12, axis=0)
    under = pltpu.roll(column_turn(value, 1), 64 - 12, axis=0)
    value = value + jnp.where(last, over, 0.0) + jnp.where(first, under, 0.0)
    first = (row % 4) == 0
    last = (row % 4) == 3
    over = pltpu.roll(radial_turn(value, -1) * keep_upper, 3, axis=0)
    under = pltpu.roll(radial_turn(value, 1) * keep_lower, 64 - 3, axis=0)
    return value + jnp.where(last, over, 0.0) + jnp.where(first, under, 0.0)


def diagonal_kernel(lower, upper, geo, table, scale):
    lanes = scale.shape[1]
    la, lb = geo[0:1, :lanes], geo[1:2, :lanes]

    def local(lz, rows):
        return (
            la * lb / (2.0 * lz) * table[rows, 0:1]
            + lz * lb / (2.0 * la) * table[rows, 1:2]
            + lz * la / (2.0 * lb) * table[rows, 2:3]
        )

    value = local(geo[2:3, :lanes], slice(0, 64))
    first = value[0:16] + local(lower[128:129, :lanes], slice(48, 64))
    last = value[48:64] + local(upper[128:129, :lanes], slice(0, 16))
    scale[...] = assemble_coarse(jnp.concatenate([first, value[16:48], last]))


def coarse_outer_kernel(local, below, above, scale, coef, prolong, field, out, pack, up, down):
    lanes = local.shape[1]
    value = local[...]
    value = jnp.concatenate([value[0:16] + below[...], value[16:48], value[48:64] + above[...]])
    value = assemble_coarse(value) / scale[...]
    high, low = halves(value)
    pack[0, 0:64] = high
    pack[0, 64:128] = low
    pack[0, 128:192] = high
    for at, i in enumerate((0, 1, 6, 7)):
        correct(i, slice(at * 64, at * 64 + 64), coef, prolong, pack, field, out)
    up[...] = out[128:256]
    down[...] = out[0:128]


def coarse_inner_kernel(pack, coef, prolong, total_inner, total_outer, field, sum_inner, sum_outer, out):
    for at, i in enumerate((2, 3, 4, 5)):
        correct(i, slice(at * 64, at * 64 + 64), coef, prolong, pack, field, out)
    for start, stop in chunks(pack.shape[2]):
        for i in range(PTS):
            value = dot(prolong[i * 64 : i * 64 + 64], pack[0, :, start:stop])
            if i in (0, 7):
                at = slice(i // 7 * 64, i // 7 * 64 + 64)
                sum_outer[at, start:stop] = total_outer[at, start:stop] + value
            else:
                at = slice(i * 64 - 64, i * 64)
                sum_inner[at, start:stop] = total_inner[at, start:stop] + value


def correct(i, to, coef, prolong, pack, field, out):
    here = slice(i * 64, i * 64 + 64)
    for start, stop in chunks(pack.shape[2]):
        sides = (8, PTS, stop - start)
        value = 0.0
        for n in range(3):
            rows = slice((n + 1) * 512 + i * 64, (n + 1) * 512 + i * 64 + 64)
            term = dot(prolong[rows], pack[0, :, start:stop]).reshape(sides)
            value = value + term * coef[n * PTS : (n + 1) * PTS, start:stop]
        out[to, start:stop] = field[here, start:stop] - value.reshape(64, stop - start)


def finish_inner_kernel(rot, local, total_inner, total_outer, sol, res, ext):
    tiles = local.shape[1] // TILE
    for i in range(6):
        store(ext, slice(i * 64, i * 64 + 64), local[i * 64 + 64 : i * 64 + 128])
    assemble_sides(ext, range(6), tiles)
    for case in range(4):

        @pl.when(rot[0] == case)
        def _(case=case):
            start = (LEFT + case - RINGS[0][0]) * RADIAL
            for plane in range(PTS):
                here = slice(plane * 64, plane * 64 + 64)
                if plane in (0, 7):
                    at = plane // 7 * 64
                    sol[here] = total_outer[at : at + 64, start : start + OWN]
                else:
                    before = slice(plane * 64 - 64, plane * 64)
                    sol[here] = total_inner[before, start : start + OWN]
                    res[before] = load(ext, before, tiles)[:, start : start + OWN]


def finish_outer_kernel(rot, local, below, above, inner, res, ext):
    tiles = local.shape[1] // TILE
    store(ext, slice(0, 64), local[0:64] + below[...])
    store(ext, slice(64, 128), local[448:512] + above[...])
    assemble_sides(ext, range(2), tiles)
    res[64:448] = inner[...]
    for case in range(4):

        @pl.when(rot[0] == case)
        def _(case=case):
            start = (LEFT + case - RINGS[0][0]) * RADIAL
            res[0:64] = load(ext, slice(0, 64), tiles)[:, start : start + OWN]
            res[448:512] = load(ext, slice(64, 128), tiles)[:, start : start + OWN]


def call(kernel, name, args, outs, scratch=(), scalars=0, flops=0, untouched=0):
    spaces = [pltpu.SMEM] * scalars + [pl.ANY] * untouched
    spaces += [pltpu.VMEM] * (len(args) - len(spaces))
    in_specs = [pl.BlockSpec(memory_space=space) for space in spaces]
    return pl.pallas_call(
        kernel,
        out_shape=[
            jax.ShapeDtypeStruct(out, jnp.float32 if len(out) == 2 else jnp.bfloat16) for out in outs
        ],
        in_specs=in_specs,
        out_specs=[pl.BlockSpec(memory_space=pltpu.VMEM) for _ in outs],
        scratch_shapes=list(scratch),
        name=name,
        cost_estimate=pl.CostEstimate(flops=flops, bytes_accessed=4_000_000, transcendentals=0),
        compiler_params=pltpu.CompilerParams(vmem_limit_bytes=40 * 1024 * 1024),
    )(*args)


def per_device(rhs, spacing_z, spacing_a, spacing_b, rotation):
    mats = matrices()
    group = lax.axis_index("grp")
    member = lax.axis_index("sub")
    groups = lax.axis_size("grp")
    members = lax.axis_size("sub")
    wide, narrow = jnp.float32, jnp.bfloat16
    vmem = pltpu.VMEM

    def shifted(value, axis, count, steps):
        return lax.ppermute(value, axis, [(n, (n + steps) % count) for n in range(count)])

    def neighbours(up, down):
        return shifted(up, "grp", groups, 1), shifted(down, "grp", groups, -1)

    def beside(value):
        return shifted(value, "sub", members, 1), shifted(value, "sub", members, -1)

    def shapes(tiles, *rows):
        return tuple((count, tiles * TILE) for count in rows)

    own = rhs.reshape(512, OWN)
    left, right = beside(jnp.concatenate([own[0:128], own[384:512]]))
    rot = lax.dynamic_slice(rotation, (group,), (1,))
    ring = jnp.concatenate([spacing_a, spacing_a, spacing_a])
    columns = lax.dynamic_slice(ring, (spacing_a.shape[0] + member * COLS_DEV - LEFT,), (WIN,))
    columns = jnp.concatenate([columns[start:stop] for start, stop in RINGS])
    geo = jnp.stack(
        [
            jnp.repeat(columns, RADIAL),
            jnp.tile(spacing_b, WIN),
            jnp.broadcast_to(spacing_z, (LANES,)),
        ]
    )
    geo = jnp.concatenate([geo, jnp.ones((5, LANES), wide)])
    lam, coef, own, middle = call(
        tables_kernel,
        "tables",
        (geo, mats["modes"], own),
        ((4 * MODES, LANES), (24, LANES), (256, OWN), (256, OWN)),
    )
    (middle,) = call(follow_kernel, "follow", (left, right, middle), ((256, OWN),), untouched=2)
    near, far = beside(middle)
    outer, up, down = call(
        outer_kernel,
        "outer",
        (rot, left, own, right, geo),
        ((256, LANES), (136, LANES), (136, LANES)),
        scalars=1,
    )
    lower, upper = neighbours(up, down)
    (inner,) = call(
        inner_kernel, "inner", (rot, near, middle, far), ((256, LANES),), scalars=1, flops=EARLY
    )

    def solve(fields, below, above, before, tiles):
        lanes = tiles * TILE
        start_up = len(fields) == 2
        share_inner, spectrum = call(
            functools.partial(solve_inner_kernel, start_up, before, tiles),
            "solve_inner",
            (*fields, mats["forward_inner"]),
            shapes(tiles, 384, 4 * MODES),
            (
                vmem((before, 384, TILE), wide),
                vmem((4 * tiles, INNER, TILE), wide),
                vmem((4, 3 * INNER, lanes), narrow),
            ),
        )
        share_outer, modes, up, down = call(
            functools.partial(solve_outer_kernel, start_up, before, tiles),
            "solve_outer",
            (fields[0], below, above, spectrum, lam, mats["forward_outer"], *mats["backward_outer"]),
            (*shapes(tiles, 128), (4, 2 * MODES, lanes), *shapes(tiles, 64, 64)),
            (
                vmem((before, 256, TILE), wide),
                vmem((4 * tiles, 128, TILE), wide),
                vmem((4, 3 * OUTER, lanes), narrow),
            ),
        )
        return (share_inner, share_outer), (modes, up, down), neighbours(up, down)

    def advance(kind, local, messages, share, before, total, width, tiles):
        lanes = tiles * TILE

        def scratch(rows, folded):
            return [
                vmem((width, rows, TILE), wide),
                vmem((4 * width, 128, TILE), wide),
                vmem((4, folded, lanes), narrow),
            ]

        def pick(at):
            return [pair[at] for pair in (before, total) if pair is not None]

        kept = [count for count, used in ((1, kind in (0, 2)), (1, kind != 0)) if used]
        *inner, image = call(
            functools.partial(step_inner_kernel, kind, width, tiles),
            f"step{kind}_inner",
            (local[0], *pick(0), coef, mats["apply_inner"], *mats["backward_inner"]),
            shapes(tiles, *(384 for _ in kept), 512),
            scratch(384, 288),
        )
        sent = {0: 128, 1: 16, 2: 128, 3: 64}[kind]
        extra = scratch(128, 96)
        if kind == 1:
            extra.append(vmem((1024, lanes), narrow))
        out = call(
            functools.partial(step_outer_kernel, kind, width, tiles),
            f"step{kind}_outer",
            (
                *(local[1], messages[0], local[2], messages[1]),
                *(*pick(1), *share, image, coef, mats["apply_outer"]),
                *(mats["restrict"] if kind == 1 else ()),
            ),
            shapes(tiles, *(128 for _ in kept), 512, sent, sent, *((64,) if kind == 1 else ())),
            extra,
        )
        outer, (field, up, down, *coarse) = out[: len(kept)], out[len(kept) :]
        return list(zip(inner, outer)), field, neighbours(up, down), *coarse

    share, local, messages = solve((outer, inner), lower, upper, 5, 5)
    (step,), field, messages = advance(0, local, messages, share, None, None, 5, 5)
    share, local, messages = solve((field,), *messages, 5, 5)
    (total,), field, messages, coarse = advance(1, local, messages, share, step, step, 5, 4)
    (scale,) = call(diagonal_kernel, "diagonal", (lower, upper, geo, mats["coarse"]), shapes(4, 64))
    outer, terms, up, down = call(
        coarse_outer_kernel,
        "coarse_outer",
        (coarse, *messages, scale, coef, mats["prolong"], field),
        (*shapes(4, 256), (1, 192, 4 * TILE), *shapes(4, 128, 128)),
    )
    messages = neighbours(up, down)
    *total, inner = call(
        coarse_inner_kernel,
        "coarse_inner",
        (terms, coef, mats["prolong"], *total, field),
        shapes(4, 384, 128, 256),
    )
    share, local, messages = solve((outer, inner), *messages, 4, 4)
    (step, total), field, messages = advance(2, local, messages, share, None, total, 4, 4)
    share, local, messages = solve((field,), *messages, 4, 3)
    (total,), field, messages = advance(3, local, messages, share, step, total, 3, 3)
    sol, inner = call(
        finish_inner_kernel,
        "finish_inner",
        (rot, field, *total),
        ((512, OWN), (384, OWN)),
        (vmem((3, 384, TILE), wide),),
        scalars=1,
    )
    (res,) = call(
        finish_outer_kernel,
        "finish_outer",
        (rot, field, *messages, inner),
        ((512, OWN),),
        (vmem((3, 128, TILE), wide),),
        scalars=1,
    )
    return sol.reshape(rhs.shape), res.reshape(rhs.shape)


def solution(mesh):
    return jax.shard_map(
        per_device,
        mesh=mesh,
        in_specs=(P(None, None, None, ("grp", "sub")), P("grp"), P(), P(), P()),
        out_specs=(P(None, None, None, ("grp", "sub")), P(None, None, None, ("grp", "sub"))),
        check_vma=False,
    )
```

```python
import functools

import jax
import jax.numpy as jnp
import ml_dtypes
import numpy as np
from jax import lax
from jax.experimental import pallas as pl
from jax.experimental.pallas import tpu as pltpu
from jax.sharding import PartitionSpec as P

PTS = 8
CPTS = 4
COLS_DEV = 16
RADIAL = 16
SMOOTH = 2

WIN = 40
LEFT = 10
LANES = WIN * RADIAL
RINGS = ((8, 32), (4, 8), (32, 36), (0, 4), (36, 40))
OWN = COLS_DEV * RADIAL
CLASSES = ((0, 0), (0, 1), (1, 0), (1, 1))
INNER = 160
OUTER = 80
MODES = 256
TILE = 128
TILES = LANES // TILE
TERMS = 32
BATCH = 4
EARLY = 20_000_000_000

cheb_upper = 2.0
cheb_ratio = 0.1
theta = 0.5 * (cheb_upper + cheb_upper * cheb_ratio)
delta = 0.5 * (cheb_upper - cheb_upper * cheb_ratio)
sigma = theta / delta
rho_first = 1.0 / sigma
rho_second = 1.0 / (2.0 * sigma - rho_first)


def legendre_rows(gll_nodes, poly_order):
    values = np.zeros((gll_nodes.size, poly_order + 1))
    values[:, 0] = 1.0
    values[:, 1] = gll_nodes
    for degree in range(2, poly_order + 1):
        values[:, degree] = (
            (2 * degree - 1) * gll_nodes * values[:, degree - 1]
            - (degree - 1) * values[:, degree - 2]
        ) / degree
    return values


def jacobi_eigen(matrix):
    order = matrix.shape[0]
    current = matrix.copy()
    vectors = np.eye(order)
    for sweep in range(12):
        for first in range(order - 1):
            for second in range(first + 1, order):
                off_value = current[first, second]
                spread = current[second, second] - current[first, first]
                sense = np.where(spread >= 0.0, 1.0, -1.0)
                denom = spread + sense * np.sqrt(spread * spread + 4.0 * off_value * off_value)
                denom = np.where(denom == 0.0, 1.0, denom)
                tangent = 2.0 * off_value / denom
                cosine = 1.0 / np.sqrt(1.0 + tangent * tangent)
                sine = tangent * cosine
                rotate = np.eye(order)
                rotate[first, first] = cosine
                rotate[second, second] = cosine
                rotate[first, second] = sine
                rotate[second, first] = -sine
                current = rotate.T @ current @ rotate
                vectors = vectors @ rotate
    diag_ids = np.arange(order)
    return (current[diag_ids, diag_ids].copy(), vectors)


def lobatto(poly_order):
    gll_nodes = np.cos(np.pi * np.arange(poly_order + 1) / poly_order)
    for newton in range(100):
        values = legendre_rows(gll_nodes, poly_order)
        gll_nodes = gll_nodes - (gll_nodes * values[:, poly_order] - values[:, poly_order - 1]) / (
            (poly_order + 1) * values[:, poly_order]
        )
    values = legendre_rows(gll_nodes, poly_order)
    gll_nodes = gll_nodes[::-1].copy()
    top_poly = values[::-1, poly_order].copy()
    weights = 2.0 / (poly_order * (poly_order + 1) * top_poly**2)
    derivative = np.zeros((poly_order + 1, poly_order + 1))
    for row_index in range(poly_order + 1):
        for col_index in range(poly_order + 1):
            if row_index != col_index:
                derivative[row_index, col_index] = top_poly[row_index] / (
                    top_poly[col_index] * (gll_nodes[row_index] - gll_nodes[col_index])
                )
    derivative[0, 0] = -poly_order * (poly_order + 1) / 4.0
    derivative[poly_order, poly_order] = poly_order * (poly_order + 1) / 4.0
    stiffness = derivative.T @ (weights[:, None] * derivative)
    return (gll_nodes, weights, stiffness)


def element_tables():
    fine_nodes, fine_weights, fine_stiff = lobatto(PTS - 1)
    coarse_nodes, coarse_weights, coarse_stiff = lobatto(CPTS - 1)
    interp = np.ones((PTS, CPTS))
    for target_col in range(CPTS):
        for other_col in range(CPTS):
            if other_col != target_col:
                interp[:, target_col] *= (fine_nodes - coarse_nodes[other_col]) / (
                    coarse_nodes[target_col] - coarse_nodes[other_col]
                )
    poly_order = PTS - 1
    node_count = 3 * poly_order + 1
    joined_stiff = np.zeros((node_count, node_count))
    joined_mass = np.zeros(node_count)
    for piece_index in range(3):
        first_node = piece_index * poly_order
        joined_stiff[first_node : first_node + PTS, first_node : first_node + PTS] += fine_stiff
        joined_mass[first_node : first_node + PTS] += fine_weights
    kept = slice(poly_order - 1, 2 * poly_order + 2)
    root_mass = np.sqrt(joined_mass[kept])
    eigen_values, eigen_vectors = jacobi_eigen(
        joined_stiff[kept, kept] / root_mass[:, None] / root_mass[None, :]
    )
    eigen_basis = eigen_vectors / root_mass[:, None]
    coarse_diag = np.diag(coarse_stiff).copy()
    return fine_stiff, fine_weights, eigen_basis, eigen_values, interp, coarse_diag, coarse_weights


def split(table):
    high = table.astype(np.float32).astype(ml_dtypes.bfloat16)
    low = (table - high.astype(np.float64)).astype(np.float32).astype(ml_dtypes.bfloat16)
    return high, low


def kron3(first, second, third):
    return np.kron(first, np.kron(second, third))


def spread(values):
    terms = np.zeros((values.shape[0], TERMS), ml_dtypes.bfloat16)
    for at in range(3):
        high, rest = split(values[:, at])
        middle, low = split(values[:, at] - high.astype(np.float64))
        for n, part in enumerate((high, high, high, middle, middle, low)):
            terms[:, at * 6 + n] = part
    return terms


def matrices():
    stiff, weights, basis, values, interp, coarse_diag, coarse_weights = element_tables()
    parts = ([], [])
    for mode in range(PTS + 2):
        column = basis[:, mode]
        odd = np.abs(column + column[::-1]).sum() < np.abs(column - column[::-1]).sum()
        parts[int(odd)].append(mode)
    signs = (1.0, -1.0)
    pure = basis.copy()
    for parity in (0, 1):
        for mode in parts[parity]:
            pure[:, mode] = 0.5 * (basis[:, mode] + signs[parity] * basis[::-1, mode])
    center = pure[1:-1, :]
    edges = pure[[0, -1], :]

    def folded(matrix, parity):
        half = PTS // 2
        return 0.5 * (matrix[:half, :half] + signs[parity] * matrix[:half, ::-1][:, :half])

    mass = np.diag(weights)
    halved = np.ones(PTS // 2)
    halved[0] = 0.5
    forward_inner = np.zeros((4, MODES, INNER))
    forward_outer = np.zeros((4, MODES, OUTER))
    backward = np.zeros((4, PTS * 16, MODES))
    apply_inner = np.zeros((4, 320, 96))
    apply_outer = np.zeros((4, 192, 32))
    mode_values = np.ones((4, MODES, 3))
    for at, (pi, pk) in enumerate(CLASSES):
        ci, ck = center[:4, parts[pi]], center[:4, parts[pk]]
        ei, ek = edges[:1, parts[pi]], edges[:1, parts[pk]]
        count = len(parts[pi]) * len(parts[pk]) * (PTS + 2)
        rest = ci[1:]
        gap = lambda rows: np.zeros((rows, count))
        columns = [kron3(rest, ck, center), kron3(rest, ek, center), gap(8)]
        columns += [kron3(rest, ck, edges[:1]), gap(4), kron3(rest, ck, edges[1:]), gap(4)]
        forward_inner[at, :count] = np.concatenate(columns, axis=0).T
        columns = [kron3(ci[:1], ck, center), kron3(ei, ck, center), kron3(ci[:1], ek, center)]
        columns += [kron3(ci[:1], ck, edges[:1]), kron3(ci[:1], ck, edges[1:])]
        forward_outer[at, :count] = np.concatenate(columns, axis=0).T
        backward[at, :, :count] = kron3(halved[:, None] * ci, halved[:, None] * ck, center)
        vi, vk = values[parts[pi]], values[parts[pk]]
        ones = np.ones
        mode_values[at, :count, 0] = kron3(vi, ones(len(vk)), ones(PTS + 2))
        mode_values[at, :count, 1] = kron3(ones(len(vi)), vk, ones(PTS + 2))
        mode_values[at, :count, 2] = kron3(ones(len(vi)), ones(len(vk)), values)
        si, sk = folded(stiff, pi), folded(stiff, pk)
        mi, mk = folded(mass, pi), folded(mass, pk)
        along_z, along_a, along_b = kron3(si, mk, mass), kron3(mi, sk, mass), kron3(mi, mk, stiff)
        apply_inner[at] = np.concatenate([along_z[:, 32:], along_a[32:, 32:], along_b[32:, 32:]])
        apply_outer[at] = np.concatenate([along_z[:, :32], along_a[:32, :32], along_b[:32, :32]])
    mass_up, stiff_up = mass @ interp, stiff @ interp
    prolong = np.concatenate(
        [
            kron3(interp, interp, interp),
            kron3(stiff_up, mass_up, mass_up),
            kron3(mass_up, stiff_up, mass_up),
            kron3(mass_up, mass_up, stiff_up),
        ],
        axis=0,
    )
    restrict = kron3(interp.T, interp.T, interp.T)
    coarse = np.zeros((CPTS**3, 8))
    coarse[:, 0] = kron3(coarse_diag, coarse_weights, coarse_weights)
    coarse[:, 1] = kron3(coarse_weights, coarse_diag, coarse_weights)
    coarse[:, 2] = kron3(coarse_weights, coarse_weights, coarse_diag)

    def pair(table):
        high, low = split(table)
        return jnp.asarray(np.concatenate([high, high], axis=-1)), jnp.asarray(low)

    def triple(table):
        high, low = split(table)
        return jnp.asarray(np.concatenate([high, high, low], axis=-1))

    return {
        "forward_inner": triple(forward_inner),
        "forward_outer": triple(forward_outer),
        "backward_outer": pair(backward[:, :32]),
        "backward_inner": pair(backward[:, 32:]),
        "apply_inner": triple(apply_inner),
        "apply_outer": triple(apply_outer),
        "restrict": pair(restrict),
        "prolong": triple(prolong),
        "modes": jnp.asarray(spread(mode_values.reshape(4 * MODES, 3))),
        "coarse": jnp.asarray(coarse.astype(np.float32)),
    }


def halves(value):
    high = value.astype(jnp.bfloat16)
    low = (value - high.astype(jnp.float32)).astype(jnp.bfloat16)
    return high, low


def dot(left, right):
    return jnp.dot(left, right, preferred_element_type=jnp.float32)


def join(tiles):
    return jnp.concatenate(tiles, axis=1)


def tiles_of(value):
    return [value[:, t * TILE : (t + 1) * TILE] for t in range(value.shape[1] // TILE)]


def radial_turn(value, steps):
    return join([pltpu.roll(tile, steps % TILE, axis=1) for tile in tiles_of(value)])


def column_turn(value, direction):
    tiles = tiles_of(value)
    count = len(tiles)
    lane = lax.broadcasted_iota(jnp.int32, tiles[0].shape, 1)
    near = [pltpu.roll(tile, (direction * RADIAL) % TILE, axis=1) for tile in tiles]
    far = lambda at: pltpu.roll(tiles[at], (TILE // 2 + direction * RADIAL) % TILE, axis=1)
    out = list(near)
    if direction < 0:
        high_end, low_end = lane >= TILE - RADIAL, (lane >= TILE // 2 - RADIAL) & (lane < TILE // 2)
        out[0] = jnp.where(high_end, near[1], near[0])
        out[1] = jnp.where(high_end, near[2], near[1])
        inner, outer, middle = 2, high_end, low_end
        edge = 0
    else:
        high_end, low_end = lane < RADIAL, (lane >= TILE // 2) & (lane < TILE // 2 + RADIAL)
        out[1] = jnp.where(high_end, near[0], near[1])
        out[2] = jnp.where(high_end, near[1], near[2])
        inner, outer, middle = 0, high_end, low_end
        edge = 2
    if count > 3:
        first_ring = far(3)
        out[inner] = jnp.where(outer, first_ring, out[inner])
        out[3] = jnp.where(middle, far(edge), near[3])
    if count > 4:
        out[3] = jnp.where(outer, far(4), out[3])
        out[4] = jnp.where(middle, first_ring, near[4])
    return join(out)


def lane_masks(rows, lanes):
    radial = lax.broadcasted_iota(jnp.int32, (rows, lanes), 1) % RADIAL
    keep_upper = (radial < RADIAL - 1).astype(jnp.float32)
    keep_lower = (radial > 0).astype(jnp.float32)
    return keep_upper, keep_lower


def chunks(lanes):
    return [(start, min(start + 2 * TILE, lanes)) for start in range(0, lanes, 2 * TILE)]


def point_factor(lanes):
    point = lax.broadcasted_iota(jnp.int32, (PTS, lanes), 0)
    radial = lax.broadcasted_iota(jnp.int32, (PTS, lanes), 1) % RADIAL
    shared = ((point == 0) & (radial > 0)) | ((point == PTS - 1) & (radial < RADIAL - 1))
    return jnp.where(shared, 0.5, 1.0)


def side_factor(i, k):
    return (0.5 if i in (0, PTS - 1) else 1.0) * (0.5 if k in (0, PTS - 1) else 1.0)


def plane_factor(factor, i):
    return jnp.concatenate([factor * side_factor(i, k) for k in range(PTS)])


def block(plane, k):
    start = plane * 64 + k * PTS
    return slice(start, start + PTS)


def load(ref, rows, tiles, base=0):
    return join([ref[base + t, rows, :] for t in range(tiles)])


def store(ref, rows, value, base=0):
    for t, tile in enumerate(tiles_of(value)):
        ref[base + t, rows, :] = tile


def assemble_sides(field, planes, tiles):
    batches = [planes[start : start + BATCH] for start in range(0, len(planes), BATCH)]
    for batch in batches:
        left = jnp.concatenate([load(field, block(plane, 0), tiles) for plane in batch])
        right = jnp.concatenate([load(field, block(plane, PTS - 1), tiles) for plane in batch])
        new_right = right + column_turn(left, -1)
        new_left = left + column_turn(right, 1)
        for at, plane in enumerate(batch):
            store(field, block(plane, PTS - 1), new_right[at * PTS : (at + 1) * PTS])
            store(field, block(plane, 0), new_left[at * PTS : (at + 1) * PTS])
    keep_upper, keep_lower = lane_masks(PTS * BATCH, tiles * TILE)
    for batch in batches:
        rows = len(batch) * PTS
        inner_at = [pl.ds(plane * 64, PTS, stride=PTS) for plane in batch]
        outer_at = [pl.ds(plane * 64 + PTS - 1, PTS, stride=PTS) for plane in batch]
        inner = jnp.concatenate([load(field, at, tiles) for at in inner_at])
        outer = jnp.concatenate([load(field, at, tiles) for at in outer_at])
        new_outer = outer + radial_turn(inner, -1) * keep_upper[:rows]
        new_inner = inner + radial_turn(outer, 1) * keep_lower[:rows]
        for at in range(len(batch)):
            store(field, outer_at[at], new_outer[at * PTS : (at + 1) * PTS])
            store(field, inner_at[at], new_inner[at * PTS : (at + 1) * PTS])


def fold(a, b, c, d):
    sum_k, diff_k = a + b, a - b
    sum_m, diff_m = c + d, c - d
    return sum_k + sum_m, sum_k - sum_m, diff_k + diff_m, diff_k - diff_m


def each_class(body, rolled):
    if rolled:

        def step(c, carry):
            body(c)
            return carry

        lax.fori_loop(0, 4, step, 0)
    else:
        for c in range(4):
            body(c)


def class_rows(c, rows):
    return slice(c * rows, (c + 1) * rows) if isinstance(c, int) else pl.ds(pl.multiple_of(c * rows, rows), rows)


def pack(parts, packed, rows, tiles, rolled=False):
    def body(c):
        for t in range(tiles):
            lanes = slice(t * TILE, (t + 1) * TILE)
            high, low = halves(parts[c * tiles + t, 0:rows, :])
            packed[c, 0:rows, lanes] = high
            packed[c, rows : 2 * rows, lanes] = low
            packed[c, 2 * rows : 3 * rows, lanes] = high

    each_class(body, rolled)


def unfold(ss, sa, as_, aa):
    sum_k, sum_m = ss + sa, ss - sa
    diff_k, diff_m = as_ + aa, as_ - aa
    return sum_k + diff_k, sum_k - diff_k, sum_m + diff_m, sum_m - diff_m


def mirrored(i, k):
    return (i, k), (PTS - 1 - i, k), (i, PTS - 1 - k), (PTS - 1 - i, PTS - 1 - k)


def coefficient_terms(values):
    rows = []
    for value in values:
        parts = []
        for _ in range(3):
            part = value.astype(jnp.bfloat16).astype(jnp.float32)
            parts.append(part)
            value = value - part
        high, middle, low = parts
        rows += [high, middle, low, high, middle, high]
    rows.append(jnp.zeros((TERMS - len(rows), value.shape[1]), jnp.float32))
    return jnp.concatenate(rows).astype(jnp.bfloat16)


def tables_kernel(rot, geo, modes, own, lam, coef, middle):
    middle[...] = own[128:384]
    la, lb, lz = (geo[n : n + 1] for n in range(3))
    cz = la * lb / (2.0 * lz)
    ca = lz * lb / (2.0 * la)
    cb = lz * la / (2.0 * lb)
    for at, value in enumerate((cz, ca, cb)):
        coef[at * PTS : (at + 1) * PTS] = jnp.broadcast_to(value, (PTS, LANES))
    terms = coefficient_terms((cz, ca, cb))
    for start, stop in chunks(LANES):
        for c in range(4):
            here = slice(c * MODES, (c + 1) * MODES)
            lam[here, start:stop] = 1.0 / dot(modes[here], terms[:, start:stop])


def window(case, left, own, right, rows):
    shift = (COLS_DEV - LEFT - case) * RADIAL
    joined = join([left[rows], own, right[rows]])
    joined = pltpu.roll(joined, joined.shape[1] - shift, axis=1)[:, :LANES]
    first, *center, last = tiles_of(joined)
    lane = lax.broadcasted_iota(jnp.int32, first.shape, 1)
    half = TILE // 2
    near = jnp.where(lane < half, pltpu.roll(first, half, axis=1), pltpu.roll(last, half, axis=1))
    return join([*center, near, jnp.where(lane < half, first, last)])


def outer_kernel(rot, left, own, right, geo, field, up, down):
    factor = point_factor(LANES)
    for case in range(4):

        @pl.when(rot[0] == case)
        def _(case=case):
            for at, i in enumerate((0, 1, 6, 7)):
                here = slice(at * 64, at * 64 + 64)
                value = window(case, left, own[here], right, here)
                field[here] = value * plane_factor(factor, i)

    up[0:128] = field[128:256]
    down[0:128] = field[0:128]
    length = jnp.broadcast_to(geo[2:3], (PTS, LANES))
    up[128:136] = length
    down[128:136] = length


def follow_kernel(left, right, own, inner):
    inner[...] = own[...]


def inner_kernel(rot, left, own, right, field):
    factor = point_factor(LANES)
    for case in range(4):

        @pl.when(rot[0] == case)
        def _(case=case):
            for at, i in enumerate((2, 3, 4, 5)):
                here = slice(at * 64, at * 64 + 64)
                field[here] = window(case, left, own[here], right, here) * plane_factor(factor, i)


def put(parts, tiles, at, values):
    for c in range(4):
        store(parts, at, values[c], c * tiles)


def layer(value, at):
    return value[at * PTS : (at + 1) * PTS]


def column_halos(field, planes, wide, lanes):
    before = jnp.concatenate([load(field, block(plane, PTS - 2), wide) for plane in planes])
    after = jnp.concatenate([load(field, block(plane, 1), wide) for plane in planes])
    return column_turn(before, 1)[:, :lanes], column_turn(after, -1)[:, :lanes]


def radial_halos(parts, tiles, count):
    masks = lane_masks(4 * count, tiles * TILE)
    found = []
    for first, steps, keep in ((PTS - 2, 1, masks[1]), (1, -1, masks[0])):
        rows = pl.ds(first, count, stride=PTS)
        values = [load(parts, rows, tiles, c * tiles) for c in range(4)]
        values = radial_turn(jnp.concatenate(values), steps) * keep
        found.append([values[c * count : (c + 1) * count] for c in range(4)])
    return found


def solve_inner_kernel(start_up, wide, tiles, *refs):
    if start_up:
        outer, inner, *refs = refs
        planes = [outer[64:128]] + [inner[i * 64 : i * 64 + 64] for i in range(4)] + [outer[128:192]]
    else:
        field, *refs = refs
        planes = [field[i * 64 : i * 64 + 64] for i in range(1, 7)]
    fwd, share, spectrum, ext, parts, packed = refs
    lanes = tiles * TILE
    factor = point_factor(lanes)
    for at, plane in enumerate(planes):
        store(ext, slice(at * 64, at * 64 + 64), plane)
    assemble_sides(ext, range(6), wide)
    for at in range(6):
        here = slice(at * 64, at * 64 + 64)
        share[here] = load(ext, here, tiles) * plane_factor(factor, at + 1)
    for i in range(3):
        for k in range(4):
            corners = ((i, k), (5 - i, k), (i, 7 - k), (5 - i, 7 - k))
            values = fold(*(load(ext, block(p, q), tiles) for p, q in corners))
            put(parts, tiles, block(0, i * 4 + k), values)
    before, after = column_halos(ext, range(6), wide, lanes)
    for i in range(3):
        values = fold(layer(before, i), layer(before, 5 - i), layer(after, i), layer(after, 5 - i))
        put(parts, tiles, slice(96 + i * 8, 104 + i * 8), values)
    put(parts, tiles, slice(120, 128), [jnp.zeros((PTS, lanes), jnp.float32)] * 4)
    lower, upper = radial_halos(parts, tiles, 16)
    put(parts, tiles, slice(128, 144), lower)
    put(parts, tiles, slice(144, 160), upper)
    pack(parts, packed, INNER, tiles, True)

    def forward(c):
        for start, stop in chunks(lanes):
            spectrum[class_rows(c, MODES), start:stop] = dot(fwd[c], packed[c, :, start:stop])

    each_class(forward, True)


def solve_outer_kernel(start_up, wide, tiles, *refs):
    field, below, above, spectrum, lam, fwd, bwd, bwd_low = refs[:8]
    share, modes, up, down, ext, parts, packed = refs[8:]
    lanes = tiles * TILE
    factor = point_factor(lanes)
    last = 192 if start_up else 448
    store(ext, slice(0, 64), below[0:64])
    store(ext, slice(64, 128), field[0:64] + below[64:128])
    store(ext, slice(128, 192), field[last : last + 64] + above[0:64])
    store(ext, slice(192, 256), above[64:128])
    assemble_sides(ext, range(4), wide)
    share[0:64] = load(ext, slice(64, 128), tiles) * plane_factor(factor, 0)
    share[64:128] = load(ext, slice(128, 192), tiles) * plane_factor(factor, 7)
    for k in range(4):
        for at, (p, q) in enumerate(((1, 2), (0, 3))):
            corners = ((p, k), (q, k), (p, 7 - k), (q, 7 - k))
            values = fold(*(load(ext, block(*corner), tiles) for corner in corners))
            put(parts, tiles, block(0, at * 4 + k), values)
    before, after = column_halos(ext, (1, 2), wide, lanes)
    values = fold(layer(before, 0), layer(before, 1), layer(after, 0), layer(after, 1))
    put(parts, tiles, slice(64, 72), values)
    lower, upper = radial_halos(parts, tiles, 4)
    put(parts, tiles, slice(72, 80), [jnp.concatenate(pair) for pair in zip(lower, upper)])
    pack(parts, packed, OUTER, tiles)
    for c in range(4):
        for start, stop in chunks(lanes):
            here = slice(c * MODES, (c + 1) * MODES)
            value = dot(fwd[c], packed[c, :, start:stop]) + spectrum[here, start:stop]
            modes[c, 0:MODES, start:stop], modes[c, MODES:, start:stop] = halves(value * lam[here, start:stop])
    back(modes, bwd, bwd_low, parts, tiles, 32, False)
    for k in range(4):
        classes = (load(parts, block(0, k), tiles, c * tiles) for c in range(4))
        values = unfold(*classes)
        for (p, q), value in zip(mirrored(0, k), values):
            (down if p == 0 else up)[block(0, q)] = value * factor


def back(modes, bwd, bwd_low, parts, tiles, rows, rolled):
    def body(c):
        for start, stop in chunks(tiles * TILE):
            value = dot(bwd[c], modes[c, :, start:stop])
            value = value + dot(bwd_low[c], modes[c, 0:MODES, start:stop])
            store(parts, slice(0, rows), value, c * tiles + start // TILE)

    each_class(body, rolled)


def stepped(kind, value, before):
    if kind in (0, 2):
        return value * (1.0 / theta)
    return before * (rho_second * rho_first) + value * (2.0 * rho_second / delta)


def step_inner_kernel(kind, wide, tiles, *refs):
    take = iter(refs)
    modes = next(take)
    before = next(take) if kind in (1, 3) else None
    total = next(take) if kind != 0 else None
    coef, app, bwd, bwd_low = (next(take) for _ in range(4))
    step = next(take) if kind in (0, 2) else None
    sum_out = next(take) if kind != 0 else None
    image, ext, parts, packed = take
    lanes = tiles * TILE
    factor = point_factor(wide * TILE)
    back(modes, bwd, bwd_low, parts, wide, 96, True)
    for i in range(3):
        for k in range(4):
            classes = (load(parts, block(0, i * 4 + k), wide, c * wide) for c in range(4))
            corners = ((i, k), (5 - i, k), (i, 7 - k), (5 - i, 7 - k))
            for corner, value in zip(corners, unfold(*classes)):
                store(ext, block(*corner), value * factor)
    assemble_sides(ext, range(6), wide)
    for i in range(6):
        here = slice(i * 64, i * 64 + 64)
        value = stepped(kind, load(ext, here, tiles), None if before is None else before[here, :lanes])
        if step is not None:
            step[here] = value
        if sum_out is not None:
            sum_out[here] = total[here, :lanes] + value
        store(ext, here, value)
    for i in range(3):
        for k in range(4):
            corners = ((i, k), (5 - i, k), (i, 7 - k), (5 - i, 7 - k))
            values = fold(*(load(ext, block(p, q), tiles) for p, q in corners))
            put(parts, tiles, block(0, i * 4 + k), values)
    pack(parts, packed, 96, tiles, True)

    def operate(c):
        for start, stop in chunks(lanes):
            terms = dot(app[c], packed[c, :, start:stop]).reshape(40, PTS, stop - start)
            value = terms[0:16] * coef[0:8, start:stop]
            sides = terms[16:28] * coef[8:16, start:stop] + terms[28:40] * coef[16:24, start:stop]
            value = jnp.concatenate([value[0:4], value[4:16] + sides])
            image[class_rows(c, 128), start:stop] = value.reshape(128, stop - start)

    each_class(operate, True)


def step_outer_kernel(kind, wide, tiles, *refs):
    take = iter(refs)
    last, below, first, above = (next(take) for _ in range(4))
    before = next(take) if kind in (1, 3) else None
    total = next(take) if kind != 0 else None
    share_inner, share_outer, image, coef, app = (next(take) for _ in range(5))
    res, res_low = (next(take), next(take)) if kind == 1 else (None, None)
    step = next(take) if kind in (0, 2) else None
    sum_out = next(take) if kind != 0 else None
    field, up, down = next(take), next(take), next(take)
    coarse = next(take) if kind == 1 else None
    ext, parts, packed = next(take), next(take), next(take)
    split_field = next(take) if kind == 1 else None
    lanes = tiles * TILE
    store(ext, slice(0, 64), first[...] + below[...])
    store(ext, slice(64, 128), last[...] + above[...])
    assemble_sides(ext, range(2), wide)
    for at in range(2):
        here = slice(at * 64, at * 64 + 64)
        value = stepped(kind, load(ext, here, tiles), None if before is None else before[here, :lanes])
        if step is not None:
            step[here] = value
        if sum_out is not None:
            sum_out[here] = total[here, :lanes] + value
        store(ext, here, value)
    for k in range(4):
        corners = ((0, k), (1, k), (0, 7 - k), (1, 7 - k))
        values = fold(*(load(ext, block(p, q), tiles) for p, q in corners))
        put(parts, tiles, block(0, k), values)
    pack(parts, packed, 32, tiles)
    for c in range(4):
        for start, stop in chunks(lanes):
            terms = dot(app[c], packed[c, :, start:stop]).reshape(24, PTS, stop - start)
            value = terms[0:16] * coef[0:8, start:stop]
            sides = terms[16:20] * coef[8:16, start:stop] + terms[20:24] * coef[16:24, start:stop]
            value = jnp.concatenate([value[0:4] + sides, value[4:16]]).reshape(128, stop - start)
            value = value + image[c * 128 : (c + 1) * 128, start:stop]
            store(parts, slice(0, 128), value, c * tiles + start // TILE)
    for i in range(4):
        for k in range(4):
            classes = (load(parts, block(0, i * 4 + k), tiles, c * tiles) for c in range(4))
            for (p, q), value in zip(mirrored(i, k), unfold(*classes)):
                if p in (0, 7):
                    shared = share_outer[block(p // 7, q), :lanes]
                else:
                    shared = share_inner[block(p - 1, q), :lanes]
                field[block(p, q)] = shared - value
    if kind == 1:
        split_field[0:512], split_field[512:1024] = halves(field[...])
        for start, stop in chunks(lanes):
            value = dot(res[...], split_field[:, start:stop])
            coarse[:, start:stop] = value + dot(res_low[...], split_field[0:512, start:stop])
        up[...] = coarse[48:64]
        down[...] = coarse[0:16]
    elif kind == 3:
        up[...] = field[448:512]
        down[...] = field[0:64]
    else:
        up[...] = field[384:512]
        down[...] = field[0:128]


def assemble_coarse(value):
    lanes = value.shape[1]
    row = lax.broadcasted_iota(jnp.int32, (64, lanes), 0)
    keep_upper, keep_lower = lane_masks(64, lanes)
    first = (row % 16) < 4
    last = (row % 16) >= 12
    over = pltpu.roll(column_turn(value, -1), 12, axis=0)
    under = pltpu.roll(column_turn(value, 1), 64 - 12, axis=0)
    value = value + jnp.where(last, over, 0.0) + jnp.where(first, under, 0.0)
    first = (row % 4) == 0
    last = (row % 4) == 3
    over = pltpu.roll(radial_turn(value, -1) * keep_upper, 3, axis=0)
    under = pltpu.roll(radial_turn(value, 1) * keep_lower, 64 - 3, axis=0)
    return value + jnp.where(last, over, 0.0) + jnp.where(first, under, 0.0)


def diagonal_kernel(lower, upper, geo, table, scale):
    lanes = scale.shape[1]
    la, lb = geo[0:1, :lanes], geo[1:2, :lanes]

    def local(lz, rows):
        return (
            la * lb / (2.0 * lz) * table[rows, 0:1]
            + lz * lb / (2.0 * la) * table[rows, 1:2]
            + lz * la / (2.0 * lb) * table[rows, 2:3]
        )

    value = local(geo[2:3, :lanes], slice(0, 64))
    first = value[0:16] + local(lower[128:129, :lanes], slice(48, 64))
    last = value[48:64] + local(upper[128:129, :lanes], slice(0, 16))
    scale[...] = assemble_coarse(jnp.concatenate([first, value[16:48], last]))


def coarse_outer_kernel(local, below, above, scale, coef, prolong, field, out, pack, up, down):
    lanes = local.shape[1]
    value = local[...]
    value = jnp.concatenate([value[0:16] + below[...], value[16:48], value[48:64] + above[...]])
    value = assemble_coarse(value) / scale[...]
    high, low = halves(value)
    pack[0, 0:64] = high
    pack[0, 64:128] = low
    pack[0, 128:192] = high
    for at, i in enumerate((0, 1, 6, 7)):
        correct(i, slice(at * 64, at * 64 + 64), coef, prolong, pack, field, out)
    up[...] = out[128:256]
    down[...] = out[0:128]


def coarse_inner_kernel(pack, coef, prolong, total_inner, total_outer, field, sum_inner, sum_outer, out):
    for at, i in enumerate((2, 3, 4, 5)):
        correct(i, slice(at * 64, at * 64 + 64), coef, prolong, pack, field, out)
    for start, stop in chunks(pack.shape[2]):
        for i in range(PTS):
            value = dot(prolong[i * 64 : i * 64 + 64], pack[0, :, start:stop])
            if i in (0, 7):
                at = slice(i // 7 * 64, i // 7 * 64 + 64)
                sum_outer[at, start:stop] = total_outer[at, start:stop] + value
            else:
                at = slice(i * 64 - 64, i * 64)
                sum_inner[at, start:stop] = total_inner[at, start:stop] + value


def correct(i, to, coef, prolong, pack, field, out):
    here = slice(i * 64, i * 64 + 64)
    for start, stop in chunks(pack.shape[2]):
        sides = (8, PTS, stop - start)
        value = 0.0
        for n in range(3):
            rows = slice((n + 1) * 512 + i * 64, (n + 1) * 512 + i * 64 + 64)
            term = dot(prolong[rows], pack[0, :, start:stop]).reshape(sides)
            value = value + term * coef[n * PTS : (n + 1) * PTS, start:stop]
        out[to, start:stop] = field[here, start:stop] - value.reshape(64, stop - start)


def finish_inner_kernel(rot, local, total_inner, total_outer, sol, res, ext):
    tiles = local.shape[1] // TILE
    for i in range(6):
        store(ext, slice(i * 64, i * 64 + 64), local[i * 64 + 64 : i * 64 + 128])
    assemble_sides(ext, range(6), tiles)
    for case in range(4):

        @pl.when(rot[0] == case)
        def _(case=case):
            start = (LEFT + case - RINGS[0][0]) * RADIAL
            for plane in range(PTS):
                here = slice(plane * 64, plane * 64 + 64)
                if plane in (0, 7):
                    at = plane // 7 * 64
                    sol[here] = total_outer[at : at + 64, start : start + OWN]
                else:
                    before = slice(plane * 64 - 64, plane * 64)
                    sol[here] = total_inner[before, start : start + OWN]
                    res[before] = load(ext, before, tiles)[:, start : start + OWN]


def finish_outer_kernel(rot, local, below, above, inner, res, ext):
    tiles = local.shape[1] // TILE
    store(ext, slice(0, 64), local[0:64] + below[...])
    store(ext, slice(64, 128), local[448:512] + above[...])
    assemble_sides(ext, range(2), tiles)
    res[64:448] = inner[...]
    for case in range(4):

        @pl.when(rot[0] == case)
        def _(case=case):
            start = (LEFT + case - RINGS[0][0]) * RADIAL
            res[0:64] = load(ext, slice(0, 64), tiles)[:, start : start + OWN]
            res[448:512] = load(ext, slice(64, 128), tiles)[:, start : start + OWN]


def call(kernel, name, args, outs, scratch=(), scalars=0, flops=0, untouched=0):
    spaces = [pltpu.SMEM] * scalars + [pl.ANY] * untouched
    spaces += [pltpu.VMEM] * (len(args) - len(spaces))
    in_specs = [pl.BlockSpec(memory_space=space) for space in spaces]
    return pl.pallas_call(
        kernel,
        out_shape=[
            jax.ShapeDtypeStruct(out, jnp.float32 if len(out) == 2 else jnp.bfloat16) for out in outs
        ],
        in_specs=in_specs,
        out_specs=[pl.BlockSpec(memory_space=pltpu.VMEM) for _ in outs],
        scratch_shapes=list(scratch),
        name=name,
        cost_estimate=pl.CostEstimate(flops=flops, bytes_accessed=4_000_000, transcendentals=0),
        compiler_params=pltpu.CompilerParams(vmem_limit_bytes=20 * 1024 * 1024),
    )(*args)


def per_device(rhs, spacing_z, spacing_a, spacing_b, rotation):
    mats = matrices()
    group = lax.axis_index("grp")
    member = lax.axis_index("sub")
    groups = lax.axis_size("grp")
    members = lax.axis_size("sub")
    wide, narrow = jnp.float32, jnp.bfloat16
    vmem = pltpu.VMEM

    def shifted(value, axis, count, steps):
        return lax.ppermute(value, axis, [(n, (n + steps) % count) for n in range(count)])

    def neighbours(up, down):
        return shifted(up, "grp", groups, 1), shifted(down, "grp", groups, -1)

    def beside(value):
        return shifted(value, "sub", members, 1), shifted(value, "sub", members, -1)

    def shapes(tiles, *rows):
        return tuple((count, tiles * TILE) for count in rows)

    own = rhs.reshape(512, OWN)
    ends = jnp.concatenate([own[0:128], own[384:512]])
    left, right = beside(ends)
    rot = lax.dynamic_slice(rotation, (group,), (1,))
    ring = jnp.concatenate([spacing_a, spacing_a, spacing_a])
    columns = lax.dynamic_slice(ring, (spacing_a.shape[0] + member * COLS_DEV - LEFT,), (WIN,))
    columns = jnp.concatenate([columns[start:stop] for start, stop in RINGS])
    geo = jnp.stack(
        [
            jnp.repeat(columns, RADIAL),
            jnp.tile(spacing_b, WIN),
            jnp.broadcast_to(spacing_z, (LANES,)),
        ]
    )
    geo = jnp.concatenate([geo, jnp.ones((5, LANES), wide)])
    lam, coef, middle = call(
        tables_kernel,
        "tables",
        (rot, geo, mats["modes"], own),
        ((4 * MODES, LANES), (24, LANES), (256, OWN)),
        scalars=1,
    )
    (middle,) = call(follow_kernel, "follow", (left, right, middle), ((256, OWN),), untouched=2)
    near, far = beside(middle)
    outer, up, down = call(
        outer_kernel,
        "outer",
        (rot, left, ends, right, geo),
        ((256, LANES), (136, LANES), (136, LANES)),
        scalars=1,
    )
    lower, upper = neighbours(up, down)
    (inner,) = call(
        inner_kernel, "inner", (rot, near, middle, far), ((256, LANES),), scalars=1, flops=EARLY
    )

    def solve(fields, below, above, before, tiles):
        lanes = tiles * TILE
        start_up = len(fields) == 2
        share_inner, spectrum = call(
            functools.partial(solve_inner_kernel, start_up, before, tiles),
            "solve_inner",
            (*fields, mats["forward_inner"]),
            shapes(tiles, 384, 4 * MODES),
            (
                vmem((before, 384, TILE), wide),
                vmem((4 * tiles, INNER, TILE), wide),
                vmem((4, 3 * INNER, lanes), narrow),
            ),
        )
        share_outer, modes, up, down = call(
            functools.partial(solve_outer_kernel, start_up, before, tiles),
            "solve_outer",
            (fields[0], below, above, spectrum, lam, mats["forward_outer"], *mats["backward_outer"]),
            (*shapes(tiles, 128), (4, 2 * MODES, lanes), *shapes(tiles, 64, 64)),
            (
                vmem((before, 256, TILE), wide),
                vmem((4 * tiles, 128, TILE), wide),
                vmem((4, 3 * OUTER, lanes), narrow),
            ),
        )
        return (share_inner, share_outer), (modes, up, down), neighbours(up, down)

    def advance(kind, local, messages, share, before, total, width, tiles):
        lanes = tiles * TILE

        def scratch(rows, folded):
            return [
                vmem((width, rows, TILE), wide),
                vmem((4 * width, 128, TILE), wide),
                vmem((4, folded, lanes), narrow),
            ]

        def pick(at):
            return [pair[at] for pair in (before, total) if pair is not None]

        kept = [count for count, used in ((1, kind in (0, 2)), (1, kind != 0)) if used]
        *inner, image = call(
            functools.partial(step_inner_kernel, kind, width, tiles),
            f"step{kind}_inner",
            (local[0], *pick(0), coef, mats["apply_inner"], *mats["backward_inner"]),
            shapes(tiles, *(384 for _ in kept), 512),
            scratch(384, 288),
        )
        sent = {0: 128, 1: 16, 2: 128, 3: 64}[kind]
        extra = scratch(128, 96)
        if kind == 1:
            extra.append(vmem((1024, lanes), narrow))
        out = call(
            functools.partial(step_outer_kernel, kind, width, tiles),
            f"step{kind}_outer",
            (
                *(local[1], messages[0], local[2], messages[1]),
                *(*pick(1), *share, image, coef, mats["apply_outer"]),
                *(mats["restrict"] if kind == 1 else ()),
            ),
            shapes(tiles, *(128 for _ in kept), 512, sent, sent, *((64,) if kind == 1 else ())),
            extra,
        )
        outer, (field, up, down, *coarse) = out[: len(kept)], out[len(kept) :]
        return list(zip(inner, outer)), field, neighbours(up, down), *coarse

    share, local, messages = solve((outer, inner), lower, upper, 5, 5)
    (step,), field, messages = advance(0, local, messages, share, None, None, 5, 5)
    share, local, messages = solve((field,), *messages, 5, 5)
    (total,), field, messages, coarse = advance(1, local, messages, share, step, step, 5, 4)
    (scale,) = call(diagonal_kernel, "diagonal", (lower, upper, geo, mats["coarse"]), shapes(4, 64))
    outer, terms, up, down = call(
        coarse_outer_kernel,
        "coarse_outer",
        (coarse, *messages, scale, coef, mats["prolong"], field),
        (*shapes(4, 256), (1, 192, 4 * TILE), *shapes(4, 128, 128)),
    )
    messages = neighbours(up, down)
    *total, inner = call(
        coarse_inner_kernel,
        "coarse_inner",
        (terms, coef, mats["prolong"], *total, field),
        shapes(4, 384, 128, 256),
    )
    share, local, messages = solve((outer, inner), *messages, 4, 4)
    (step, total), field, messages = advance(2, local, messages, share, None, total, 4, 4)
    share, local, messages = solve((field,), *messages, 4, 3)
    (total,), field, messages = advance(3, local, messages, share, step, total, 3, 3)
    sol, inner = call(
        finish_inner_kernel,
        "finish_inner",
        (rot, field, *total),
        ((512, OWN), (384, OWN)),
        (vmem((3, 384, TILE), wide),),
        scalars=1,
    )
    (res,) = call(
        finish_outer_kernel,
        "finish_outer",
        (rot, field, *messages, inner),
        ((512, OWN),),
        (vmem((3, 128, TILE), wide),),
        scalars=1,
    )
    return sol.reshape(rhs.shape), res.reshape(rhs.shape)


def solution(mesh):
    return jax.shard_map(
        per_device,
        mesh=mesh,
        in_specs=(P(None, None, None, ("grp", "sub")), P("grp"), P(), P(), P()),
        out_specs=(P(None, None, None, ("grp", "sub")), P(None, None, None, ("grp", "sub"))),
        check_vma=False,
    )
```

```python
import functools

import jax
import jax.numpy as jnp
import ml_dtypes
import numpy as np
from jax import lax
from jax.experimental import pallas as pl
from jax.experimental.pallas import tpu as pltpu
from jax.sharding import PartitionSpec as P

PTS = 8
CPTS = 4
COLS_DEV = 16
RADIAL = 16
SMOOTH = 2

WIN = 40
LEFT = 10
LANES = WIN * RADIAL
RINGS = ((8, 32), (4, 8), (32, 36), (0, 4), (36, 40))
OWN = COLS_DEV * RADIAL
CLASSES = ((0, 0), (0, 1), (1, 0), (1, 1))
INNER = 160
OUTER = 80
MODES = 256
TILE = 128
TILES = LANES // TILE
TERMS = 32
BATCH = 4
EARLY = 20_000_000_000

cheb_upper = 2.0
cheb_ratio = 0.1
theta = 0.5 * (cheb_upper + cheb_upper * cheb_ratio)
delta = 0.5 * (cheb_upper - cheb_upper * cheb_ratio)
sigma = theta / delta
rho_first = 1.0 / sigma
rho_second = 1.0 / (2.0 * sigma - rho_first)


def legendre_rows(gll_nodes, poly_order):
    values = np.zeros((gll_nodes.size, poly_order + 1))
    values[:, 0] = 1.0
    values[:, 1] = gll_nodes
    for degree in range(2, poly_order + 1):
        values[:, degree] = (
            (2 * degree - 1) * gll_nodes * values[:, degree - 1]
            - (degree - 1) * values[:, degree - 2]
        ) / degree
    return values


def jacobi_eigen(matrix):
    order = matrix.shape[0]
    current = matrix.copy()
    vectors = np.eye(order)
    for sweep in range(12):
        for first in range(order - 1):
            for second in range(first + 1, order):
                off_value = current[first, second]
                spread = current[second, second] - current[first, first]
                sense = np.where(spread >= 0.0, 1.0, -1.0)
                denom = spread + sense * np.sqrt(spread * spread + 4.0 * off_value * off_value)
                denom = np.where(denom == 0.0, 1.0, denom)
                tangent = 2.0 * off_value / denom
                cosine = 1.0 / np.sqrt(1.0 + tangent * tangent)
                sine = tangent * cosine
                rotate = np.eye(order)
                rotate[first, first] = cosine
                rotate[second, second] = cosine
                rotate[first, second] = sine
                rotate[second, first] = -sine
                current = rotate.T @ current @ rotate
                vectors = vectors @ rotate
    diag_ids = np.arange(order)
    return (current[diag_ids, diag_ids].copy(), vectors)


def lobatto(poly_order):
    gll_nodes = np.cos(np.pi * np.arange(poly_order + 1) / poly_order)
    for newton in range(100):
        values = legendre_rows(gll_nodes, poly_order)
        gll_nodes = gll_nodes - (gll_nodes * values[:, poly_order] - values[:, poly_order - 1]) / (
            (poly_order + 1) * values[:, poly_order]
        )
    values = legendre_rows(gll_nodes, poly_order)
    gll_nodes = gll_nodes[::-1].copy()
    top_poly = values[::-1, poly_order].copy()
    weights = 2.0 / (poly_order * (poly_order + 1) * top_poly**2)
    derivative = np.zeros((poly_order + 1, poly_order + 1))
    for row_index in range(poly_order + 1):
        for col_index in range(poly_order + 1):
            if row_index != col_index:
                derivative[row_index, col_index] = top_poly[row_index] / (
                    top_poly[col_index] * (gll_nodes[row_index] - gll_nodes[col_index])
                )
    derivative[0, 0] = -poly_order * (poly_order + 1) / 4.0
    derivative[poly_order, poly_order] = poly_order * (poly_order + 1) / 4.0
    stiffness = derivative.T @ (weights[:, None] * derivative)
    return (gll_nodes, weights, stiffness)


def element_tables():
    fine_nodes, fine_weights, fine_stiff = lobatto(PTS - 1)
    coarse_nodes, coarse_weights, coarse_stiff = lobatto(CPTS - 1)
    interp = np.ones((PTS, CPTS))
    for target_col in range(CPTS):
        for other_col in range(CPTS):
            if other_col != target_col:
                interp[:, target_col] *= (fine_nodes - coarse_nodes[other_col]) / (
                    coarse_nodes[target_col] - coarse_nodes[other_col]
                )
    poly_order = PTS - 1
    node_count = 3 * poly_order + 1
    joined_stiff = np.zeros((node_count, node_count))
    joined_mass = np.zeros(node_count)
    for piece_index in range(3):
        first_node = piece_index * poly_order
        joined_stiff[first_node : first_node + PTS, first_node : first_node + PTS] += fine_stiff
        joined_mass[first_node : first_node + PTS] += fine_weights
    kept = slice(poly_order - 1, 2 * poly_order + 2)
    root_mass = np.sqrt(joined_mass[kept])
    eigen_values, eigen_vectors = jacobi_eigen(
        joined_stiff[kept, kept] / root_mass[:, None] / root_mass[None, :]
    )
    eigen_basis = eigen_vectors / root_mass[:, None]
    coarse_diag = np.diag(coarse_stiff).copy()
    return fine_stiff, fine_weights, eigen_basis, eigen_values, interp, coarse_diag, coarse_weights


def split(table):
    high = table.astype(np.float32).astype(ml_dtypes.bfloat16)
    low = (table - high.astype(np.float64)).astype(np.float32).astype(ml_dtypes.bfloat16)
    return high, low


def kron3(first, second, third):
    return np.kron(first, np.kron(second, third))


def spread(values):
    terms = np.zeros((values.shape[0], TERMS), ml_dtypes.bfloat16)
    for at in range(3):
        high, rest = split(values[:, at])
        middle, low = split(values[:, at] - high.astype(np.float64))
        for n, part in enumerate((high, high, high, middle, middle, low)):
            terms[:, at * 6 + n] = part
    return terms


def matrices():
    stiff, weights, basis, values, interp, coarse_diag, coarse_weights = element_tables()
    parts = ([], [])
    for mode in range(PTS + 2):
        column = basis[:, mode]
        odd = np.abs(column + column[::-1]).sum() < np.abs(column - column[::-1]).sum()
        parts[int(odd)].append(mode)
    signs = (1.0, -1.0)
    pure = basis.copy()
    for parity in (0, 1):
        for mode in parts[parity]:
            pure[:, mode] = 0.5 * (basis[:, mode] + signs[parity] * basis[::-1, mode])
    center = pure[1:-1, :]
    edges = pure[[0, -1], :]

    def folded(matrix, parity):
        half = PTS // 2
        return 0.5 * (matrix[:half, :half] + signs[parity] * matrix[:half, ::-1][:, :half])

    mass = np.diag(weights)
    halved = np.ones(PTS // 2)
    halved[0] = 0.5
    forward_inner = np.zeros((4, MODES, INNER))
    forward_outer = np.zeros((4, MODES, OUTER))
    backward = np.zeros((4, PTS * 16, MODES))
    apply_inner = np.zeros((4, 320, 96))
    apply_outer = np.zeros((4, 192, 32))
    mode_values = np.ones((4, MODES, 3))
    for at, (pi, pk) in enumerate(CLASSES):
        ci, ck = center[:4, parts[pi]], center[:4, parts[pk]]
        ei, ek = edges[:1, parts[pi]], edges[:1, parts[pk]]
        count = len(parts[pi]) * len(parts[pk]) * (PTS + 2)
        rest = ci[1:]
        gap = lambda rows: np.zeros((rows, count))
        columns = [kron3(rest, ck, center), kron3(rest, ek, center), gap(8)]
        columns += [kron3(rest, ck, edges[:1]), gap(4), kron3(rest, ck, edges[1:]), gap(4)]
        forward_inner[at, :count] = np.concatenate(columns, axis=0).T
        columns = [kron3(ci[:1], ck, center), kron3(ei, ck, center), kron3(ci[:1], ek, center)]
        columns += [kron3(ci[:1], ck, edges[:1]), kron3(ci[:1], ck, edges[1:])]
        forward_outer[at, :count] = np.concatenate(columns, axis=0).T
        backward[at, :, :count] = kron3(halved[:, None] * ci, halved[:, None] * ck, center)
        vi, vk = values[parts[pi]], values[parts[pk]]
        ones = np.ones
        mode_values[at, :count, 0] = kron3(vi, ones(len(vk)), ones(PTS + 2))
        mode_values[at, :count, 1] = kron3(ones(len(vi)), vk, ones(PTS + 2))
        mode_values[at, :count, 2] = kron3(ones(len(vi)), ones(len(vk)), values)
        si, sk = folded(stiff, pi), folded(stiff, pk)
        mi, mk = folded(mass, pi), folded(mass, pk)
        along_z, along_a, along_b = kron3(si, mk, mass), kron3(mi, sk, mass), kron3(mi, mk, stiff)
        apply_inner[at] = np.concatenate([along_z[:, 32:], along_a[32:, 32:], along_b[32:, 32:]])
        apply_outer[at] = np.concatenate([along_z[:, :32], along_a[:32, :32], along_b[:32, :32]])
    mass_up, stiff_up = mass @ interp, stiff @ interp
    prolong = np.concatenate(
        [
            kron3(interp, interp, interp),
            kron3(stiff_up, mass_up, mass_up),
            kron3(mass_up, stiff_up, mass_up),
            kron3(mass_up, mass_up, stiff_up),
        ],
        axis=0,
    )
    restrict = kron3(interp.T, interp.T, interp.T)
    coarse = np.zeros((CPTS**3, 8))
    coarse[:, 0] = kron3(coarse_diag, coarse_weights, coarse_weights)
    coarse[:, 1] = kron3(coarse_weights, coarse_diag, coarse_weights)
    coarse[:, 2] = kron3(coarse_weights, coarse_weights, coarse_diag)

    def pair(table):
        high, low = split(table)
        return jnp.asarray(np.concatenate([high, high], axis=-1)), jnp.asarray(low)

    def triple(table):
        high, low = split(table)
        return jnp.asarray(np.concatenate([high, high, low], axis=-1))

    return {
        "forward_inner": triple(forward_inner),
        "forward_outer": triple(forward_outer),
        "backward_outer": pair(backward[:, :32]),
        "backward_inner": pair(backward[:, 32:]),
        "apply_inner": triple(apply_inner),
        "apply_outer": triple(apply_outer),
        "restrict": pair(restrict),
        "prolong": triple(prolong),
        "modes": jnp.asarray(spread(mode_values.reshape(4 * MODES, 3))),
        "coarse": jnp.asarray(coarse.astype(np.float32)),
    }


def halves(value):
    high = value.astype(jnp.bfloat16)
    low = (value - high.astype(jnp.float32)).astype(jnp.bfloat16)
    return high, low


def dot(left, right):
    return jnp.dot(left, right, preferred_element_type=jnp.float32)


def sided(rot, off, near):
    odd = rot[1] == 1
    return jnp.where(odd, near, off), jnp.where(odd, off, near)


def send(rot, off, near, up, down):
    odd = rot[1] == 1
    off[...] = jnp.where(odd, up, down)
    near[...] = jnp.where(odd, down, up)


def join(tiles):
    return jnp.concatenate(tiles, axis=1)


def tiles_of(value):
    return [value[:, t * TILE : (t + 1) * TILE] for t in range(value.shape[1] // TILE)]


def radial_turn(value, steps):
    return join([pltpu.roll(tile, steps % TILE, axis=1) for tile in tiles_of(value)])


def column_turn(value, direction):
    tiles = tiles_of(value)
    count = len(tiles)
    lane = lax.broadcasted_iota(jnp.int32, tiles[0].shape, 1)
    near = [pltpu.roll(tile, (direction * RADIAL) % TILE, axis=1) for tile in tiles]
    far = lambda at: pltpu.roll(tiles[at], (TILE // 2 + direction * RADIAL) % TILE, axis=1)
    out = list(near)
    if direction < 0:
        high_end, low_end = lane >= TILE - RADIAL, (lane >= TILE // 2 - RADIAL) & (lane < TILE // 2)
        out[0] = jnp.where(high_end, near[1], near[0])
        out[1] = jnp.where(high_end, near[2], near[1])
        inner, outer, middle = 2, high_end, low_end
        edge = 0
    else:
        high_end, low_end = lane < RADIAL, (lane >= TILE // 2) & (lane < TILE // 2 + RADIAL)
        out[1] = jnp.where(high_end, near[0], near[1])
        out[2] = jnp.where(high_end, near[1], near[2])
        inner, outer, middle = 0, high_end, low_end
        edge = 2
    if count > 3:
        first_ring = far(3)
        out[inner] = jnp.where(outer, first_ring, out[inner])
        out[3] = jnp.where(middle, far(edge), near[3])
    if count > 4:
        out[3] = jnp.where(outer, far(4), out[3])
        out[4] = jnp.where(middle, first_ring, near[4])
    return join(out)


def lane_masks(rows, lanes):
    radial = lax.broadcasted_iota(jnp.int32, (rows, lanes), 1) % RADIAL
    keep_upper = (radial < RADIAL - 1).astype(jnp.float32)
    keep_lower = (radial > 0).astype(jnp.float32)
    return keep_upper, keep_lower


def chunks(lanes):
    return [(start, min(start + 2 * TILE, lanes)) for start in range(0, lanes, 2 * TILE)]


def point_factor(lanes):
    point = lax.broadcasted_iota(jnp.int32, (PTS, lanes), 0)
    radial = lax.broadcasted_iota(jnp.int32, (PTS, lanes), 1) % RADIAL
    shared = ((point == 0) & (radial > 0)) | ((point == PTS - 1) & (radial < RADIAL - 1))
    return jnp.where(shared, 0.5, 1.0)


def side_factor(i, k):
    return (0.5 if i in (0, PTS - 1) else 1.0) * (0.5 if k in (0, PTS - 1) else 1.0)


def plane_factor(factor, i):
    return jnp.concatenate([factor * side_factor(i, k) for k in range(PTS)])


def block(plane, k):
    start = plane * 64 + k * PTS
    return slice(start, start + PTS)


def load(ref, rows, tiles, base=0):
    return join([ref[base + t, rows, :] for t in range(tiles)])


def store(ref, rows, value, base=0):
    for t, tile in enumerate(tiles_of(value)):
        ref[base + t, rows, :] = tile


def assemble_sides(field, planes, tiles):
    batches = [planes[start : start + BATCH] for start in range(0, len(planes), BATCH)]
    for batch in batches:
        left = jnp.concatenate([load(field, block(plane, 0), tiles) for plane in batch])
        right = jnp.concatenate([load(field, block(plane, PTS - 1), tiles) for plane in batch])
        new_right = right + column_turn(left, -1)
        new_left = left + column_turn(right, 1)
        for at, plane in enumerate(batch):
            store(field, block(plane, PTS - 1), new_right[at * PTS : (at + 1) * PTS])
            store(field, block(plane, 0), new_left[at * PTS : (at + 1) * PTS])
    keep_upper, keep_lower = lane_masks(PTS * BATCH, tiles * TILE)
    for batch in batches:
        rows = len(batch) * PTS
        inner_at = [pl.ds(plane * 64, PTS, stride=PTS) for plane in batch]
        outer_at = [pl.ds(plane * 64 + PTS - 1, PTS, stride=PTS) for plane in batch]
        inner = jnp.concatenate([load(field, at, tiles) for at in inner_at])
        outer = jnp.concatenate([load(field, at, tiles) for at in outer_at])
        new_outer = outer + radial_turn(inner, -1) * keep_upper[:rows]
        new_inner = inner + radial_turn(outer, 1) * keep_lower[:rows]
        for at in range(len(batch)):
            store(field, outer_at[at], new_outer[at * PTS : (at + 1) * PTS])
            store(field, inner_at[at], new_inner[at * PTS : (at + 1) * PTS])


def fold(a, b, c, d):
    sum_k, diff_k = a + b, a - b
    sum_m, diff_m = c + d, c - d
    return sum_k + sum_m, sum_k - sum_m, diff_k + diff_m, diff_k - diff_m


def each_class(body, rolled):
    if rolled:

        def step(c, carry):
            body(c)
            return carry

        lax.fori_loop(0, 4, step, 0)
    else:
        for c in range(4):
            body(c)


def class_rows(c, rows):
    return slice(c * rows, (c + 1) * rows) if isinstance(c, int) else pl.ds(pl.multiple_of(c * rows, rows), rows)


def pack(parts, packed, rows, tiles, rolled=False):
    def body(c):
        for t in range(tiles):
            lanes = slice(t * TILE, (t + 1) * TILE)
            high, low = halves(parts[c * tiles + t, 0:rows, :])
            packed[c, 0:rows, lanes] = high
            packed[c, rows : 2 * rows, lanes] = low
            packed[c, 2 * rows : 3 * rows, lanes] = high

    each_class(body, rolled)


def unfold(ss, sa, as_, aa):
    sum_k, sum_m = ss + sa, ss - sa
    diff_k, diff_m = as_ + aa, as_ - aa
    return sum_k + diff_k, sum_k - diff_k, sum_m + diff_m, sum_m - diff_m


def mirrored(i, k):
    return (i, k), (PTS - 1 - i, k), (i, PTS - 1 - k), (PTS - 1 - i, PTS - 1 - k)


def coefficient_terms(values):
    rows = []
    for value in values:
        parts = []
        for _ in range(3):
            part = value.astype(jnp.bfloat16).astype(jnp.float32)
            parts.append(part)
            value = value - part
        high, middle, low = parts
        rows += [high, middle, low, high, middle, high]
    rows.append(jnp.zeros((TERMS - len(rows), value.shape[1]), jnp.float32))
    return jnp.concatenate(rows).astype(jnp.bfloat16)


def tables_kernel(rot, geo, modes, own, lam, coef, middle):
    middle[...] = own[128:384]
    la, lb, lz = (geo[n : n + 1] for n in range(3))
    cz = la * lb / (2.0 * lz)
    ca = lz * lb / (2.0 * la)
    cb = lz * la / (2.0 * lb)
    for at, value in enumerate((cz, ca, cb)):
        coef[at * PTS : (at + 1) * PTS] = jnp.broadcast_to(value, (PTS, LANES))
    terms = coefficient_terms((cz, ca, cb))
    for start, stop in chunks(LANES):
        for c in range(4):
            here = slice(c * MODES, (c + 1) * MODES)
            lam[here, start:stop] = 1.0 / dot(modes[here], terms[:, start:stop])


def window(case, left, own, right, rows):
    shift = (COLS_DEV - LEFT - case) * RADIAL
    joined = join([left[rows], own, right[rows]])
    joined = pltpu.roll(joined, joined.shape[1] - shift, axis=1)[:, :LANES]
    first, *center, last = tiles_of(joined)
    lane = lax.broadcasted_iota(jnp.int32, first.shape, 1)
    half = TILE // 2
    near = jnp.where(lane < half, pltpu.roll(first, half, axis=1), pltpu.roll(last, half, axis=1))
    return join([*center, near, jnp.where(lane < half, first, last)])


def outer_kernel(rot, left, own, right, geo, field, up, down):
    factor = point_factor(LANES)
    for case in range(4):

        @pl.when(rot[0] == case)
        def _(case=case):
            for at, i in enumerate((0, 1, 6, 7)):
                here = slice(at * 64, at * 64 + 64)
                value = window(case, left, own[here], right, here)
                field[here] = value * plane_factor(factor, i)

    length = jnp.broadcast_to(geo[2:3], (PTS, LANES))
    send(rot, up, down, jnp.concatenate([field[128:256], length]), jnp.concatenate([field[0:128], length]))


def follow_kernel(left, right, own, inner):
    inner[...] = own[...]


def inner_kernel(rot, left, own, right, field):
    factor = point_factor(LANES)
    for case in range(4):

        @pl.when(rot[0] == case)
        def _(case=case):
            for at, i in enumerate((2, 3, 4, 5)):
                here = slice(at * 64, at * 64 + 64)
                field[here] = window(case, left, own[here], right, here) * plane_factor(factor, i)


def put(parts, tiles, at, values):
    for c in range(4):
        store(parts, at, values[c], c * tiles)


def layer(value, at):
    return value[at * PTS : (at + 1) * PTS]


def column_halos(field, planes, wide, lanes):
    before = jnp.concatenate([load(field, block(plane, PTS - 2), wide) for plane in planes])
    after = jnp.concatenate([load(field, block(plane, 1), wide) for plane in planes])
    return column_turn(before, 1)[:, :lanes], column_turn(after, -1)[:, :lanes]


def radial_halos(parts, tiles, count):
    masks = lane_masks(4 * count, tiles * TILE)
    found = []
    for first, steps, keep in ((PTS - 2, 1, masks[1]), (1, -1, masks[0])):
        rows = pl.ds(first, count, stride=PTS)
        values = [load(parts, rows, tiles, c * tiles) for c in range(4)]
        values = radial_turn(jnp.concatenate(values), steps) * keep
        found.append([values[c * count : (c + 1) * count] for c in range(4)])
    return found


def solve_inner_kernel(start_up, wide, tiles, *refs):
    if start_up:
        outer, inner, *refs = refs
        planes = [outer[64:128]] + [inner[i * 64 : i * 64 + 64] for i in range(4)] + [outer[128:192]]
    else:
        field, *refs = refs
        planes = [field[i * 64 : i * 64 + 64] for i in range(1, 7)]
    fwd, share, spectrum, ext, parts, packed = refs
    lanes = tiles * TILE
    factor = point_factor(lanes)
    for at, plane in enumerate(planes):
        store(ext, slice(at * 64, at * 64 + 64), plane)
    assemble_sides(ext, range(6), wide)
    for at in range(6):
        here = slice(at * 64, at * 64 + 64)
        share[here] = load(ext, here, tiles) * plane_factor(factor, at + 1)
    for i in range(3):
        for k in range(4):
            corners = ((i, k), (5 - i, k), (i, 7 - k), (5 - i, 7 - k))
            values = fold(*(load(ext, block(p, q), tiles) for p, q in corners))
            put(parts, tiles, block(0, i * 4 + k), values)
    before, after = column_halos(ext, range(6), wide, lanes)
    for i in range(3):
        values = fold(layer(before, i), layer(before, 5 - i), layer(after, i), layer(after, 5 - i))
        put(parts, tiles, slice(96 + i * 8, 104 + i * 8), values)
    put(parts, tiles, slice(120, 128), [jnp.zeros((PTS, lanes), jnp.float32)] * 4)
    lower, upper = radial_halos(parts, tiles, 16)
    put(parts, tiles, slice(128, 144), lower)
    put(parts, tiles, slice(144, 160), upper)
    pack(parts, packed, INNER, tiles, True)

    def forward(c):
        for start, stop in chunks(lanes):
            spectrum[class_rows(c, MODES), start:stop] = dot(fwd[c], packed[c, :, start:stop])

    each_class(forward, True)


def solve_outer_kernel(start_up, wide, tiles, *refs):
    rot, field, off, near, spectrum, lam, fwd, bwd, bwd_low = refs[:9]
    share, modes, up, down, to_off, to_near, ext, parts, packed = refs[9:]
    below, above = sided(rot, off[0:128], near[0:128])
    odd = rot[1] == 1
    lanes = tiles * TILE
    factor = point_factor(lanes)
    last = 192 if start_up else 448
    store(ext, slice(0, 64), below[0:64])
    store(ext, slice(64, 128), field[0:64] + below[64:128])
    store(ext, slice(128, 192), field[last : last + 64] + above[0:64])
    store(ext, slice(192, 256), above[64:128])
    assemble_sides(ext, range(4), wide)
    share[0:64] = load(ext, slice(64, 128), tiles) * plane_factor(factor, 0)
    share[64:128] = load(ext, slice(128, 192), tiles) * plane_factor(factor, 7)
    for k in range(4):
        for at, (p, q) in enumerate(((1, 2), (0, 3))):
            corners = ((p, k), (q, k), (p, 7 - k), (q, 7 - k))
            values = fold(*(load(ext, block(*corner), tiles) for corner in corners))
            put(parts, tiles, block(0, at * 4 + k), values)
    before, after = column_halos(ext, (1, 2), wide, lanes)
    values = fold(layer(before, 0), layer(before, 1), layer(after, 0), layer(after, 1))
    put(parts, tiles, slice(64, 72), values)
    lower, upper = radial_halos(parts, tiles, 4)
    put(parts, tiles, slice(72, 80), [jnp.concatenate(pair) for pair in zip(lower, upper)])
    pack(parts, packed, OUTER, tiles)
    for c in range(4):
        for start, stop in chunks(lanes):
            here = slice(c * MODES, (c + 1) * MODES)
            value = dot(fwd[c], packed[c, :, start:stop]) + spectrum[here, start:stop]
            modes[c, 0:MODES, start:stop], modes[c, MODES:, start:stop] = halves(value * lam[here, start:stop])
    back(modes, bwd, bwd_low, parts, tiles, 32, False)
    for k in range(4):
        classes = (load(parts, block(0, k), tiles, c * tiles) for c in range(4))
        values = unfold(*classes)
        first, last, first_mirror, last_mirror = (value * factor for value in values)
        for q, low, high in ((k, first, last), (PTS - 1 - k, first_mirror, last_mirror)):
            here = block(0, q)
            down[here] = low
            up[here] = high
            to_off[here] = jnp.where(odd, high, low)
            to_near[here] = jnp.where(odd, low, high)


def back(modes, bwd, bwd_low, parts, tiles, rows, rolled):
    def body(c):
        for start, stop in chunks(tiles * TILE):
            value = dot(bwd[c], modes[c, :, start:stop])
            value = value + dot(bwd_low[c], modes[c, 0:MODES, start:stop])
            store(parts, slice(0, rows), value, c * tiles + start // TILE)

    each_class(body, rolled)


def stepped(kind, value, before):
    if kind in (0, 2):
        return value * (1.0 / theta)
    return before * (rho_second * rho_first) + value * (2.0 * rho_second / delta)


def step_inner_kernel(kind, wide, tiles, *refs):
    take = iter(refs)
    modes = next(take)
    before = next(take) if kind in (1, 3) else None
    total = next(take) if kind != 0 else None
    coef, app, bwd, bwd_low = (next(take) for _ in range(4))
    step = next(take) if kind in (0, 2) else None
    sum_out = next(take) if kind != 0 else None
    image, ext, parts, packed = take
    lanes = tiles * TILE
    factor = point_factor(wide * TILE)
    back(modes, bwd, bwd_low, parts, wide, 96, True)
    for i in range(3):
        for k in range(4):
            classes = (load(parts, block(0, i * 4 + k), wide, c * wide) for c in range(4))
            corners = ((i, k), (5 - i, k), (i, 7 - k), (5 - i, 7 - k))
            for corner, value in zip(corners, unfold(*classes)):
                store(ext, block(*corner), value * factor)
    assemble_sides(ext, range(6), wide)
    for i in range(6):
        here = slice(i * 64, i * 64 + 64)
        value = stepped(kind, load(ext, here, tiles), None if before is None else before[here, :lanes])
        if step is not None:
            step[here] = value
        if sum_out is not None:
            sum_out[here] = total[here, :lanes] + value
        store(ext, here, value)
    for i in range(3):
        for k in range(4):
            corners = ((i, k), (5 - i, k), (i, 7 - k), (5 - i, 7 - k))
            values = fold(*(load(ext, block(p, q), tiles) for p, q in corners))
            put(parts, tiles, block(0, i * 4 + k), values)
    pack(parts, packed, 96, tiles, True)

    def operate(c):
        for start, stop in chunks(lanes):
            terms = dot(app[c], packed[c, :, start:stop]).reshape(40, PTS, stop - start)
            value = terms[0:16] * coef[0:8, start:stop]
            sides = terms[16:28] * coef[8:16, start:stop] + terms[28:40] * coef[16:24, start:stop]
            value = jnp.concatenate([value[0:4], value[4:16] + sides])
            image[class_rows(c, 128), start:stop] = value.reshape(128, stop - start)

    each_class(operate, True)


def step_outer_kernel(kind, wide, tiles, *refs):
    take = iter(refs)
    rot, last, below, first, above = (next(take) for _ in range(5))
    below, above = sided(rot, below[...], above[...])
    before = next(take) if kind in (1, 3) else None
    total = next(take) if kind != 0 else None
    share_inner, share_outer, image, coef, app = (next(take) for _ in range(5))
    res, res_low = (next(take), next(take)) if kind == 1 else (None, None)
    step = next(take) if kind in (0, 2) else None
    sum_out = next(take) if kind != 0 else None
    field, up, down = next(take), next(take), next(take)
    coarse = next(take) if kind == 1 else None
    ext, parts, packed = next(take), next(take), next(take)
    split_field = next(take) if kind == 1 else None
    lanes = tiles * TILE
    store(ext, slice(0, 64), first[...] + below)
    store(ext, slice(64, 128), last[...] + above)
    assemble_sides(ext, range(2), wide)
    for at in range(2):
        here = slice(at * 64, at * 64 + 64)
        value = stepped(kind, load(ext, here, tiles), None if before is None else before[here, :lanes])
        if step is not None:
            step[here] = value
        if sum_out is not None:
            sum_out[here] = total[here, :lanes] + value
        store(ext, here, value)
    for k in range(4):
        corners = ((0, k), (1, k), (0, 7 - k), (1, 7 - k))
        values = fold(*(load(ext, block(p, q), tiles) for p, q in corners))
        put(parts, tiles, block(0, k), values)
    pack(parts, packed, 32, tiles)
    for c in range(4):
        for start, stop in chunks(lanes):
            terms = dot(app[c], packed[c, :, start:stop]).reshape(24, PTS, stop - start)
            value = terms[0:16] * coef[0:8, start:stop]
            sides = terms[16:20] * coef[8:16, start:stop] + terms[20:24] * coef[16:24, start:stop]
            value = jnp.concatenate([value[0:4] + sides, value[4:16]]).reshape(128, stop - start)
            value = value + image[c * 128 : (c + 1) * 128, start:stop]
            store(parts, slice(0, 128), value, c * tiles + start // TILE)
    for i in range(4):
        for k in range(4):
            classes = (load(parts, block(0, i * 4 + k), tiles, c * tiles) for c in range(4))
            for (p, q), value in zip(mirrored(i, k), unfold(*classes)):
                if p in (0, 7):
                    shared = share_outer[block(p // 7, q), :lanes]
                else:
                    shared = share_inner[block(p - 1, q), :lanes]
                field[block(p, q)] = shared - value
    if kind == 1:
        split_field[0:512], split_field[512:1024] = halves(field[...])
        for start, stop in chunks(lanes):
            value = dot(res[...], split_field[:, start:stop])
            coarse[:, start:stop] = value + dot(res_low[...], split_field[0:512, start:stop])
        send(rot, up, down, coarse[48:64], coarse[0:16])
    elif kind == 3:
        send(rot, up, down, field[448:512], field[0:64])
    else:
        send(rot, up, down, field[384:512], field[0:128])


def assemble_coarse(value):
    lanes = value.shape[1]
    row = lax.broadcasted_iota(jnp.int32, (64, lanes), 0)
    keep_upper, keep_lower = lane_masks(64, lanes)
    first = (row % 16) < 4
    last = (row % 16) >= 12
    over = pltpu.roll(column_turn(value, -1), 12, axis=0)
    under = pltpu.roll(column_turn(value, 1), 64 - 12, axis=0)
    value = value + jnp.where(last, over, 0.0) + jnp.where(first, under, 0.0)
    first = (row % 4) == 0
    last = (row % 4) == 3
    over = pltpu.roll(radial_turn(value, -1) * keep_upper, 3, axis=0)
    under = pltpu.roll(radial_turn(value, 1) * keep_lower, 64 - 3, axis=0)
    return value + jnp.where(last, over, 0.0) + jnp.where(first, under, 0.0)


def diagonal_kernel(rot, lower, upper, geo, table, scale):
    lanes = scale.shape[1]
    la, lb = geo[0:1, :lanes], geo[1:2, :lanes]

    def local(lz, rows):
        return (
            la * lb / (2.0 * lz) * table[rows, 0:1]
            + lz * lb / (2.0 * la) * table[rows, 1:2]
            + lz * la / (2.0 * lb) * table[rows, 2:3]
        )

    value = local(geo[2:3, :lanes], slice(0, 64))
    lz_below, lz_above = sided(rot, lower[128:129, :lanes], upper[128:129, :lanes])
    first = value[0:16] + local(lz_below, slice(48, 64))
    last = value[48:64] + local(lz_above, slice(0, 16))
    scale[...] = assemble_coarse(jnp.concatenate([first, value[16:48], last]))


def coarse_outer_kernel(rot, local, below, above, scale, coef, prolong, field, out, pack, up, down):
    lanes = local.shape[1]
    value = local[...]
    below, above = sided(rot, below[...], above[...])
    value = jnp.concatenate([value[0:16] + below, value[16:48], value[48:64] + above])
    value = assemble_coarse(value) / scale[...]
    high, low = halves(value)
    pack[0, 0:64] = high
    pack[0, 64:128] = low
    pack[0, 128:192] = high
    for at, i in enumerate((0, 1, 6, 7)):
        correct(i, slice(at * 64, at * 64 + 64), coef, prolong, pack, field, out)
    send(rot, up, down, out[128:256], out[0:128])


def coarse_inner_kernel(pack, coef, prolong, total_inner, total_outer, field, sum_inner, sum_outer, out):
    for at, i in enumerate((2, 3, 4, 5)):
        correct(i, slice(at * 64, at * 64 + 64), coef, prolong, pack, field, out)
    for start, stop in chunks(pack.shape[2]):
        for i in range(PTS):
            value = dot(prolong[i * 64 : i * 64 + 64], pack[0, :, start:stop])
            if i in (0, 7):
                at = slice(i // 7 * 64, i // 7 * 64 + 64)
                sum_outer[at, start:stop] = total_outer[at, start:stop] + value
            else:
                at = slice(i * 64 - 64, i * 64)
                sum_inner[at, start:stop] = total_inner[at, start:stop] + value


def correct(i, to, coef, prolong, pack, field, out):
    here = slice(i * 64, i * 64 + 64)
    for start, stop in chunks(pack.shape[2]):
        sides = (8, PTS, stop - start)
        value = 0.0
        for n in range(3):
            rows = slice((n + 1) * 512 + i * 64, (n + 1) * 512 + i * 64 + 64)
            term = dot(prolong[rows], pack[0, :, start:stop]).reshape(sides)
            value = value + term * coef[n * PTS : (n + 1) * PTS, start:stop]
        out[to, start:stop] = field[here, start:stop] - value.reshape(64, stop - start)


def finish_inner_kernel(rot, local, total_inner, total_outer, sol, res, ext):
    tiles = local.shape[1] // TILE
    for i in range(6):
        store(ext, slice(i * 64, i * 64 + 64), local[i * 64 + 64 : i * 64 + 128])
    assemble_sides(ext, range(6), tiles)
    for case in range(4):

        @pl.when(rot[0] == case)
        def _(case=case):
            start = (LEFT + case - RINGS[0][0]) * RADIAL
            for plane in range(PTS):
                here = slice(plane * 64, plane * 64 + 64)
                if plane in (0, 7):
                    at = plane // 7 * 64
                    sol[here] = total_outer[at : at + 64, start : start + OWN]
                else:
                    before = slice(plane * 64 - 64, plane * 64)
                    sol[here] = total_inner[before, start : start + OWN]
                    res[before] = load(ext, before, tiles)[:, start : start + OWN]


def finish_outer_kernel(rot, local, below, above, inner, res, ext):
    tiles = local.shape[1] // TILE
    below, above = sided(rot, below[...], above[...])
    store(ext, slice(0, 64), local[0:64] + below)
    store(ext, slice(64, 128), local[448:512] + above)
    assemble_sides(ext, range(2), tiles)
    res[64:448] = inner[...]
    for case in range(4):

        @pl.when(rot[0] == case)
        def _(case=case):
            start = (LEFT + case - RINGS[0][0]) * RADIAL
            res[0:64] = load(ext, slice(0, 64), tiles)[:, start : start + OWN]
            res[448:512] = load(ext, slice(64, 128), tiles)[:, start : start + OWN]


def call(kernel, name, args, outs, scratch=(), scalars=0, flops=0, untouched=0):
    spaces = [pltpu.SMEM] * scalars + [pl.ANY] * untouched
    spaces += [pltpu.VMEM] * (len(args) - len(spaces))
    in_specs = [pl.BlockSpec(memory_space=space) for space in spaces]
    return pl.pallas_call(
        kernel,
        out_shape=[
            jax.ShapeDtypeStruct(out, jnp.float32 if len(out) == 2 else jnp.bfloat16) for out in outs
        ],
        in_specs=in_specs,
        out_specs=[pl.BlockSpec(memory_space=pltpu.VMEM) for _ in outs],
        scratch_shapes=list(scratch),
        name=name,
        cost_estimate=pl.CostEstimate(flops=flops, bytes_accessed=4_000_000, transcendentals=0),
        compiler_params=pltpu.CompilerParams(vmem_limit_bytes=20 * 1024 * 1024),
    )(*args)


def per_device(rhs, spacing_z, spacing_a, spacing_b, rotation):
    mats = matrices()
    group = lax.axis_index("grp")
    member = lax.axis_index("sub")
    groups = lax.axis_size("grp")
    members = lax.axis_size("sub")
    wide, narrow = jnp.float32, jnp.bfloat16
    vmem = pltpu.VMEM

    def shifted(value, axis, count, steps):
        return lax.ppermute(value, axis, [(n, (n + steps) % count) for n in range(count)])

    swap_off = [(n, (n + 1) % groups if n % 2 else (n - 1) % groups) for n in range(groups)]
    swap_near = [(n, n - 1 if n % 2 else n + 1) for n in range(groups)]

    def neighbours(off, near):
        return lax.ppermute(off, "grp", swap_off), lax.ppermute(near, "grp", swap_near)

    def beside(value):
        return shifted(value, "sub", members, 1), shifted(value, "sub", members, -1)

    def shapes(tiles, *rows):
        return tuple((count, tiles * TILE) for count in rows)

    own = rhs.reshape(512, OWN)
    ends = jnp.concatenate([own[0:128], own[384:512]])
    left, right = beside(ends)
    rot = jnp.concatenate([lax.dynamic_slice(rotation, (group,), (1,)), jnp.reshape(group % 2, (1,))])
    ring = jnp.concatenate([spacing_a, spacing_a, spacing_a])
    columns = lax.dynamic_slice(ring, (spacing_a.shape[0] + member * COLS_DEV - LEFT,), (WIN,))
    columns = jnp.concatenate([columns[start:stop] for start, stop in RINGS])
    geo = jnp.stack(
        [
            jnp.repeat(columns, RADIAL),
            jnp.tile(spacing_b, WIN),
            jnp.broadcast_to(spacing_z, (LANES,)),
        ]
    )
    geo = jnp.concatenate([geo, jnp.ones((5, LANES), wide)])
    lam, coef, middle = call(
        tables_kernel,
        "tables",
        (rot, geo, mats["modes"], own),
        ((4 * MODES, LANES), (24, LANES), (256, OWN)),
        scalars=1,
    )
    (middle,) = call(follow_kernel, "follow", (left, right, middle), ((256, OWN),), untouched=2)
    near, far = beside(middle)
    outer, up, down = call(
        outer_kernel,
        "outer",
        (rot, left, ends, right, geo),
        ((256, LANES), (136, LANES), (136, LANES)),
        scalars=1,
    )
    lower, upper = neighbours(up, down)
    (inner,) = call(
        inner_kernel, "inner", (rot, near, middle, far), ((256, LANES),), scalars=1, flops=EARLY
    )

    def solve(fields, below, above, before, tiles):
        lanes = tiles * TILE
        start_up = len(fields) == 2
        share_inner, spectrum = call(
            functools.partial(solve_inner_kernel, start_up, before, tiles),
            "solve_inner",
            (*fields, mats["forward_inner"]),
            shapes(tiles, 384, 4 * MODES),
            (
                vmem((before, 384, TILE), wide),
                vmem((4 * tiles, INNER, TILE), wide),
                vmem((4, 3 * INNER, lanes), narrow),
            ),
        )
        share_outer, modes, up, down, off, near = call(
            functools.partial(solve_outer_kernel, start_up, before, tiles),
            "solve_outer",
            (rot, fields[0], below, above, spectrum, lam, mats["forward_outer"], *mats["backward_outer"]),
            (*shapes(tiles, 128), (4, 2 * MODES, lanes), *shapes(tiles, 64, 64, 64, 64)),
            (
                vmem((before, 256, TILE), wide),
                vmem((4 * tiles, 128, TILE), wide),
                vmem((4, 3 * OUTER, lanes), narrow),
            ),
            scalars=1,
        )
        return (share_inner, share_outer), (modes, up, down), neighbours(off, near)

    def advance(kind, local, messages, share, before, total, width, tiles):
        lanes = tiles * TILE

        def scratch(rows, folded):
            return [
                vmem((width, rows, TILE), wide),
                vmem((4 * width, 128, TILE), wide),
                vmem((4, folded, lanes), narrow),
            ]

        def pick(at):
            return [pair[at] for pair in (before, total) if pair is not None]

        kept = [count for count, used in ((1, kind in (0, 2)), (1, kind != 0)) if used]
        *inner, image = call(
            functools.partial(step_inner_kernel, kind, width, tiles),
            f"step{kind}_inner",
            (local[0], *pick(0), coef, mats["apply_inner"], *mats["backward_inner"]),
            shapes(tiles, *(384 for _ in kept), 512),
            scratch(384, 288),
        )
        sent = {0: 128, 1: 16, 2: 128, 3: 64}[kind]
        extra = scratch(128, 96)
        if kind == 1:
            extra.append(vmem((1024, lanes), narrow))
        out = call(
            functools.partial(step_outer_kernel, kind, width, tiles),
            f"step{kind}_outer",
            (
                *(rot, local[1], messages[0], local[2], messages[1]),
                *(*pick(1), *share, image, coef, mats["apply_outer"]),
                *(mats["restrict"] if kind == 1 else ()),
            ),
            shapes(tiles, *(128 for _ in kept), 512, sent, sent, *((64,) if kind == 1 else ())),
            extra,
            scalars=1,
        )
        outer, (field, up, down, *coarse) = out[: len(kept)], out[len(kept) :]
        return list(zip(inner, outer)), field, neighbours(up, down), *coarse

    share, local, messages = solve((outer, inner), lower, upper, 5, 5)
    (step,), field, messages = advance(0, local, messages, share, None, None, 5, 5)
    share, local, messages = solve((field,), *messages, 5, 5)
    (total,), field, messages, coarse = advance(1, local, messages, share, step, step, 5, 4)
    (scale,) = call(
        diagonal_kernel, "diagonal", (rot, lower, upper, geo, mats["coarse"]), shapes(4, 64), scalars=1
    )
    outer, terms, up, down = call(
        coarse_outer_kernel,
        "coarse_outer",
        (rot, coarse, *messages, scale, coef, mats["prolong"], field),
        (*shapes(4, 256), (1, 192, 4 * TILE), *shapes(4, 128, 128)),
        scalars=1,
    )
    messages = neighbours(up, down)
    *total, inner = call(
        coarse_inner_kernel,
        "coarse_inner",
        (terms, coef, mats["prolong"], *total, field),
        shapes(4, 384, 128, 256),
    )
    share, local, messages = solve((outer, inner), *messages, 4, 4)
    (step, total), field, messages = advance(2, local, messages, share, None, total, 4, 4)
    share, local, messages = solve((field,), *messages, 4, 3)
    (total,), field, messages = advance(3, local, messages, share, step, total, 3, 3)
    sol, inner = call(
        finish_inner_kernel,
        "finish_inner",
        (rot, field, *total),
        ((512, OWN), (384, OWN)),
        (vmem((3, 384, TILE), wide),),
        scalars=1,
    )
    (res,) = call(
        finish_outer_kernel,
        "finish_outer",
        (rot, field, *messages, inner),
        ((512, OWN),),
        (vmem((3, 128, TILE), wide),),
        scalars=1,
    )
    return sol.reshape(rhs.shape), res.reshape(rhs.shape)


def solution(mesh):
    return jax.shard_map(
        per_device,
        mesh=mesh,
        in_specs=(P(None, None, None, ("grp", "sub")), P("grp"), P(), P(), P()),
        out_specs=(P(None, None, None, ("grp", "sub")), P(None, None, None, ("grp", "sub"))),
        check_vma=False,
    )
```
